32 devices in a mesh: section: 4 (over y, core), expert: 8 (over z, x).
Axes of the slice: x: 2, y: 2, z: 4, core: 2. Of those that a mesh axis runs over, the one named last changes fastest.
Arguments:
- act_in: bfloat16 [4, 1024, 2048], P('section', 'expert'), may hold values from -6 to 6
- saved_in: bfloat16 [4, 1024, 2048], P('section', 'expert'), may hold values from -6 to 6
- grad_in: bfloat16 [4, 1024, 2048], P('section', 'expert'), may hold values from -6 to 6
- norm_gain: float32 [4, 2048], P('section'), may hold values from 0.1 to 1.9
- w_gate: bfloat16 [4, 2048, 1536], P('section', None, 'expert'), may hold values from -0.125 to 0.125
- w_up: bfloat16 [4, 2048, 1536], P('section', None, 'expert'), may hold values from -0.125 to 0.125
- w_down: bfloat16 [4, 1536, 2048], P('section', 'expert'), may hold values from -0.21875 to 0.21875
- routes_fwd: int32 [4, 1024, 1], P('section', 'expert'), may hold values from 0 to 1; in each aligned block of 128 rows (0 to 127, 128 to 255, ..., all dimensions but the last counted through in order) at most 66 rows name the same one
- gates_fwd: float32 [4, 1024, 1], P('section', 'expert'), may hold values from 0.1 to 1
- routes_bwd: int32 [4, 1024, 1], P('section', 'expert'), may hold values from 0 to 1; in each aligned block of 128 rows (0 to 127, 128 to 255, ..., all dimensions but the last counted through in order) at most 66 rows name the same one
- gates_bwd: float32 [4, 1024, 1], P('section', 'expert'), may hold values from 0.1 to 1
Outputs:
- act_out: bfloat16 [4, 1024, 2048], P('section', 'expert')
- grad_out: bfloat16 [4, 1024, 2048], P('section', 'expert')
The draws below stay inside these ranges and needn't reach their ends.
Inputs may be any that keep to these rules, and one draw needn't show every extreme that they name: `routes_fwd`: the 1 expert of a token differ; within the 128 tokens of one device no expert is named by more than 66 routes, and in some such blocks one expert is named by exactly 66. `routes_bwd`: as for routes_fwd.
All inputs are finite; a program needn't handle non-finite values.
Results may differ from the reference program's by a relative error of at most 0.005.
Values may be sent and summed in bfloat16 or wider, within the bound.
No kernel may reach another device: no remote copies, remote signals or barrier semaphores. Data moves between devices by JAX's collectives and lax.ppermute only.
A program may use at most 64 MiB of HBM per device.

```python
import math
import jax
import jax.numpy as jnp
import numpy as np
from jax import lax

D = 2048
FF = 768
SPLIT = 4
TOPK = 1
TOK = 128
FF_DEV = 192
EXPERTS = 2
CAP = 66
TOKENS = 1024
N_SECTION = 4


def block_scale(rng, extent, split, least, high):
    def one(position, blocks):
        steps = jax.random.uniform(jax.random.fold_in(jax.random.fold_in(rng, 6), position), (blocks,), jnp.float32, least / len(split), high / len(split))
        return jnp.repeat(jnp.exp(steps), extent[position] // blocks).reshape((-1,) + (1,) * (len(extent) - position - 1))

    loudness = one(*split[0])
    for cut in split[1:]:
        loudness = loudness * one(*cut)
    return loudness


def shared_out(stream_key, own, number, rows, count, top, limit, skew):
    order = jax.random.permutation(stream_key, count)
    packed, usual = portions_of(count, rows * top, limit, skew, True), portions_of(count, rows * top, limit, skew, False)
    places = jnp.arange(count)

    def named(sizes, turn):
        used = int((sizes > 0).sum())
        fixed = max(1, used // 4)
        moved = fixed + (places - fixed + turn * (used - fixed)) % max(1, count - fixed)
        return jnp.zeros((count,), jnp.int32).at[order[jnp.where(places < fixed, places, moved)]].set(jnp.asarray(sizes, jnp.int32))

    sizes = jnp.where(number % 4 == 0, named(packed, number // 4), named(usual, number - number // 4 - 1))
    mixed = jax.random.permutation(jax.random.fold_in(own, 3), count)
    donor, sink = mixed[0:count // 2 * 2:2], mixed[1:count // 2 * 2:2]
    room = jnp.minimum(sizes[donor] - 1, limit - sizes[sink]) // 2
    room = jnp.where((donor == order[0]) | (sink == order[0]) | (sizes[sink] == 0), 0, jnp.maximum(room, 0))
    moved = jax.random.randint(jax.random.fold_in(own, 4), (count // 2,), 0, 1 << 20) % (room + 1)
    sizes = sizes.at[donor].add(-moved).at[sink].add(moved)
    items = jnp.searchsorted(jnp.cumsum(sizes), jnp.arange(rows * top), side="right").astype(jnp.int32)
    grid = items.reshape(top, rows).T
    grid = grid[jax.random.permutation(jax.random.fold_in(own, 1), rows)]
    turn = jax.random.randint(jax.random.fold_in(own, 2), (rows, 1), 0, top)
    return jnp.take_along_axis(grid, (jnp.arange(top)[None, :] + turn) % top, axis=1)


def portions_of(number_of, total, most, skew, full):
    portions = [(1 << 20) // math.isqrt(rank ** skew) + 1 for rank in range(1, number_of + 1)]
    largest = most if full else min(most, max(-(-total // number_of), total * portions[0] // sum(portions)))
    least = 1 if total - largest >= number_of - 1 else 0
    given, rest = [largest] + [least] * (number_of - 1), total - largest - least * (number_of - 1)
    while rest > 0:
        candidates = [i for i in range(1, number_of) if given[i] < largest] or [i for i in range(1, number_of) if given[i] < most]
        pool, remaining = sum([portions[i] for i in candidates]), rest
        for i in candidates:
            addition = min(most - given[i], max(1, remaining * portions[i] // pool), rest)
            given[i] = given[i] + addition
            rest = rest - addition
    return np.array(given)


def bell_draw(rng, shape, spread, bound, split=(), held_as=jnp.bfloat16):
    entries = jax.random.normal(rng, shape, jnp.float32) * spread
    if len(split) > 0:
        entries = block_scale(rng, shape, split, -0.22, 0.18) * entries
    return jnp.clip(entries, min=-bound, max=bound).astype(held_as)


def setup_inputs(seed: int = 0) -> dict:
    key_list = jax.random.split(jax.random.key(seed), 12)
    act_in = bell_draw(key_list[0], (N_SECTION, TOKENS, D), 1.0, 6.0, ((0, 4), (1, 8)))
    saved_in = bell_draw(key_list[1], (N_SECTION, TOKENS, D), 1.0, 6.0, ((0, 4), (1, 8)))
    grad_in = bell_draw(key_list[2], (N_SECTION, TOKENS, D), 1.0, 6.0, ((0, 4), (1, 8)))
    norm_gain = jnp.clip(1.0 + 0.18 * jax.random.normal(key_list[3], (N_SECTION, D), jnp.float32), 0.1, 1.9)
    w_gate = bell_draw(key_list[4], (N_SECTION, D, EXPERTS * FF), D ** -0.5, 0.125, ((0, 4), (2, 8)))
    w_up = bell_draw(key_list[5], (N_SECTION, D, EXPERTS * FF), D ** -0.5, 0.125, ((0, 4), (2, 8)))
    w_down = bell_draw(key_list[6], (N_SECTION, EXPERTS * FF, D), FF ** -0.5, 0.21875, ((0, 4), (1, 8)))
    routes_fwd_keys = jax.random.split(jax.random.fold_in(key_list[7], 1), N_SECTION * TOKENS // TOK)
    routes_fwd_turns = jax.random.permutation(jax.random.fold_in(key_list[7], 3), N_SECTION * TOKENS // TOK)
    routes_fwd = jax.vmap(lambda own, number: shared_out(jax.random.fold_in(key_list[7], 2), own, number, TOK, EXPERTS, TOPK, CAP, 2))(routes_fwd_keys, routes_fwd_turns).reshape((N_SECTION, TOKENS, TOPK))
    gates_fwd = jnp.clip(jnp.exp(math.log(1.0) - 2.3025851 * jax.random.uniform(key_list[8], (N_SECTION, TOKENS, TOPK), jnp.float32) ** block_scale(key_list[8], (N_SECTION, TOKENS, TOPK), ((0, 4), (1, 8)), -0.2, 0.2)), 0.1, 1.0)
    routes_bwd_keys = jax.random.split(jax.random.fold_in(key_list[9], 1), N_SECTION * TOKENS // TOK)
    routes_bwd_turns = jax.random.permutation(jax.random.fold_in(key_list[9], 3), N_SECTION * TOKENS // TOK)
    routes_bwd = jax.vmap(lambda own, number: shared_out(jax.random.fold_in(key_list[9], 2), own, number, TOK, EXPERTS, TOPK, CAP, 2))(routes_bwd_keys, routes_bwd_turns).reshape((N_SECTION, TOKENS, TOPK))
    gates_bwd = jnp.clip(jnp.exp(math.log(1.0) - 2.3025851 * jax.random.uniform(key_list[10], (N_SECTION, TOKENS, TOPK), jnp.float32) ** block_scale(key_list[10], (N_SECTION, TOKENS, TOPK), ((0, 4), (1, 8)), -0.2, 0.2)), 0.1, 1.0)
    return {"act_in": act_in, "saved_in": saved_in, "grad_in": grad_in, "norm_gain": norm_gain, "w_gate": w_gate, "w_up": w_up, "w_down": w_down, "routes_fwd": routes_fwd, "gates_fwd": gates_fwd, "routes_bwd": routes_bwd, "gates_bwd": gates_bwd}


norm_eps = 1e-06

def silu_parts(values):
    sigma = jax.nn.sigmoid(values)
    return (values * sigma, sigma * (1.0 + values * (1.0 - sigma)))

def normalize(block_rows, gain_row):
    values = block_rows.astype(jnp.float32)
    inv_scale = lax.rsqrt(lax.optimization_barrier(jnp.mean(values * values, axis=-1, keepdims=True)) + norm_eps)
    return (values * inv_scale * gain_row, inv_scale)

def slot_targets(routes):
    total = routes.shape[0]
    top_count = routes.shape[1]
    blocks = total // TOK
    flat_routes = routes.reshape(blocks, TOK * top_count)
    onehot = (flat_routes[:, :, None] == jnp.arange(EXPERTS, dtype=jnp.int32)[None, None, :]).astype(jnp.int32)
    before = jnp.cumsum(onehot, axis=1) - onehot
    slot_index = lax.optimization_barrier(jnp.sum(before * onehot, axis=2))
    device_index = jnp.arange(blocks, dtype=jnp.int32)[:, None]
    target = flat_routes * (blocks * CAP) + device_index * CAP + slot_index
    return target.reshape(total * top_count).astype(jnp.int32)

def section_pass(x_fwd, x_bwd, upstream, gain_row, gate_all, up_all, down_all, r_fwd, g_fwd, r_bwd, g_bwd):
    total = x_fwd.shape[0]
    slot_total = total // TOK * CAP
    n_fwd = normalize(x_fwd, gain_row)[0].astype(jnp.bfloat16)
    values_b, inv_scale = normalize(x_bwd, gain_row)
    n_bwd = values_b.astype(jnp.bfloat16)
    target_f = slot_targets(r_fwd)
    target_b = slot_targets(r_bwd)
    token_index = jnp.repeat(jnp.arange(total, dtype=jnp.int32), TOPK)
    empty = jnp.zeros((EXPERTS * slot_total, D), jnp.bfloat16)
    buffer_f = empty.at[target_f].set(n_fwd[token_index])
    buffer_b = empty.at[target_b].set(n_bwd[token_index])
    buffer_g = empty.at[target_b].set(upstream[token_index])
    outs_f = []
    outs_b = []
    for expert_id in range(EXPERTS):
        gate_w = gate_all[:, expert_id * FF:(expert_id + 1) * FF]
        up_w = up_all[:, expert_id * FF:(expert_id + 1) * FF]
        down_w = down_all[expert_id * FF:(expert_id + 1) * FF]
        lower = expert_id * slot_total
        slot_rows = buffer_f[lower:lower + slot_total]
        gate_pre = jnp.dot(slot_rows, gate_w, preferred_element_type=jnp.float32)
        up_pre = jnp.dot(slot_rows, up_w, preferred_element_type=jnp.float32)
        activation, _ = silu_parts(gate_pre)
        hidden = (activation * up_pre).astype(jnp.bfloat16)
        summed = jnp.zeros((slot_total, D), jnp.float32)
        for share in range(SPLIT):
            cut = slice(share * FF_DEV, (share + 1) * FF_DEV)
            partial_value = jnp.dot(hidden[:, cut], down_w[cut], preferred_element_type=jnp.float32).astype(jnp.bfloat16)
            summed = summed + partial_value.astype(jnp.float32)
        outs_f.append(summed)
        slot_rows = buffer_b[lower:lower + slot_total]
        grad_rows = buffer_g[lower:lower + slot_total]
        gate_pre = jnp.dot(slot_rows, gate_w, preferred_element_type=jnp.float32)
        up_pre = jnp.dot(slot_rows, up_w, preferred_element_type=jnp.float32)
        activation, derivative = silu_parts(gate_pre)
        d_hidden = jnp.dot(grad_rows, down_w.T, preferred_element_type=jnp.float32)
        d_gate = (d_hidden * up_pre * derivative).astype(jnp.bfloat16)
        d_up = (d_hidden * activation).astype(jnp.bfloat16)
        summed = jnp.zeros((slot_total, D), jnp.float32)
        for share in range(SPLIT):
            cut = slice(share * FF_DEV, (share + 1) * FF_DEV)
            partial_value = jnp.dot(d_gate[:, cut], gate_w[:, cut].T, preferred_element_type=jnp.float32)
            partial_value = partial_value + jnp.dot(d_up[:, cut], up_w[:, cut].T, preferred_element_type=jnp.float32)
            summed = summed + partial_value.astype(jnp.bfloat16).astype(jnp.float32)
        outs_b.append(summed)
    values_f = jnp.concatenate(outs_f, axis=0)
    values_bk = jnp.concatenate(outs_b, axis=0)
    mixed = lax.optimization_barrier(jnp.sum(values_f[target_f].reshape(total, TOPK, D) * g_fwd[:, :, None], axis=1))
    act_out = (x_fwd.astype(jnp.float32) + mixed).astype(jnp.bfloat16)
    d_norm = lax.optimization_barrier(jnp.sum(values_bk[target_b].reshape(total, TOPK, D) * g_bwd[:, :, None], axis=1))
    scaled = d_norm * gain_row
    base = x_bwd.astype(jnp.float32)
    d_input = inv_scale * (scaled - base * inv_scale * inv_scale * lax.optimization_barrier(jnp.mean(scaled * base, axis=-1, keepdims=True)))
    grad_out = (upstream.astype(jnp.float32) + d_input).astype(jnp.bfloat16)
    return (act_out, grad_out)

def reference(act_in, saved_in, grad_in, norm_gain, w_gate, w_up, w_down, routes_fwd, gates_fwd, routes_bwd, gates_bwd):
    sections = act_in.shape[0]
    arrived = jnp.roll(act_in, 1, axis=0)
    upstream = jnp.roll(grad_in, -1, axis=0)
    outs_a = []
    outs_g = []
    for section_id in range(sections):
        first_out, second_out = section_pass(arrived[section_id], saved_in[section_id], upstream[section_id], norm_gain[section_id], w_gate[section_id], w_up[section_id], w_down[section_id], routes_fwd[section_id], gates_fwd[section_id], routes_bwd[section_id], gates_bwd[section_id])
        outs_a.append(first_out)
        outs_g.append(second_out)
    return (jnp.stack(outs_a, axis=0), jnp.stack(outs_g, axis=0))
```

```python
import jax
import jax.numpy as jnp
from jax import lax
from jax.sharding import PartitionSpec as P

SPLIT = 4
EPS = 1e-06


def shifted(value, axis, steps):
    count = lax.axis_size(axis)
    return lax.ppermute(value, axis, [(i, (i + steps) % count) for i in range(count)])


def swapped(value, axis, bit):
    count = lax.axis_size(axis)
    return lax.ppermute(value, axis, [(i, i ^ bit) for i in range(count)])


def silu_parts(values):
    sigma = jax.nn.sigmoid(values)
    return (values * sigma, sigma * (1.0 + values * (1.0 - sigma)))


def normalize(block_rows, gain_row):
    values = block_rows.astype(jnp.float32)
    inv_scale = lax.rsqrt(jnp.mean(values * values, axis=-1, keepdims=True) + EPS)
    return (values * inv_scale * gain_row, inv_scale)


def slot_targets(routes, own, experts, rows):
    flat = routes.reshape(-1)
    onehot = (flat[:, None] == jnp.arange(experts, dtype=jnp.int32)[None, :]).astype(jnp.int32)
    before = jnp.cumsum(onehot, axis=0) - onehot
    slot = jnp.sum(before * onehot, axis=1)
    return (lax.rem(flat - own + experts, experts) * rows + slot).reshape(routes.shape)


def chooser_of(target, total):
    picks = jnp.arange(total, dtype=jnp.int32)[:, None, None] == target[None]
    return jnp.sum(picks.astype(jnp.float32), axis=2).astype(jnp.bfloat16)


def pack(chooser, values, experts):
    packed = jnp.dot(chooser, values, preferred_element_type=jnp.float32).astype(jnp.bfloat16)
    return packed.reshape(experts, -1, values.shape[1])


def fetch_rows(blocks):
    mine = [blocks[0]]
    theirs = [swapped(blocks[0], "expert", 2)]
    for j in range(1, blocks.shape[0]):
        got = shifted(blocks[j], "expert", SPLIT * j)
        mine.append(got)
        theirs.append(swapped(got, "expert", 2))
    return jnp.concatenate(mine + theirs, axis=0)


def return_rows(partial, experts):
    half = partial.shape[0] // 2
    rows = half // experts
    own = partial[:half]
    away = partial[half:].astype(jnp.bfloat16)
    home = []
    for j in range(experts):
        cut = slice(j * rows, (j + 1) * rows)
        total = (own[cut] + swapped(away[cut], "expert", 2).astype(jnp.float32)).astype(jnp.bfloat16)
        home.append(total if j == 0 else shifted(total, "expert", -SPLIT * j))
    return jnp.concatenate(home, axis=0)


def weighted_sum(target, gates, rows):
    place = jnp.arange(rows.shape[0], dtype=jnp.int32)[None, None, :] == target[:, :, None]
    width = rows.shape[1]
    picked = jnp.dot(
        place.astype(jnp.bfloat16).reshape(-1, rows.shape[0]), rows, preferred_element_type=jnp.float32
    )
    return jnp.sum(picked.reshape(target.shape + (width,)) * gates[:, :, None], axis=1)


CONTRACT = (((1,), (1,)), ((), ()))


def forward_rows(rows, shares):
    out = None
    for gate_up, down in shares:
        units = down.shape[0]
        both = jnp.dot(rows, gate_up, preferred_element_type=jnp.float32)
        hidden = (silu_parts(both[:, :units])[0] * both[:, units:]).astype(jnp.bfloat16)
        part = jnp.dot(hidden, down, preferred_element_type=jnp.float32)
        out = part if out is None else out + part
    return out


def backward_rows(rows, grads, shares):
    out = None
    for gate_up, down in shares:
        units = down.shape[0]
        both = jnp.dot(rows, gate_up, preferred_element_type=jnp.float32)
        activation, derivative = silu_parts(both[:, :units])
        d_hidden = lax.dot_general(grads, down, CONTRACT, preferred_element_type=jnp.float32)
        d_gate = (d_hidden * both[:, units:] * derivative).astype(jnp.bfloat16)
        d_up = (d_hidden * activation).astype(jnp.bfloat16)
        d_both = jnp.concatenate([d_gate, d_up], axis=1)
        part = lax.dot_general(d_both, gate_up, CONTRACT, preferred_element_type=jnp.float32)
        out = part if out is None else out + part
    return out


def per_device(act_in, saved_in, grad_in, norm_gain, w_gate, w_up, w_down, routes_fwd, gates_fwd, routes_bwd, gates_bwd):
    experts = lax.axis_size("expert") // SPLIT
    own = lax.axis_index("expert") // SPLIT
    tok_count, top_count = routes_fwd.shape[1:]
    capacity = min(tok_count, tok_count * top_count // experts + 2)
    rows = -(-capacity // 8) * 8
    gain_row = norm_gain[0]

    incoming = shifted(act_in[0], "section", 1)
    upstream = shifted(grad_in[0], "section", -1)
    gate_up = jnp.concatenate([w_gate[0], w_up[0]], axis=1)
    down = w_down[0]
    other_gate_up = swapped(gate_up, "expert", 1)
    other_down = swapped(down, "expert", 1)
    shares = ((gate_up, down), (other_gate_up, other_down))

    target_b = slot_targets(routes_bwd[0], own, experts, rows)
    chooser_b = chooser_of(target_b, experts * rows)
    base = saved_in[0].astype(jnp.float32)
    values_b, inv_scale = normalize(saved_in[0], gain_row)
    rows_b = fetch_rows(pack(chooser_b, values_b.astype(jnp.bfloat16), experts))
    rows_g = fetch_rows(pack(chooser_b, upstream, experts))
    target_f = slot_targets(routes_fwd[0], own, experts, rows)
    chooser_f = chooser_of(target_f, experts * rows)
    n_fwd = normalize(incoming, gain_row)[0].astype(jnp.bfloat16)
    rows_f = fetch_rows(pack(chooser_f, n_fwd, experts))

    back_b = return_rows(backward_rows(rows_b, rows_g, shares), experts)
    back_f = return_rows(forward_rows(rows_f, shares), experts)

    d_norm = weighted_sum(target_b, gates_bwd[0], back_b)
    scaled = d_norm * gain_row
    d_input = inv_scale * (
        scaled - base * inv_scale * inv_scale * jnp.mean(scaled * base, axis=-1, keepdims=True)
    )
    grad_out = (upstream.astype(jnp.float32) + d_input).astype(jnp.bfloat16)
    mixed = weighted_sum(target_f, gates_fwd[0], back_f)
    act_out = (incoming.astype(jnp.float32) + mixed).astype(jnp.bfloat16)
    return (act_out[None], grad_out[None])


def solution(mesh):
    tokens = P("section", "expert", None)
    in_specs = (
        tokens,
        tokens,
        tokens,
        P("section", None),
        P("section", None, "expert"),
        P("section", None, "expert"),
        tokens,
        tokens,
        tokens,
        tokens,
        tokens,
    )
    return jax.shard_map(
        per_device, mesh=mesh, in_specs=in_specs, out_specs=(tokens, tokens), check_vma=False
    )
```

```python
import functools

import jax
import jax.numpy as jnp
from jax import lax
from jax.experimental import pallas as pl
from jax.experimental.pallas import tpu as pltpu
from jax.sharding import PartitionSpec as P

SPLIT = 4
EPS = 1e-06
CONTRACT = (((1,), (1,)), ((), ()))
OVER_ROWS = (((0,), (0,)), ((), ()))
F32 = jnp.float32
BF16 = jnp.bfloat16


def shifted(value, axis, steps):
    count = lax.axis_size(axis)
    return lax.ppermute(value, axis, [(i, (i + steps) % count) for i in range(count)])


def swapped(value, axis, bit):
    count = lax.axis_size(axis)
    return lax.ppermute(value, axis, [(i, i ^ bit) for i in range(count)])


def local_call(body, out_shape, scratch=(), vmem_mib=16, **names):
    return pl.pallas_call(
        body,
        out_shape=out_shape,
        scratch_shapes=scratch,
        compiler_params=pltpu.CompilerParams(vmem_limit_bytes=vmem_mib << 20),
        cost_estimate=pl.CostEstimate(flops=1000, bytes_accessed=1000, transcendentals=0),
        **names,
    )


def silu_parts(values):
    sigma = jax.nn.sigmoid(values)
    return (values * sigma, sigma * (1.0 + values * (1.0 - sigma)))


def inverse_rms(values):
    return lax.rsqrt(jnp.mean(values * values, axis=-1, keepdims=True) + EPS)


def slots_of(routes, own, experts):
    count = routes.shape[1]
    height = -(-experts // 8) * 8
    ids = lax.broadcasted_iota(jnp.int32, (height, count), 0)
    onehot = (ids == routes).astype(F32)
    earlier = (
        lax.broadcasted_iota(jnp.int32, (count, count), 0) < lax.broadcasted_iota(jnp.int32, (count, count), 1)
    ).astype(F32)
    before = jnp.dot(onehot.astype(BF16), earlier.astype(BF16), preferred_element_type=F32)
    slot = jnp.sum(before * onehot, axis=0, keepdims=True).astype(jnp.int32)
    block = routes - own
    return (jnp.where(block < 0, block + experts, block), slot)


def chooser_of(block, slot, j, rows):
    place = lax.broadcasted_iota(jnp.int32, (rows, block.shape[1]), 0)
    return jnp.where((place == slot) & (block == j), 1.0, 0.0).astype(BF16)


def pack_body(experts, own_ref, routes_ref, *refs):
    if len(refs) == experts + 2:
        gain_ref, x_ref, *outs = refs
        values = x_ref[...].astype(F32)
        values = (values * inverse_rms(values) * gain_ref[...]).astype(BF16)
    else:
        x_ref, *outs = refs
        values = x_ref[...]
    block, slot = slots_of(routes_ref[...], own_ref[0], experts)
    for j, out in enumerate(outs):
        chooser = chooser_of(block, slot, j, out.shape[0])
        out[...] = jnp.dot(chooser, values, preferred_element_type=F32).astype(BF16)


def gather_blocks(refs, wide_ref):
    rows = refs[0].shape[0]
    pitch = wide_ref.shape[0] // len(refs)
    for i, ref in enumerate(refs):
        wide_ref[pl.ds(i * pitch, rows), :] = ref[...]
    return pitch


def spread_out(total, refs, pitch):
    for i, ref in enumerate(refs):
        ref[...] = total[i * pitch:i * pitch + ref.shape[0]].astype(ref.dtype)


def forward_body(count, *refs):
    row_refs, refs = refs[:count], refs[count:]
    shares, refs = (refs[0:2], refs[2:4]), refs[4:]
    outs, wide_ref = refs[:-1], refs[-1]
    pitch = gather_blocks(row_refs, wide_ref)
    rows = wide_ref[...]
    total = None
    for gate_up, down in shares:
        units = down.shape[0]
        both = jnp.dot(rows, gate_up[...], preferred_element_type=F32)
        hidden = (silu_parts(both[:, :units])[0] * both[:, units:]).astype(BF16)
        part = jnp.dot(hidden, down[...], preferred_element_type=F32)
        total = part if total is None else total + part
    spread_out(total, outs, pitch)


def backward_body(count, *refs):
    row_refs, grad_refs, refs = refs[:count], refs[count:2 * count], refs[2 * count:]
    shares, refs = (refs[0:2], refs[2:4]), refs[4:]
    outs, wide_ref, grad_wide_ref = refs[:-2], refs[-2], refs[-1]
    pitch = gather_blocks(row_refs, wide_ref)
    gather_blocks(grad_refs, grad_wide_ref)
    rows = wide_ref[...]
    grads = grad_wide_ref[...]
    total = None
    for gate_up, down in shares:
        units = down.shape[0]
        both = jnp.dot(rows, gate_up[...], preferred_element_type=F32)
        activation, derivative = silu_parts(both[:, :units])
        d_hidden = lax.dot_general(grads, down[...], CONTRACT, preferred_element_type=F32)
        d_gate = (d_hidden * both[:, units:] * derivative).astype(BF16)
        d_up = (d_hidden * activation).astype(BF16)
        d_both = jnp.concatenate([d_gate, d_up], axis=1)
        part = lax.dot_general(d_both, gate_up[...], CONTRACT, preferred_element_type=F32)
        total = part if total is None else total + part
    spread_out(total, outs, pitch)


def routed_sum(experts, own_ref, routes_ref, gates_ref, home_refs):
    block, slot = slots_of(routes_ref[...], own_ref[0], experts)
    first, second, *crossed = home_refs
    own_rows = (first[...] + second[...].astype(F32)).astype(BF16)
    total = None
    for j in range(experts):
        rows = own_rows if j == 0 else crossed[j - 1][...]
        chooser = chooser_of(block, slot, j, rows.shape[0])
        part = lax.dot_general(chooser, rows, OVER_ROWS, preferred_element_type=F32)
        total = part if total is None else total + part
    count = block.shape[1]
    diagonal = lax.broadcasted_iota(jnp.int32, (count, count), 0) == lax.broadcasted_iota(
        jnp.int32, (count, count), 1
    )
    gates = jnp.sum(jnp.where(diagonal, gates_ref[...], 0.0), axis=1, keepdims=True)
    return total * gates


def forward_home_body(experts, own_ref, routes_ref, gates_ref, x_ref, *refs):
    mixed = routed_sum(experts, own_ref, routes_ref, gates_ref, refs[:-1])
    refs[-1][...] = (x_ref[...].astype(F32) + mixed).astype(BF16)


def backward_home_body(experts, own_ref, routes_ref, gates_ref, gain_ref, saved_ref, up_ref, *refs):
    d_norm = routed_sum(experts, own_ref, routes_ref, gates_ref, refs[:-1])
    base = saved_ref[...].astype(F32)
    inv_scale = inverse_rms(base)
    scaled = d_norm * gain_ref[...]
    d_input = inv_scale * (
        scaled - base * inv_scale * inv_scale * jnp.mean(scaled * base, axis=-1, keepdims=True)
    )
    refs[-1][...] = (up_ref[...].astype(F32) + d_input).astype(BF16)


def fetch_rows(blocks):
    got = [blocks[0]] + [shifted(blocks[j], "expert", SPLIT * j) for j in range(1, len(blocks))]
    return got + [swapped(block, "expert", 2) for block in got]


def return_rows(partial):
    experts = len(partial) // 2
    mine, theirs = partial[:experts], partial[experts:]
    home = []
    for j in range(1, experts):
        total = (mine[j] + swapped(theirs[j], "expert", 2).astype(F32)).astype(BF16)
        home.append(shifted(total, "expert", -SPLIT * j))
    return [mine[0], swapped(theirs[0], "expert", 2)] + home


def per_device(act_in, saved_in, grad_in, norm_gain, w_gate, w_up, w_down, routes_fwd, gates_fwd, routes_bwd, gates_bwd):
    experts = lax.axis_size("expert") // SPLIT
    own = (lax.axis_index("expert") // SPLIT).astype(jnp.int32).reshape(1)
    tok_count, top_count = routes_fwd.shape[1:]
    assert top_count == 1
    width = act_in.shape[2]
    rows = -(-min(tok_count, tok_count // experts + 2) // 8) * 8
    pitch = -(-rows // 16) * 16
    scalar = pl.BlockSpec(memory_space=pltpu.SMEM)
    whole = pl.BlockSpec(memory_space=pltpu.VMEM)

    packed = [jax.ShapeDtypeStruct((rows, width), BF16)] * experts
    partial = [jax.ShapeDtypeStruct((rows, width), F32)] * experts + packed
    tokens = jax.ShapeDtypeStruct((tok_count, width), BF16)
    wide = pltpu.VMEM((2 * experts * pitch, width), BF16)

    incoming = shifted(act_in[0], "section", 1)
    upstream = shifted(grad_in[0], "section", -1)
    gate_up = jnp.concatenate([w_gate[0], w_up[0]], axis=1)
    down = w_down[0]
    shares = (gate_up, down, swapped(gate_up, "expert", 1), swapped(down, "expert", 1))
    r_fwd = routes_fwd.reshape(1, tok_count)
    r_bwd = routes_bwd.reshape(1, tok_count)
    g_fwd = gates_fwd.reshape(1, tok_count)
    g_bwd = gates_bwd.reshape(1, tok_count)

    def pack(name, routes, *args):
        return local_call(
            functools.partial(pack_body, experts),
            packed,
            in_specs=[scalar] + [whole] * (len(args) + 1),
            out_specs=[whole] * experts,
            name=name,
        )(own, routes, *args)

    rows_b = fetch_rows(pack("pack_saved", r_bwd, norm_gain, saved_in[0]))
    rows_g = fetch_rows(pack("pack_grad", r_bwd, upstream))
    rows_f = fetch_rows(pack("pack_act", r_fwd, norm_gain, incoming))

    count = 2 * experts
    back_b = return_rows(
        local_call(
            functools.partial(backward_body, count), partial, scratch=[wide, wide], vmem_mib=40, name="experts_bwd"
        )(*rows_b, *rows_g, *shares)
    )
    back_f = return_rows(
        local_call(
            functools.partial(forward_body, count), partial, scratch=[wide], vmem_mib=32, name="experts_fwd"
        )(*rows_f, *shares)
    )

    grad_out = local_call(
        functools.partial(backward_home_body, experts),
        tokens,
        in_specs=[scalar] + [whole] * (6 + experts),
        out_specs=whole,
        name="home_bwd",
    )(own, r_bwd, g_bwd, norm_gain, saved_in[0], upstream, *back_b)
    act_out = local_call(
        functools.partial(forward_home_body, experts),
        tokens,
        in_specs=[scalar] + [whole] * (4 + experts),
        out_specs=whole,
        name="home_fwd",
    )(own, r_fwd, g_fwd, incoming, *back_f)
    return (act_out[None], grad_out[None])


def solution(mesh):
    tokens = P("section", "expert", None)
    in_specs = (
        tokens,
        tokens,
        tokens,
        P("section", None),
        P("section", None, "expert"),
        P("section", None, "expert"),
        tokens,
        tokens,
        tokens,
        tokens,
        tokens,
    )
    return jax.shard_map(
        per_device, mesh=mesh, in_specs=in_specs, out_specs=(tokens, tokens), check_vma=False
    )
```

```python
import functools

import jax
import jax.numpy as jnp
from jax import lax
from jax.experimental import pallas as pl
from jax.experimental.pallas import tpu as pltpu
from jax.sharding import PartitionSpec as P

SPLIT = 4
EPS = 1e-06
CONTRACT = (((1,), (1,)), ((), ()))
OVER_ROWS = (((0,), (0,)), ((), ()))
F32 = jnp.float32
BF16 = jnp.bfloat16


def shifted(value, axis, steps):
    count = lax.axis_size(axis)
    return lax.ppermute(value, axis, [(i, (i + steps) % count) for i in range(count)])


def swapped(value, axis, bit):
    count = lax.axis_size(axis)
    return lax.ppermute(value, axis, [(i, i ^ bit) for i in range(count)])


def local_call(body, out_shape, scratch=(), vmem_mib=16, **names):
    return pl.pallas_call(
        body,
        out_shape=out_shape,
        scratch_shapes=scratch,
        compiler_params=pltpu.CompilerParams(vmem_limit_bytes=vmem_mib << 20),
        cost_estimate=pl.CostEstimate(flops=1000, bytes_accessed=1000, transcendentals=0),
        **names,
    )


def silu_parts(values):
    sigma = jax.nn.sigmoid(values)
    return (values * sigma, sigma * (1.0 + values * (1.0 - sigma)))


def inverse_rms(values):
    return lax.rsqrt(jnp.mean(values * values, axis=-1, keepdims=True) + EPS)


def slots_of(routes, own, experts):
    count = routes.shape[1]
    height = -(-experts // 8) * 8
    ids = lax.broadcasted_iota(jnp.int32, (height, count), 0)
    onehot = (ids == routes).astype(F32)
    earlier = (
        lax.broadcasted_iota(jnp.int32, (count, count), 0) < lax.broadcasted_iota(jnp.int32, (count, count), 1)
    ).astype(F32)
    before = jnp.dot(onehot.astype(BF16), earlier.astype(BF16), preferred_element_type=F32)
    slot = jnp.sum(before * onehot, axis=0, keepdims=True).astype(jnp.int32)
    block = routes - own
    return (jnp.where(block < 0, block + experts, block), slot)


def chooser_of(block, slot, j, rows):
    place = lax.broadcasted_iota(jnp.int32, (rows, block.shape[1]), 0)
    return jnp.where((place == slot) & (block == j), 1.0, 0.0).astype(BF16)


def join_body(*refs):
    *parts, out, sems = refs
    units = parts[0].shape[0]
    copies = [
        pltpu.make_async_copy(part, out.at[pl.ds(i * units, units), :], sems.at[i]) for i, part in enumerate(parts)
    ]
    for copy in copies:
        copy.start()
    for copy in copies:
        copy.wait()


def pack_body(experts, own_ref, routes_ref, *refs):
    if len(refs) == experts + 2:
        gain_ref, x_ref, *outs = refs
        values = x_ref[...].astype(F32)
        values = (values * inverse_rms(values) * gain_ref[...]).astype(BF16)
    else:
        x_ref, *outs = refs
        values = x_ref[...]
    block, slot = slots_of(routes_ref[...], own_ref[0], experts)
    for j, out in enumerate(outs):
        chooser = chooser_of(block, slot, j, out.shape[0])
        out[...] = jnp.dot(chooser, values, preferred_element_type=F32).astype(BF16)


def gather_blocks(refs, wide_ref):
    rows = refs[0].shape[0]
    pitch = wide_ref.shape[0] // len(refs)
    for i, ref in enumerate(refs):
        wide_ref[pl.ds(i * pitch, rows), :] = ref[...]
    return pitch


def spread_out(total, refs, pitch):
    for i, ref in enumerate(refs):
        ref[...] = total[i * pitch:i * pitch + ref.shape[0]].astype(ref.dtype)


def thirds(share):
    units = share.shape[0] // 3
    return [share[pl.ds(i * units, units), :] for i in range(3)]


def forward_body(count, *refs):
    row_refs, refs = refs[:count], refs[count:]
    shares, refs = refs[:2], refs[2:]
    outs, wide_ref = refs[:-1], refs[-1]
    pitch = gather_blocks(row_refs, wide_ref)
    rows = wide_ref[...]
    total = None
    for share in shares:
        gate, up, down = thirds(share)
        gate_pre = lax.dot_general(rows, gate, CONTRACT, preferred_element_type=F32)
        up_pre = lax.dot_general(rows, up, CONTRACT, preferred_element_type=F32)
        hidden = (silu_parts(gate_pre)[0] * up_pre).astype(BF16)
        part = jnp.dot(hidden, down, preferred_element_type=F32)
        total = part if total is None else total + part
    spread_out(total, outs, pitch)


def backward_body(count, *refs):
    row_refs, grad_refs, refs = refs[:count], refs[count:2 * count], refs[2 * count:]
    shares, refs = refs[:2], refs[2:]
    outs, wide_ref, grad_wide_ref = refs[:-2], refs[-2], refs[-1]
    pitch = gather_blocks(row_refs, wide_ref)
    gather_blocks(grad_refs, grad_wide_ref)
    rows = wide_ref[...]
    grads = grad_wide_ref[...]
    total = None
    for share in shares:
        gate, up, down = thirds(share)
        gate_pre = lax.dot_general(rows, gate, CONTRACT, preferred_element_type=F32)
        up_pre = lax.dot_general(rows, up, CONTRACT, preferred_element_type=F32)
        activation, derivative = silu_parts(gate_pre)
        d_hidden = lax.dot_general(grads, down, CONTRACT, preferred_element_type=F32)
        d_gate = (d_hidden * up_pre * derivative).astype(BF16)
        d_up = (d_hidden * activation).astype(BF16)
        part = jnp.dot(d_gate, gate, preferred_element_type=F32)
        part = part + jnp.dot(d_up, up, preferred_element_type=F32)
        total = part if total is None else total + part
    spread_out(total, outs, pitch)


def routed_sum(experts, own_ref, routes_ref, gates_ref, home_refs):
    block, slot = slots_of(routes_ref[...], own_ref[0], experts)
    first, second, *crossed = home_refs
    own_rows = (first[...] + second[...].astype(F32)).astype(BF16)
    total = None
    for j in range(experts):
        rows = own_rows if j == 0 else crossed[j - 1][...]
        chooser = chooser_of(block, slot, j, rows.shape[0])
        part = lax.dot_general(chooser, rows, OVER_ROWS, preferred_element_type=F32)
        total = part if total is None else total + part
    count = block.shape[1]
    diagonal = lax.broadcasted_iota(jnp.int32, (count, count), 0) == lax.broadcasted_iota(
        jnp.int32, (count, count), 1
    )
    gates = jnp.sum(jnp.where(diagonal, gates_ref[...], 0.0), axis=1, keepdims=True)
    return total * gates


def forward_home_body(experts, own_ref, routes_ref, gates_ref, x_ref, *refs):
    mixed = routed_sum(experts, own_ref, routes_ref, gates_ref, refs[:-1])
    refs[-1][...] = (x_ref[...].astype(F32) + mixed).astype(BF16)


def backward_home_body(experts, own_ref, routes_ref, gates_ref, gain_ref, saved_ref, up_ref, *refs):
    d_norm = routed_sum(experts, own_ref, routes_ref, gates_ref, refs[:-1])
    base = saved_ref[...].astype(F32)
    inv_scale = inverse_rms(base)
    scaled = d_norm * gain_ref[...]
    d_input = inv_scale * (
        scaled - base * inv_scale * inv_scale * jnp.mean(scaled * base, axis=-1, keepdims=True)
    )
    refs[-1][...] = (up_ref[...].astype(F32) + d_input).astype(BF16)


def after(value, *others):
    return lax.optimization_barrier((value, *others))[0]


def crossed(blocks):
    return [blocks[0]] + [shifted(blocks[j], "expert", SPLIT * j) for j in range(1, len(blocks))]


def partners(blocks, *others):
    return [swapped(after(block, *others) if others else block, "expert", 2) for block in blocks]


def crossing_home(partial):
    experts = len(partial) // 2
    mine, theirs = partial[:experts], partial[experts:]
    totals = [
        (mine[j] + swapped(theirs[j], "expert", 2).astype(F32)).astype(BF16) for j in range(1, experts)
    ]
    return totals, [shifted(totals[j - 1], "expert", -SPLIT * j) for j in range(1, experts)]


def per_device(act_in, saved_in, grad_in, norm_gain, w_gate, w_up, w_down, routes_fwd, gates_fwd, routes_bwd, gates_bwd):
    experts = lax.axis_size("expert") // SPLIT
    own = (lax.axis_index("expert") // SPLIT).astype(jnp.int32).reshape(1)
    tok_count, top_count = routes_fwd.shape[1:]
    assert top_count == 1
    width = act_in.shape[2]
    rows = -(-min(tok_count, tok_count // experts + 2) // 8) * 8
    pitch = -(-rows // 16) * 16
    scalar = pl.BlockSpec(memory_space=pltpu.SMEM)
    whole = pl.BlockSpec(memory_space=pltpu.VMEM)

    packed = [jax.ShapeDtypeStruct((rows, width), BF16)] * experts
    partial = [jax.ShapeDtypeStruct((rows, width), F32)] * experts + packed
    tokens = jax.ShapeDtypeStruct((tok_count, width), BF16)
    wide = pltpu.VMEM((2 * experts * pitch, width), BF16)

    incoming = shifted(act_in[0], "section", 1)
    upstream = shifted(grad_in[0], "section", -1)
    r_fwd = routes_fwd.reshape(1, tok_count)
    r_bwd = routes_bwd.reshape(1, tok_count)
    g_fwd = gates_fwd.reshape(1, tok_count)
    g_bwd = gates_bwd.reshape(1, tok_count)

    def pack(name, routes, *args):
        return local_call(
            functools.partial(pack_body, experts),
            packed,
            in_specs=[scalar] + [whole] * (len(args) + 1),
            out_specs=[whole] * experts,
            name=name,
        )(own, routes, *args)

    own_share = local_call(
        join_body,
        jax.ShapeDtypeStruct((3 * w_down.shape[1], width), BF16),
        in_specs=[pl.BlockSpec(memory_space=pl.ANY)] * 3,
        out_specs=pl.BlockSpec(memory_space=pl.ANY),
        scratch=[pltpu.SemaphoreType.DMA((3,))],
        name="join_weights",
    )(w_gate[0].T, w_up[0].T, w_down[0])
    shares = (own_share, swapped(own_share, "expert", 1))

    packed_b = pack("pack_saved", r_bwd, norm_gain, saved_in[0])
    rows_b = crossed(packed_b)
    swap_b = partners(rows_b[:1])
    packed_g = pack("pack_grad", r_bwd, after(upstream, packed_b[0]))
    rows_g = crossed(packed_g)
    packed_f = pack("pack_act", r_fwd, norm_gain, after(incoming, packed_g[0], rows_b[-1]))
    rows_f = crossed(packed_f)
    swap_g = partners(rows_g[:1], rows_b[-1])
    swap_f = partners(rows_f[:1], rows_g[-1])
    rows_b = rows_b + swap_b + partners(rows_b[1:], swap_b[0])
    rows_g = rows_g + swap_g + partners(rows_g[1:], swap_g[0])
    rows_f = rows_f + swap_f + partners(rows_f[1:], swap_f[0], rows_b[-1])

    count = 2 * experts
    partial_b = local_call(
        functools.partial(backward_body, count), partial, scratch=[wide, wide], vmem_mib=40, name="experts_bwd"
    )(*rows_b, *rows_g, *shares)
    partial_f = local_call(
        functools.partial(forward_body, count), partial, scratch=[wide], vmem_mib=32, name="experts_fwd"
    )(after(rows_f[0], partial_b[0]), *rows_f[1:], *shares)
    totals_b, home_b = crossing_home(partial_b)
    totals_f, home_f = crossing_home(partial_f)
    back_b = [partial_b[0]] + partners(partial_b[experts:experts + 1], *totals_f) + home_b
    back_f = [partial_f[0]] + partners(partial_f[experts:experts + 1], *totals_f) + home_f

    grad_out = local_call(
        functools.partial(backward_home_body, experts),
        tokens,
        in_specs=[scalar] + [whole] * (6 + experts),
        out_specs=whole,
        name="home_bwd",
    )(own, r_bwd, g_bwd, norm_gain, saved_in[0], upstream, *back_b)
    act_out = local_call(
        functools.partial(forward_home_body, experts),
        tokens,
        in_specs=[scalar] + [whole] * (4 + experts),
        out_specs=whole,
        name="home_fwd",
    )(own, r_fwd, g_fwd, incoming, *back_f)
    return (act_out[None], grad_out[None])


def solution(mesh):
    tokens = P("section", "expert", None)
    in_specs = (
        tokens,
        tokens,
        tokens,
        P("section", None),
        P("section", None, "expert"),
        P("section", None, "expert"),
        tokens,
        tokens,
        tokens,
        tokens,
        tokens,
    )
    return jax.shard_map(
        per_device, mesh=mesh, in_specs=in_specs, out_specs=(tokens, tokens), check_vma=False
    )
```

```python
import functools
import math

import jax
import jax.numpy as jnp
from jax import lax
from jax.experimental import pallas as pl
from jax.experimental.pallas import tpu as pltpu
from jax.sharding import PartitionSpec as P

SPLIT = 4
EPS = 1e-06
CONTRACT = (((1,), (1,)), ((), ()))
OVER_ROWS = (((0,), (0,)), ((), ()))
F32 = jnp.float32
BF16 = jnp.bfloat16


def shifted(value, axis, steps):
    count = lax.axis_size(axis)
    return lax.ppermute(value, axis, [(i, (i + steps) % count) for i in range(count)])


def swapped(value, axis, bit):
    count = lax.axis_size(axis)
    return lax.ppermute(value, axis, [(i, i ^ bit) for i in range(count)])


def after(value, *others):
    return lax.optimization_barrier((value, *others))[0] if others else value


def local_call(body, out_shape, scratch=(), vmem_mib=16, **names):
    return pl.pallas_call(
        body,
        out_shape=out_shape,
        scratch_shapes=scratch,
        compiler_params=pltpu.CompilerParams(vmem_limit_bytes=vmem_mib << 20),
        cost_estimate=pl.CostEstimate(flops=1000, bytes_accessed=1000, transcendentals=0),
        **names,
    )


def silu_parts(values):
    sigma = jax.nn.sigmoid(values)
    return (values * sigma, sigma * (1.0 + values * (1.0 - sigma)))


def inverse_rms(values):
    return lax.rsqrt(jnp.mean(values * values, axis=-1, keepdims=True) + EPS)


def slots_of(routes, own, experts):
    count = routes.shape[1]
    height = -(-experts // 8) * 8
    ids = lax.broadcasted_iota(jnp.int32, (height, count), 0)
    onehot = (ids == routes).astype(F32)
    earlier = (
        lax.broadcasted_iota(jnp.int32, (count, count), 0) < lax.broadcasted_iota(jnp.int32, (count, count), 1)
    ).astype(F32)
    before = jnp.dot(onehot.astype(BF16), earlier.astype(BF16), preferred_element_type=F32)
    slot = jnp.sum(before * onehot, axis=0, keepdims=True).astype(jnp.int32)
    block = routes - own
    return (jnp.where(block < 0, block + experts, block), slot)


def chooser_of(block, slot, j, piece, rows, height):
    place = lax.broadcasted_iota(jnp.int32, (height, block.shape[1]), 0)
    return jnp.where((place == slot + piece * rows) & (block == j), 1.0, 0.0).astype(BF16)


def pack(values, own_ref, routes_ref, outs):
    experts = len(outs)
    height, cols = outs[0].shape
    pieces = values.shape[1] // cols
    rows = height // pieces
    block, slot = slots_of(routes_ref[...], own_ref[0], experts)
    for j, out in enumerate(outs):
        total = None
        for p in range(pieces):
            chooser = chooser_of(block, slot, j, p, rows, height)
            part = jnp.dot(chooser, values[:, p * cols:(p + 1) * cols], preferred_element_type=F32)
            total = part if total is None else total + part
        out[...] = total.astype(BF16)


def normed(x_ref, gain_ref):
    values = x_ref[...].astype(F32)
    return (values * inverse_rms(values) * gain_ref[...]).astype(BF16)


def pack_grad_body(own_ref, routes_ref, x_ref, *outs):
    pack(x_ref[...], own_ref, routes_ref, outs)


def pack_act_body(own_ref, routes_ref, gain_ref, x_ref, *outs):
    pack(normed(x_ref, gain_ref), own_ref, routes_ref, outs)


def first_body(own_ref, routes_ref, gain_ref, x_ref, *refs):
    parts, joined, outs, sems = refs[:3], refs[3], refs[4:-1], refs[-1]
    units = parts[0].shape[0]
    copies = [
        pltpu.make_async_copy(part, joined.at[pl.ds(i * units, units), :], sems.at[i]) for i, part in enumerate(parts)
    ]
    for copy in copies:
        copy.start()
    pack(normed(x_ref, gain_ref), own_ref, routes_ref, outs)
    for copy in copies:
        copy.wait()


def unpack(refs, wide_ref, rows):
    pitch = wide_ref.shape[0] // len(refs)
    pieces = refs[0].shape[0] // rows
    for i, ref in enumerate(refs):
        value = ref[...].astype(F32)
        whole = jnp.concatenate([value[p * rows:(p + 1) * rows] for p in range(pieces)], axis=1)
        wide_ref[pl.ds(i * pitch, rows), :] = whole.astype(BF16)
    return wide_ref[...]


def spread_out(total, refs, pitch, rows):
    for i, ref in enumerate(refs):
        cols = ref.shape[1]
        whole = total[i * pitch:i * pitch + rows]
        pieces = [whole[:, p * cols:(p + 1) * cols] for p in range(ref.shape[0] // rows)]
        ref[...] = jnp.concatenate(pieces, axis=0).astype(ref.dtype)


def third(shares, i):
    units = shares[0].shape[0] // 3
    return jnp.concatenate([share[pl.ds(i * units, units), :] for share in shares], axis=0)


def forward_body(count, rows, *refs):
    row_refs, shares, outs, wide_ref = refs[:count], refs[count:count + 2], refs[count + 2:-1], refs[-1]
    x = unpack(row_refs, wide_ref, rows)
    gate_pre = lax.dot_general(x, third(shares, 0), CONTRACT, preferred_element_type=F32)
    up_pre = lax.dot_general(x, third(shares, 1), CONTRACT, preferred_element_type=F32)
    hidden = (silu_parts(gate_pre)[0] * up_pre).astype(BF16)
    total = jnp.dot(hidden, third(shares, 2), preferred_element_type=F32)
    spread_out(total, outs, x.shape[0] // count, rows)


def backward_body(count, rows, *refs):
    row_refs, grad_refs, shares = refs[:count], refs[count:2 * count], refs[2 * count:2 * count + 2]
    outs, wide_ref, grad_wide_ref = refs[2 * count + 2:-2], refs[-2], refs[-1]
    x = unpack(row_refs, wide_ref, rows)
    gate, up = third(shares, 0), third(shares, 1)
    gate_pre = lax.dot_general(x, gate, CONTRACT, preferred_element_type=F32)
    up_pre = lax.dot_general(x, up, CONTRACT, preferred_element_type=F32)
    activation, derivative = silu_parts(gate_pre)
    grads = unpack(grad_refs, grad_wide_ref, rows)
    d_hidden = lax.dot_general(grads, third(shares, 2), CONTRACT, preferred_element_type=F32)
    d_gate = (d_hidden * up_pre * derivative).astype(BF16)
    d_up = (d_hidden * activation).astype(BF16)
    total = jnp.dot(d_gate, gate, preferred_element_type=F32) + jnp.dot(d_up, up, preferred_element_type=F32)
    spread_out(total, outs, x.shape[0] // count, rows)


def routed_sum(experts, rows, own_ref, routes_ref, gates_ref, home_refs):
    block, slot = slots_of(routes_ref[...], own_ref[0], experts)
    mine, theirs, *crossed_refs = home_refs
    blocks = [(mine[...] + theirs[...].astype(F32)).astype(BF16)] + [ref[...] for ref in crossed_refs]
    height = blocks[0].shape[0]
    columns = []
    for p in range(height // rows):
        total = None
        for j in range(experts):
            chooser = chooser_of(block, slot, j, p, rows, height)
            part = lax.dot_general(chooser, blocks[j], OVER_ROWS, preferred_element_type=F32)
            total = part if total is None else total + part
        columns.append(total)
    count = block.shape[1]
    diagonal = lax.broadcasted_iota(jnp.int32, (count, count), 0) == lax.broadcasted_iota(
        jnp.int32, (count, count), 1
    )
    gates = jnp.sum(jnp.where(diagonal, gates_ref[...], 0.0), axis=1, keepdims=True)
    return jnp.concatenate(columns, axis=1) * gates


def forward_home_body(experts, rows, own_ref, routes_ref, gates_ref, x_ref, *refs):
    mixed = routed_sum(experts, rows, own_ref, routes_ref, gates_ref, refs[:-1])
    refs[-1][...] = (x_ref[...].astype(F32) + mixed).astype(BF16)


def backward_home_body(experts, rows, own_ref, routes_ref, gates_ref, gain_ref, saved_ref, up_ref, *refs):
    d_norm = routed_sum(experts, rows, own_ref, routes_ref, gates_ref, refs[:-1])
    base = saved_ref[...].astype(F32)
    inv_scale = inverse_rms(base)
    scaled = d_norm * gain_ref[...]
    d_input = inv_scale * (
        scaled - base * inv_scale * inv_scale * jnp.mean(scaled * base, axis=-1, keepdims=True)
    )
    refs[-1][...] = (up_ref[...].astype(F32) + d_input).astype(BF16)


def crossed(blocks):
    return [blocks[0]] + [shifted(blocks[j], "expert", SPLIT * j) for j in range(1, len(blocks))]


def partners(blocks, *others):
    return [swapped(after(block, *others), "expert", 2) for block in blocks]


def crossing_home(partial):
    experts = len(partial) // 2
    mine, theirs = partial[:experts], partial[experts:]
    totals = [
        (mine[j] + swapped(theirs[j], "expert", 2).astype(F32)).astype(BF16) for j in range(1, experts)
    ]
    return totals, [shifted(totals[j - 1], "expert", -SPLIT * j) for j in range(1, experts)]


def per_device(act_in, saved_in, grad_in, norm_gain, w_gate, w_up, w_down, routes_fwd, gates_fwd, routes_bwd, gates_bwd):
    experts = lax.axis_size("expert") // SPLIT
    own = (lax.axis_index("expert") // SPLIT).astype(jnp.int32).reshape(1)
    tok_count, top_count = routes_fwd.shape[1:]
    assert top_count == 1
    width = act_in.shape[2]
    rows = min(tok_count, tok_count // experts + 2)
    pieces = 8 // math.gcd(rows, 8)
    pitch = -(-rows // 16) * 16
    scalar = pl.BlockSpec(memory_space=pltpu.SMEM)
    whole = pl.BlockSpec(memory_space=pltpu.VMEM)

    shape = (pieces * rows, width // pieces)
    packed = [jax.ShapeDtypeStruct(shape, BF16)] * experts
    partial = [jax.ShapeDtypeStruct(shape, F32)] * experts + packed
    tokens = jax.ShapeDtypeStruct((tok_count, width), BF16)
    wide = pltpu.VMEM((2 * experts * pitch, width), BF16)

    incoming = shifted(act_in[0], "section", 1)
    upstream = shifted(grad_in[0], "section", -1)
    r_fwd = routes_fwd.reshape(1, tok_count)
    r_bwd = routes_bwd.reshape(1, tok_count)
    g_fwd = gates_fwd.reshape(1, tok_count)
    g_bwd = gates_bwd.reshape(1, tok_count)

    own_share, *packed_b = local_call(
        first_body,
        [jax.ShapeDtypeStruct((3 * w_down.shape[1], width), BF16)] + packed,
        in_specs=[scalar] + [whole] * 3 + [pl.BlockSpec(memory_space=pltpu.HBM)] * 3,
        out_specs=[pl.BlockSpec(memory_space=pl.ANY)] + [whole] * experts,
        scratch=[pltpu.SemaphoreType.DMA((3,))],
        name="join_weights_pack_saved",
    )(own, r_bwd, norm_gain, saved_in[0], w_gate[0].T, w_up[0].T, w_down[0])
    shares = (own_share, swapped(own_share, "expert", 1))

    rows_b = crossed(packed_b)
    swap_b = partners(rows_b[:1])
    packed_g = local_call(
        pack_grad_body,
        packed,
        in_specs=[scalar] + [whole] * 2,
        out_specs=[whole] * experts,
        name="pack_grad",
    )(own, r_bwd, after(upstream, packed_b[0]))
    rows_g = crossed(packed_g)
    packed_f = local_call(
        pack_act_body,
        packed,
        in_specs=[scalar] + [whole] * 3,
        out_specs=[whole] * experts,
        name="pack_act",
    )(own, r_fwd, norm_gain, after(incoming, packed_g[0], rows_b[-1]))
    rows_f = crossed(packed_f)
    swap_g = partners(rows_g[:1], rows_b[-1])
    swap_f = partners(rows_f[:1], rows_g[-1])
    rows_b = rows_b + swap_b + partners(rows_b[1:], swap_b[0])
    rows_g = rows_g + swap_g + partners(rows_g[1:], swap_g[0])
    rows_f = rows_f + swap_f + partners(rows_f[1:], swap_f[0], rows_b[-1])

    count = 2 * experts
    partial_b = local_call(
        functools.partial(backward_body, count, rows), partial, scratch=[wide, wide], vmem_mib=40, name="experts_bwd"
    )(*rows_b, *rows_g, *shares)
    partial_f = local_call(
        functools.partial(forward_body, count, rows), partial, scratch=[wide], vmem_mib=32, name="experts_fwd"
    )(after(rows_f[0], partial_b[0]), *rows_f[1:], *shares)
    totals_b, home_b = crossing_home(partial_b)
    totals_f, home_f = crossing_home(partial_f)
    back_b = [partial_b[0]] + partners(partial_b[experts:experts + 1], *totals_b) + home_b
    back_f = [partial_f[0]] + partners(partial_f[experts:experts + 1], *totals_f) + home_f

    grad_out = local_call(
        functools.partial(backward_home_body, experts, rows),
        tokens,
        in_specs=[scalar] + [whole] * (6 + experts),
        out_specs=whole,
        name="home_bwd",
    )(own, r_bwd, g_bwd, norm_gain, saved_in[0], upstream, *back_b)
    act_out = local_call(
        functools.partial(forward_home_body, experts, rows),
        tokens,
        in_specs=[scalar] + [whole] * (4 + experts),
        out_specs=whole,
        name="home_fwd",
    )(own, r_fwd, g_fwd, incoming, *back_f)
    return (act_out[None], grad_out[None])


def solution(mesh):
    tokens = P("section", "expert", None)
    in_specs = (
        tokens,
        tokens,
        tokens,
        P("section", None),
        P("section", None, "expert"),
        P("section", None, "expert"),
        tokens,
        tokens,
        tokens,
        tokens,
        tokens,
    )
    return jax.shard_map(
        per_device, mesh=mesh, in_specs=in_specs, out_specs=(tokens, tokens), check_vma=False
    )
```

```python
import functools
import math

import jax
import jax.numpy as jnp
from jax import lax
from jax.experimental import pallas as pl
from jax.experimental.pallas import tpu as pltpu
from jax.sharding import PartitionSpec as P

SPLIT = 4
EPS = 1e-06
CONTRACT = (((1,), (1,)), ((), ()))
OVER_ROWS = (((0,), (0,)), ((), ()))
F32 = jnp.float32
BF16 = jnp.bfloat16


def shifted(value, axis, steps):
    count = lax.axis_size(axis)
    return lax.ppermute(value, axis, [(i, (i + steps) % count) for i in range(count)])


def swapped(value, axis, bit):
    count = lax.axis_size(axis)
    return lax.ppermute(value, axis, [(i, i ^ bit) for i in range(count)])


def after(value, *others):
    return lax.optimization_barrier((value, *others))[0] if others else value


def local_call(body, out_shape, scratch=(), vmem_mib=16, **names):
    return pl.pallas_call(
        body,
        out_shape=out_shape,
        scratch_shapes=scratch,
        compiler_params=pltpu.CompilerParams(vmem_limit_bytes=vmem_mib << 20),
        cost_estimate=pl.CostEstimate(flops=1000, bytes_accessed=1000, transcendentals=0),
        **names,
    )


def silu_parts(values):
    sigma = jax.nn.sigmoid(values)
    return (values * sigma, sigma * (1.0 + values * (1.0 - sigma)))


def inverse_rms(values):
    return lax.rsqrt(jnp.mean(values * values, axis=-1, keepdims=True) + EPS)


def slots_of(routes, own, experts):
    count = routes.shape[1]
    height = -(-experts // 8) * 8
    ids = lax.broadcasted_iota(jnp.int32, (height, count), 0)
    onehot = (ids == routes).astype(F32)
    earlier = (
        lax.broadcasted_iota(jnp.int32, (count, count), 0) < lax.broadcasted_iota(jnp.int32, (count, count), 1)
    ).astype(F32)
    before = jnp.dot(onehot.astype(BF16), earlier.astype(BF16), preferred_element_type=F32)
    slot = jnp.sum(before * onehot, axis=0, keepdims=True).astype(jnp.int32)
    block = routes - own
    return (jnp.where(block < 0, block + experts, block), slot)


def chooser_of(block, slot, j, piece, rows, height):
    place = lax.broadcasted_iota(jnp.int32, (height, block.shape[1]), 0)
    return jnp.where((place == slot + piece * rows) & (block == j), 1.0, 0.0).astype(BF16)


def pack(values, own_ref, routes_ref, outs):
    experts = len(outs)
    height, cols = outs[0].shape
    pieces = values.shape[1] // cols
    rows = height // pieces
    block, slot = slots_of(routes_ref[...], own_ref[0], experts)
    for j, out in enumerate(outs):
        total = None
        for p in range(pieces):
            chooser = chooser_of(block, slot, j, p, rows, height)
            part = jnp.dot(chooser, values[:, p * cols:(p + 1) * cols], preferred_element_type=F32)
            total = part if total is None else total + part
        out[...] = total.astype(BF16)


def normed(x_ref, gain_ref):
    values = x_ref[...].astype(F32)
    return (values * inverse_rms(values) * gain_ref[...]).astype(BF16)


def pack_grad_body(own_ref, routes_ref, x_ref, *outs):
    pack(x_ref[...], own_ref, routes_ref, outs)


def pack_act_body(own_ref, routes_ref, gain_ref, x_ref, *outs):
    pack(normed(x_ref, gain_ref), own_ref, routes_ref, outs)


def first_body(own_ref, routes_ref, gain_ref, x_ref, *refs):
    parts, joined, outs, sems = refs[:3], refs[3], refs[4:-1], refs[-1]
    units = parts[0].shape[0]
    copies = [
        pltpu.make_async_copy(part, joined.at[pl.ds(i * units, units), :], sems.at[i]) for i, part in enumerate(parts)
    ]
    for copy in copies:
        copy.start()
    pack(normed(x_ref, gain_ref), own_ref, routes_ref, outs)
    for copy in copies:
        copy.wait()


def unpack(refs, wide_ref, rows):
    pitch = wide_ref.shape[0] // len(refs)
    pieces = refs[0].shape[0] // rows
    for i, ref in enumerate(refs):
        value = ref[...].astype(F32)
        whole = jnp.concatenate([value[p * rows:(p + 1) * rows] for p in range(pieces)], axis=1)
        wide_ref[pl.ds(i * pitch, rows), :] = whole.astype(BF16)
    return wide_ref[...]


def spread_out(total, refs, pitch, rows):
    for i, ref in enumerate(refs):
        cols = ref.shape[1]
        whole = total[i * pitch:i * pitch + rows]
        pieces = [whole[:, p * cols:(p + 1) * cols] for p in range(ref.shape[0] // rows)]
        ref[...] = jnp.concatenate(pieces, axis=0).astype(ref.dtype)


def third(shares, i):
    units = shares[0].shape[0] // 3
    return jnp.concatenate([share[pl.ds(i * units, units), :] for share in shares], axis=0)


def forward_body(count, rows, *refs):
    row_refs, shares, outs, wide_ref = refs[:count], refs[count:count + 2], refs[count + 2:-1], refs[-1]
    x = unpack(row_refs, wide_ref, rows)
    gate_pre = lax.dot_general(x, third(shares, 0), CONTRACT, preferred_element_type=F32)
    up_pre = lax.dot_general(x, third(shares, 1), CONTRACT, preferred_element_type=F32)
    hidden = (silu_parts(gate_pre)[0] * up_pre).astype(BF16)
    total = jnp.dot(hidden, third(shares, 2), preferred_element_type=F32)
    spread_out(total, outs, x.shape[0] // count, rows)


def backward_body(count, rows, *refs):
    row_refs, grad_refs, shares = refs[:count], refs[count:2 * count], refs[2 * count:2 * count + 2]
    outs, wide_ref, grad_wide_ref = refs[2 * count + 2:-2], refs[-2], refs[-1]
    x = unpack(row_refs, wide_ref, rows)
    gate, up = third(shares, 0), third(shares, 1)
    gate_pre = lax.dot_general(x, gate, CONTRACT, preferred_element_type=F32)
    up_pre = lax.dot_general(x, up, CONTRACT, preferred_element_type=F32)
    activation, derivative = silu_parts(gate_pre)
    grads = unpack(grad_refs, grad_wide_ref, rows)
    d_hidden = lax.dot_general(grads, third(shares, 2), CONTRACT, preferred_element_type=F32)
    d_gate = (d_hidden * up_pre * derivative).astype(BF16)
    d_up = (d_hidden * activation).astype(BF16)
    total = jnp.dot(d_gate, gate, preferred_element_type=F32) + jnp.dot(d_up, up, preferred_element_type=F32)
    spread_out(total, outs, x.shape[0] // count, rows)


def routed_sum(experts, rows, own_ref, routes_ref, gates_ref, home_refs):
    block, slot = slots_of(routes_ref[...], own_ref[0], experts)
    mine, theirs, *crossed_refs = home_refs
    blocks = [(mine[...] + theirs[...].astype(F32)).astype(BF16)] + [ref[...] for ref in crossed_refs]
    height = blocks[0].shape[0]
    columns = []
    for p in range(height // rows):
        total = None
        for j in range(experts):
            chooser = chooser_of(block, slot, j, p, rows, height)
            part = lax.dot_general(chooser, blocks[j], OVER_ROWS, preferred_element_type=F32)
            total = part if total is None else total + part
        columns.append(total)
    count = block.shape[1]
    diagonal = lax.broadcasted_iota(jnp.int32, (count, count), 0) == lax.broadcasted_iota(
        jnp.int32, (count, count), 1
    )
    gates = jnp.sum(jnp.where(diagonal, gates_ref[...], 0.0), axis=1, keepdims=True)
    return jnp.concatenate(columns, axis=1) * gates


def forward_home_body(experts, rows, own_ref, routes_ref, gates_ref, x_ref, *refs):
    mixed = routed_sum(experts, rows, own_ref, routes_ref, gates_ref, refs[:-1])
    refs[-1][...] = (x_ref[...].astype(F32) + mixed).astype(BF16)


def backward_home_body(experts, rows, own_ref, routes_ref, gates_ref, gain_ref, saved_ref, up_ref, *refs):
    d_norm = routed_sum(experts, rows, own_ref, routes_ref, gates_ref, refs[:-1])
    base = saved_ref[...].astype(F32)
    inv_scale = inverse_rms(base)
    scaled = d_norm * gain_ref[...]
    d_input = inv_scale * (
        scaled - base * inv_scale * inv_scale * jnp.mean(scaled * base, axis=-1, keepdims=True)
    )
    refs[-1][...] = (up_ref[...].astype(F32) + d_input).astype(BF16)


def crossed(blocks):
    return [blocks[0]] + [shifted(blocks[j], "expert", SPLIT * j) for j in range(1, len(blocks))]


def partners(blocks, *others):
    return [swapped(after(block, *others), "expert", 2) for block in blocks]


def crossing_home(partial):
    experts = len(partial) // 2
    mine, theirs = partial[:experts], partial[experts:]
    totals = [
        (mine[j] + swapped(theirs[j], "expert", 2).astype(F32)).astype(BF16) for j in range(1, experts)
    ]
    return totals, [shifted(totals[j - 1], "expert", -SPLIT * j) for j in range(1, experts)]


def per_device(act_in, saved_in, grad_in, norm_gain, w_gate, w_up, w_down, routes_fwd, gates_fwd, routes_bwd, gates_bwd):
    experts = lax.axis_size("expert") // SPLIT
    own = (lax.axis_index("expert") // SPLIT).astype(jnp.int32).reshape(1)
    tok_count, top_count = routes_fwd.shape[1:]
    assert top_count == 1
    width = act_in.shape[2]
    rows = min(tok_count, tok_count // experts + 2)
    pieces = 8 // math.gcd(rows, 8)
    pitch = -(-rows // 16) * 16
    scalar = pl.BlockSpec(memory_space=pltpu.SMEM)
    whole = pl.BlockSpec(memory_space=pltpu.VMEM)

    shape = (pieces * rows, width // pieces)
    packed = [jax.ShapeDtypeStruct(shape, BF16)] * experts
    partial = [jax.ShapeDtypeStruct(shape, F32)] * experts + packed
    tokens = jax.ShapeDtypeStruct((tok_count, width), BF16)
    wide = pltpu.VMEM((2 * experts * pitch, width), BF16)

    incoming = shifted(act_in[0], "section", 1)
    upstream = shifted(grad_in[0], "section", -1)
    r_fwd = routes_fwd.reshape(1, tok_count)
    r_bwd = routes_bwd.reshape(1, tok_count)
    g_fwd = gates_fwd.reshape(1, tok_count)
    g_bwd = gates_bwd.reshape(1, tok_count)

    own_share, *packed_b = local_call(
        first_body,
        [jax.ShapeDtypeStruct((3 * w_down.shape[1], width), BF16)] + packed,
        in_specs=[scalar] + [whole] * 3 + [pl.BlockSpec(memory_space=pltpu.HBM)] * 3,
        out_specs=[pl.BlockSpec(memory_space=pl.ANY)] + [whole] * experts,
        scratch=[pltpu.SemaphoreType.DMA((3,))],
        vmem_mib=60,
        name="join_weights_pack_saved",
    )(own, r_bwd, norm_gain, saved_in[0], w_gate[0].T, w_up[0].T, w_down[0])
    shares = (own_share, swapped(own_share, "expert", 1))

    rows_b = crossed(packed_b)
    swap_b = partners(rows_b[:1])
    packed_g = local_call(
        pack_grad_body,
        packed,
        in_specs=[scalar] + [whole] * 2,
        out_specs=[whole] * experts,
        name="pack_grad",
    )(own, r_bwd, after(upstream, packed_b[0]))
    rows_g = crossed(packed_g)
    packed_f = local_call(
        pack_act_body,
        packed,
        in_specs=[scalar] + [whole] * 3,
        out_specs=[whole] * experts,
        name="pack_act",
    )(own, r_fwd, norm_gain, after(incoming, packed_g[0], rows_b[-1]))
    rows_f = crossed(packed_f)
    swap_g = partners(rows_g[:1], rows_b[-1])
    swap_f = partners(rows_f[:1], rows_g[-1])
    rows_b = rows_b + swap_b + partners(rows_b[1:], swap_b[0])
    rows_g = rows_g + swap_g + partners(rows_g[1:], swap_g[0])
    rows_f = rows_f + swap_f + partners(rows_f[1:], swap_f[0], rows_b[-1])

    count = 2 * experts
    partial_b = local_call(
        functools.partial(backward_body, count, rows), partial, scratch=[wide, wide], vmem_mib=40, name="experts_bwd"
    )(*rows_b, *rows_g, *shares)
    partial_f = local_call(
        functools.partial(forward_body, count, rows), partial, scratch=[wide], vmem_mib=32, name="experts_fwd"
    )(after(rows_f[0], partial_b[0]), *rows_f[1:], *shares)
    totals_b, home_b = crossing_home(partial_b)
    totals_f, home_f = crossing_home(partial_f)
    back_b = [partial_b[0]] + partners(partial_b[experts:experts + 1], *totals_b) + home_b
    back_f = [partial_f[0]] + partners(partial_f[experts:experts + 1], *totals_f) + home_f

    grad_out = local_call(
        functools.partial(backward_home_body, experts, rows),
        tokens,
        in_specs=[scalar] + [whole] * (6 + experts),
        out_specs=whole,
        name="home_bwd",
    )(own, r_bwd, g_bwd, norm_gain, saved_in[0], upstream, *back_b)
    act_out = local_call(
        functools.partial(forward_home_body, experts, rows),
        tokens,
        in_specs=[scalar] + [whole] * (4 + experts),
        out_specs=whole,
        name="home_fwd",
    )(own, r_fwd, g_fwd, incoming, *back_f)
    return (act_out[None], grad_out[None])


def solution(mesh):
    tokens = P("section", "expert", None)
    in_specs = (
        tokens,
        tokens,
        tokens,
        P("section", None),
        P("section", None, "expert"),
        P("section", None, "expert"),
        tokens,
        tokens,
        tokens,
        tokens,
        tokens,
    )
    return jax.shard_map(
        per_device, mesh=mesh, in_specs=in_specs, out_specs=(tokens, tokens), check_vma=False
    )
```

```python
import functools
import math

import jax
import jax.numpy as jnp
from jax import lax
from jax.experimental import pallas as pl
from jax.experimental.pallas import tpu as pltpu
from jax.sharding import PartitionSpec as P

SPLIT = 4
EPS = 1e-06
CONTRACT = (((1,), (1,)), ((), ()))
OVER_ROWS = (((0,), (0,)), ((), ()))
F32 = jnp.float32
BF16 = jnp.bfloat16


def shifted(value, axis, steps):
    count = lax.axis_size(axis)
    return lax.ppermute(value, axis, [(i, (i + steps) % count) for i in range(count)])


def swapped(value, axis, bit):
    count = lax.axis_size(axis)
    return lax.ppermute(value, axis, [(i, i ^ bit) for i in range(count)])


def both_shares(share):
    pairs = [[i, i + 1] for i in range(0, lax.axis_size("expert"), 2)]
    return lax.all_gather(share, "expert", axis_index_groups=pairs, tiled=True)


def after(value, *others):
    return lax.optimization_barrier((value, *others))[0] if others else value


def local_call(body, out_shape, scratch=(), vmem_mib=16, **names):
    return pl.pallas_call(
        body,
        out_shape=out_shape,
        scratch_shapes=scratch,
        compiler_params=pltpu.CompilerParams(vmem_limit_bytes=vmem_mib << 20),
        cost_estimate=pl.CostEstimate(flops=1000, bytes_accessed=1000, transcendentals=0),
        **names,
    )


def silu_parts(values):
    sigma = jax.nn.sigmoid(values)
    return (values * sigma, sigma * (1.0 + values * (1.0 - sigma)))


def inverse_rms(values):
    return lax.rsqrt(jnp.mean(values * values, axis=-1, keepdims=True) + EPS)


def slots_of(routes, own, experts):
    count = routes.shape[1]
    height = -(-experts // 8) * 8
    ids = lax.broadcasted_iota(jnp.int32, (height, count), 0)
    onehot = (ids == routes).astype(F32)
    earlier = (
        lax.broadcasted_iota(jnp.int32, (count, count), 0) < lax.broadcasted_iota(jnp.int32, (count, count), 1)
    ).astype(F32)
    before = jnp.dot(onehot.astype(BF16), earlier.astype(BF16), preferred_element_type=F32)
    slot = jnp.sum(before * onehot, axis=0, keepdims=True).astype(jnp.int32)
    block = routes - own
    return (jnp.where(block < 0, block + experts, block), slot)


def chooser_of(block, slot, j, piece, rows, height):
    place = lax.broadcasted_iota(jnp.int32, (height, block.shape[1]), 0)
    return jnp.where((place == slot + piece * rows) & (block == j), 1.0, 0.0).astype(BF16)


def pack(values, own_ref, routes_ref, outs):
    experts = len(outs)
    height, cols = outs[0].shape
    pieces = values.shape[1] // cols
    rows = height // pieces
    block, slot = slots_of(routes_ref[...], own_ref[0], experts)
    for j, out in enumerate(outs):
        total = None
        for p in range(pieces):
            chooser = chooser_of(block, slot, j, p, rows, height)
            part = jnp.dot(chooser, values[:, p * cols:(p + 1) * cols], preferred_element_type=F32)
            total = part if total is None else total + part
        out[...] = total.astype(BF16)


def normed(x_ref, gain_ref):
    values = x_ref[...].astype(F32)
    return (values * inverse_rms(values) * gain_ref[...]).astype(BF16)


def pack_grad_body(own_ref, routes_ref, x_ref, *outs):
    pack(x_ref[...], own_ref, routes_ref, outs)


def pack_act_body(own_ref, routes_ref, gain_ref, x_ref, *outs):
    pack(normed(x_ref, gain_ref), own_ref, routes_ref, outs)


def unpack(refs, wide_ref, rows):
    pitch = wide_ref.shape[0] // len(refs)
    pieces = refs[0].shape[0] // rows
    for i, ref in enumerate(refs):
        value = ref[...].astype(F32)
        whole = jnp.concatenate([value[p * rows:(p + 1) * rows] for p in range(pieces)], axis=1)
        wide_ref[pl.ds(i * pitch, rows), :] = whole.astype(BF16)
    return wide_ref[...]


def spread_out(total, refs, pitch, rows):
    for i, ref in enumerate(refs):
        cols = ref.shape[1]
        whole = total[i * pitch:i * pitch + rows]
        pieces = [whole[:, p * cols:(p + 1) * cols] for p in range(ref.shape[0] // rows)]
        ref[...] = jnp.concatenate(pieces, axis=0).astype(ref.dtype)


def forward_body(count, rows, *refs):
    row_refs, shares, outs, wide_ref = refs[:count], refs[count:count + 3], refs[count + 3:-1], refs[-1]
    x = unpack(row_refs, wide_ref, rows)
    gate_pre = lax.dot_general(x, shares[0][...], CONTRACT, preferred_element_type=F32)
    up_pre = lax.dot_general(x, shares[1][...], CONTRACT, preferred_element_type=F32)
    hidden = (silu_parts(gate_pre)[0] * up_pre).astype(BF16)
    total = jnp.dot(hidden, shares[2][...], preferred_element_type=F32)
    spread_out(total, outs, x.shape[0] // count, rows)


def backward_body(count, rows, *refs):
    row_refs, grad_refs, shares = refs[:count], refs[count:2 * count], refs[2 * count:2 * count + 3]
    outs, wide_ref, grad_wide_ref = refs[2 * count + 3:-2], refs[-2], refs[-1]
    x = unpack(row_refs, wide_ref, rows)
    gate, up = shares[0][...], shares[1][...]
    gate_pre = lax.dot_general(x, gate, CONTRACT, preferred_element_type=F32)
    up_pre = lax.dot_general(x, up, CONTRACT, preferred_element_type=F32)
    activation, derivative = silu_parts(gate_pre)
    grads = unpack(grad_refs, grad_wide_ref, rows)
    d_hidden = lax.dot_general(grads, shares[2][...], CONTRACT, preferred_element_type=F32)
    d_gate = (d_hidden * up_pre * derivative).astype(BF16)
    d_up = (d_hidden * activation).astype(BF16)
    total = jnp.dot(d_gate, gate, preferred_element_type=F32) + jnp.dot(d_up, up, preferred_element_type=F32)
    spread_out(total, outs, x.shape[0] // count, rows)


def routed_sum(experts, rows, own_ref, routes_ref, gates_ref, home_refs):
    block, slot = slots_of(routes_ref[...], own_ref[0], experts)
    mine, theirs, *crossed_refs = home_refs
    blocks = [(mine[...] + theirs[...].astype(F32)).astype(BF16)] + [ref[...] for ref in crossed_refs]
    height = blocks[0].shape[0]
    columns = []
    for p in range(height // rows):
        total = None
        for j in range(experts):
            chooser = chooser_of(block, slot, j, p, rows, height)
            part = lax.dot_general(chooser, blocks[j], OVER_ROWS, preferred_element_type=F32)
            total = part if total is None else total + part
        columns.append(total)
    count = block.shape[1]
    diagonal = lax.broadcasted_iota(jnp.int32, (count, count), 0) == lax.broadcasted_iota(
        jnp.int32, (count, count), 1
    )
    gates = jnp.sum(jnp.where(diagonal, gates_ref[...], 0.0), axis=1, keepdims=True)
    return jnp.concatenate(columns, axis=1) * gates


def forward_home_body(experts, rows, own_ref, routes_ref, gates_ref, x_ref, *refs):
    mixed = routed_sum(experts, rows, own_ref, routes_ref, gates_ref, refs[:-1])
    refs[-1][...] = (x_ref[...].astype(F32) + mixed).astype(BF16)


def backward_home_body(experts, rows, own_ref, routes_ref, gates_ref, gain_ref, saved_ref, up_ref, *refs):
    d_norm = routed_sum(experts, rows, own_ref, routes_ref, gates_ref, refs[:-1])
    base = saved_ref[...].astype(F32)
    inv_scale = inverse_rms(base)
    scaled = d_norm * gain_ref[...]
    d_input = inv_scale * (
        scaled - base * inv_scale * inv_scale * jnp.mean(scaled * base, axis=-1, keepdims=True)
    )
    refs[-1][...] = (up_ref[...].astype(F32) + d_input).astype(BF16)


def crossed(blocks):
    return [blocks[0]] + [shifted(blocks[j], "expert", SPLIT * j) for j in range(1, len(blocks))]


def partners(blocks, *others):
    return [swapped(after(block, *others), "expert", 2) for block in blocks]


def crossing_home(partial):
    experts = len(partial) // 2
    mine, theirs = partial[:experts], partial[experts:]
    totals = [
        (mine[j] + swapped(theirs[j], "expert", 2).astype(F32)).astype(BF16) for j in range(1, experts)
    ]
    return totals, [shifted(totals[j - 1], "expert", -SPLIT * j) for j in range(1, experts)]


def per_device(act_in, saved_in, grad_in, norm_gain, w_gate, w_up, w_down, routes_fwd, gates_fwd, routes_bwd, gates_bwd):
    experts = lax.axis_size("expert") // SPLIT
    own = (lax.axis_index("expert") // SPLIT).astype(jnp.int32).reshape(1)
    tok_count, top_count = routes_fwd.shape[1:]
    assert top_count == 1
    width = act_in.shape[2]
    rows = min(tok_count, tok_count // experts + 2)
    pieces = 8 // math.gcd(rows, 8)
    pitch = -(-rows // 16) * 16
    scalar = pl.BlockSpec(memory_space=pltpu.SMEM)
    whole = pl.BlockSpec(memory_space=pltpu.VMEM)

    shape = (pieces * rows, width // pieces)
    packed = [jax.ShapeDtypeStruct(shape, BF16)] * experts
    partial = [jax.ShapeDtypeStruct(shape, F32)] * experts + packed
    tokens = jax.ShapeDtypeStruct((tok_count, width), BF16)
    wide = pltpu.VMEM((2 * experts * pitch, width), BF16)

    incoming = shifted(act_in[0], "section", 1)
    upstream = shifted(grad_in[0], "section", -1)
    r_fwd = routes_fwd.reshape(1, tok_count)
    r_bwd = routes_bwd.reshape(1, tok_count)
    g_fwd = gates_fwd.reshape(1, tok_count)
    g_bwd = gates_bwd.reshape(1, tok_count)

    packed_b = local_call(
        pack_act_body,
        packed,
        in_specs=[scalar] + [whole] * 3,
        out_specs=[whole] * experts,
        name="pack_saved",
    )(own, r_bwd, norm_gain, saved_in[0])
    shares = [both_shares(share) for share in (w_gate[0].T, w_up[0].T, w_down[0])]

    rows_b = crossed(packed_b)
    swap_b = partners(rows_b[:1])
    packed_g = local_call(
        pack_grad_body,
        packed,
        in_specs=[scalar] + [whole] * 2,
        out_specs=[whole] * experts,
        name="pack_grad",
    )(own, r_bwd, after(upstream, packed_b[0]))
    rows_g = crossed(packed_g)
    packed_f = local_call(
        pack_act_body,
        packed,
        in_specs=[scalar] + [whole] * 3,
        out_specs=[whole] * experts,
        name="pack_act",
    )(own, r_fwd, norm_gain, after(incoming, packed_g[0], rows_b[-1]))
    rows_f = crossed(packed_f)
    swap_g = partners(rows_g[:1], rows_b[-1])
    swap_f = partners(rows_f[:1], rows_g[-1])
    rows_b = rows_b + swap_b + partners(rows_b[1:], swap_b[0])
    rows_g = rows_g + swap_g + partners(rows_g[1:], swap_g[0])
    rows_f = rows_f + swap_f + partners(rows_f[1:], swap_f[0], rows_b[-1])

    count = 2 * experts
    partial_b = local_call(
        functools.partial(backward_body, count, rows), partial, scratch=[wide, wide], vmem_mib=40, name="experts_bwd"
    )(*rows_b, *rows_g, *shares)
    partial_f = local_call(
        functools.partial(forward_body, count, rows), partial, scratch=[wide], vmem_mib=32, name="experts_fwd"
    )(after(rows_f[0], partial_b[0]), *rows_f[1:], *shares)
    totals_b, home_b = crossing_home(partial_b)
    totals_f, home_f = crossing_home(partial_f)
    back_b = [partial_b[0]] + partners(partial_b[experts:experts + 1], *totals_b) + home_b
    back_f = [partial_f[0]] + partners(partial_f[experts:experts + 1], *totals_f, back_b[1]) + home_f

    grad_out = local_call(
        functools.partial(backward_home_body, experts, rows),
        tokens,
        in_specs=[scalar] + [whole] * (6 + experts),
        out_specs=whole,
        name="home_bwd",
    )(own, r_bwd, g_bwd, norm_gain, saved_in[0], upstream, *back_b)
    act_out = local_call(
        functools.partial(forward_home_body, experts, rows),
        tokens,
        in_specs=[scalar] + [whole] * (4 + experts),
        out_specs=whole,
        name="home_fwd",
    )(own, r_fwd, g_fwd, incoming, *back_f)
    return (act_out[None], grad_out[None])


def solution(mesh):
    tokens = P("section", "expert", None)
    in_specs = (
        tokens,
        tokens,
        tokens,
        P("section", None),
        P("section", None, "expert"),
        P("section", None, "expert"),
        tokens,
        tokens,
        tokens,
        tokens,
        tokens,
    )
    return jax.shard_map(
        per_device, mesh=mesh, in_specs=in_specs, out_specs=(tokens, tokens), check_vma=False
    )
```

```python
import functools
import math

import jax
import jax.numpy as jnp
from jax import lax
from jax.experimental import pallas as pl
from jax.experimental.pallas import tpu as pltpu
from jax.sharding import PartitionSpec as P

SPLIT = 4
EPS = 1e-06
CONTRACT = (((1,), (1,)), ((), ()))
OVER_ROWS = (((0,), (0,)), ((), ()))
F32 = jnp.float32
BF16 = jnp.bfloat16


def shifted(value, axis, steps):
    count = lax.axis_size(axis)
    return lax.ppermute(value, axis, [(i, (i + steps) % count) for i in range(count)])


def swapped(value, axis, bit):
    count = lax.axis_size(axis)
    return lax.ppermute(value, axis, [(i, i ^ bit) for i in range(count)])


def both_shares(share):
    pairs = [[i, i + 1] for i in range(0, lax.axis_size("expert"), 2)]
    return lax.all_gather(share, "expert", axis_index_groups=pairs, tiled=True)


def after(value, *others):
    return lax.optimization_barrier((value, *others))[0] if others else value


def local_call(body, out_shape, scratch=(), vmem_mib=16, **names):
    return pl.pallas_call(
        body,
        out_shape=out_shape,
        scratch_shapes=scratch,
        compiler_params=pltpu.CompilerParams(vmem_limit_bytes=vmem_mib << 20),
        cost_estimate=pl.CostEstimate(flops=1000, bytes_accessed=1000, transcendentals=0),
        **names,
    )


def silu_parts(values):
    sigma = jax.nn.sigmoid(values)
    return (values * sigma, sigma * (1.0 + values * (1.0 - sigma)))


def inverse_rms(values):
    return lax.rsqrt(jnp.mean(values * values, axis=-1, keepdims=True) + EPS)


def slots_of(routes, own, experts):
    count = routes.shape[1]
    height = -(-experts // 8) * 8
    ids = lax.broadcasted_iota(jnp.int32, (height, count), 0)
    onehot = (ids == routes).astype(F32)
    earlier = (
        lax.broadcasted_iota(jnp.int32, (count, count), 0) < lax.broadcasted_iota(jnp.int32, (count, count), 1)
    ).astype(F32)
    before = jnp.dot(onehot.astype(BF16), earlier.astype(BF16), preferred_element_type=F32)
    slot = jnp.sum(before * onehot, axis=0, keepdims=True).astype(jnp.int32)
    block = routes - own
    return (jnp.where(block < 0, block + experts, block), slot)


def chooser_of(block, slot, j, piece, rows, height):
    place = lax.broadcasted_iota(jnp.int32, (height, block.shape[1]), 0)
    return jnp.where((place == slot + piece * rows) & (block == j), 1.0, 0.0).astype(BF16)


def pack(values, own_ref, routes_ref, outs):
    experts = len(outs)
    height, cols = outs[0].shape
    pieces = values.shape[1] // cols
    rows = height // pieces
    block, slot = slots_of(routes_ref[...], own_ref[0], experts)
    for j, out in enumerate(outs):
        total = None
        for p in range(pieces):
            chooser = chooser_of(block, slot, j, p, rows, height)
            part = jnp.dot(chooser, values[:, p * cols:(p + 1) * cols], preferred_element_type=F32)
            total = part if total is None else total + part
        out[...] = total.astype(BF16)


def normed(x_ref, gain_ref):
    values = x_ref[...].astype(F32)
    return (values * inverse_rms(values) * gain_ref[...]).astype(BF16)


def pack_grad_body(own_ref, routes_ref, x_ref, *outs):
    pack(x_ref[...], own_ref, routes_ref, outs)


def pack_act_body(own_ref, routes_ref, gain_ref, x_ref, *outs):
    pack(normed(x_ref, gain_ref), own_ref, routes_ref, outs)


def unpack(refs, wide_ref, rows):
    pitch = wide_ref.shape[0] // len(refs)
    pieces = refs[0].shape[0] // rows
    for i, ref in enumerate(refs):
        value = ref[...].astype(F32)
        whole = jnp.concatenate([value[p * rows:(p + 1) * rows] for p in range(pieces)], axis=1)
        wide_ref[pl.ds(i * pitch, rows), :] = whole.astype(BF16)
    return wide_ref[...]


def spread_out(total, refs, pitch, rows):
    for i, ref in enumerate(refs):
        cols = ref.shape[1]
        whole = total[i * pitch:i * pitch + rows]
        pieces = [whole[:, p * cols:(p + 1) * cols] for p in range(ref.shape[0] // rows)]
        ref[...] = jnp.concatenate(pieces, axis=0).astype(ref.dtype)


def whole_shares(refs):
    side_ref, gate, other_gate, up, other_up, both_down = refs
    units = gate.shape[0]
    first = pl.multiple_of(side_ref[0] * units, units)
    down = [both_down[pl.ds(first, units), :], both_down[pl.ds(units - first, units), :]]
    return [
        jnp.concatenate(parts, axis=0)
        for parts in ((gate[...], other_gate[...]), (up[...], other_up[...]), down)
    ]


def forward_body(count, rows, *refs):
    row_refs, shares, outs, wide_ref = refs[:count], refs[count:count + 6], refs[count + 6:-1], refs[-1]
    x = unpack(row_refs, wide_ref, rows)
    gate, up, down = whole_shares(shares)
    gate_pre = lax.dot_general(x, gate, CONTRACT, preferred_element_type=F32)
    up_pre = lax.dot_general(x, up, CONTRACT, preferred_element_type=F32)
    hidden = (silu_parts(gate_pre)[0] * up_pre).astype(BF16)
    total = jnp.dot(hidden, down, preferred_element_type=F32)
    spread_out(total, outs, x.shape[0] // count, rows)


def backward_body(count, rows, *refs):
    row_refs, grad_refs, shares = refs[:count], refs[count:2 * count], refs[2 * count:2 * count + 6]
    outs, wide_ref, grad_wide_ref = refs[2 * count + 6:-2], refs[-2], refs[-1]
    x = unpack(row_refs, wide_ref, rows)
    gate, up, down = whole_shares(shares)
    gate_pre = lax.dot_general(x, gate, CONTRACT, preferred_element_type=F32)
    up_pre = lax.dot_general(x, up, CONTRACT, preferred_element_type=F32)
    activation, derivative = silu_parts(gate_pre)
    grads = unpack(grad_refs, grad_wide_ref, rows)
    d_hidden = lax.dot_general(grads, down, CONTRACT, preferred_element_type=F32)
    d_gate = (d_hidden * up_pre * derivative).astype(BF16)
    d_up = (d_hidden * activation).astype(BF16)
    total = jnp.dot(d_gate, gate, preferred_element_type=F32) + jnp.dot(d_up, up, preferred_element_type=F32)
    spread_out(total, outs, x.shape[0] // count, rows)


def routed_sum(experts, rows, own_ref, routes_ref, gates_ref, home_refs):
    block, slot = slots_of(routes_ref[...], own_ref[0], experts)
    mine, theirs, *crossed_refs = home_refs
    blocks = [(mine[...] + theirs[...].astype(F32)).astype(BF16)] + [ref[...] for ref in crossed_refs]
    height = blocks[0].shape[0]
    columns = []
    for p in range(height // rows):
        total = None
        for j in range(experts):
            chooser = chooser_of(block, slot, j, p, rows, height)
            part = lax.dot_general(chooser, blocks[j], OVER_ROWS, preferred_element_type=F32)
            total = part if total is None else total + part
        columns.append(total)
    count = block.shape[1]
    diagonal = lax.broadcasted_iota(jnp.int32, (count, count), 0) == lax.broadcasted_iota(
        jnp.int32, (count, count), 1
    )
    gates = jnp.sum(jnp.where(diagonal, gates_ref[...], 0.0), axis=1, keepdims=True)
    return jnp.concatenate(columns, axis=1) * gates


def forward_home_body(experts, rows, own_ref, routes_ref, gates_ref, x_ref, *refs):
    mixed = routed_sum(experts, rows, own_ref, routes_ref, gates_ref, refs[:-1])
    refs[-1][...] = (x_ref[...].astype(F32) + mixed).astype(BF16)


def backward_home_body(experts, rows, own_ref, routes_ref, gates_ref, gain_ref, saved_ref, up_ref, *refs):
    d_norm = routed_sum(experts, rows, own_ref, routes_ref, gates_ref, refs[:-1])
    base = saved_ref[...].astype(F32)
    inv_scale = inverse_rms(base)
    scaled = d_norm * gain_ref[...]
    d_input = inv_scale * (
        scaled - base * inv_scale * inv_scale * jnp.mean(scaled * base, axis=-1, keepdims=True)
    )
    refs[-1][...] = (up_ref[...].astype(F32) + d_input).astype(BF16)


def crossed(blocks):
    return [blocks[0]] + [shifted(blocks[j], "expert", SPLIT * j) for j in range(1, len(blocks))]


def partners(blocks, *others):
    return [swapped(after(block, *others), "expert", 2) for block in blocks]


def crossing_home(partial):
    experts = len(partial) // 2
    mine, theirs = partial[:experts], partial[experts:]
    totals = [
        (mine[j] + swapped(theirs[j], "expert", 2).astype(F32)).astype(BF16) for j in range(1, experts)
    ]
    return totals, [shifted(totals[j - 1], "expert", -SPLIT * j) for j in range(1, experts)]


def per_device(act_in, saved_in, grad_in, norm_gain, w_gate, w_up, w_down, routes_fwd, gates_fwd, routes_bwd, gates_bwd):
    experts = lax.axis_size("expert") // SPLIT
    own = (lax.axis_index("expert") // SPLIT).astype(jnp.int32).reshape(1)
    tok_count, top_count = routes_fwd.shape[1:]
    assert top_count == 1
    width = act_in.shape[2]
    rows = min(tok_count, tok_count // experts + 2)
    pieces = 8 // math.gcd(rows, 8)
    pitch = -(-rows // 16) * 16
    scalar = pl.BlockSpec(memory_space=pltpu.SMEM)
    whole = pl.BlockSpec(memory_space=pltpu.VMEM)

    shape = (pieces * rows, width // pieces)
    packed = [jax.ShapeDtypeStruct(shape, BF16)] * experts
    partial = [jax.ShapeDtypeStruct(shape, F32)] * experts + packed
    tokens = jax.ShapeDtypeStruct((tok_count, width), BF16)
    wide = pltpu.VMEM((2 * experts * pitch, width), BF16)

    incoming = shifted(act_in[0], "section", 1)
    upstream = shifted(grad_in[0], "section", -1)
    r_fwd = routes_fwd.reshape(1, tok_count)
    r_bwd = routes_bwd.reshape(1, tok_count)
    g_fwd = gates_fwd.reshape(1, tok_count)
    g_bwd = gates_bwd.reshape(1, tok_count)

    packed_b = local_call(
        pack_act_body,
        packed,
        in_specs=[scalar] + [whole] * 3,
        out_specs=[whole] * experts,
        name="pack_saved",
    )(own, r_bwd, norm_gain, saved_in[0])
    gate, up = w_gate[0].T, w_up[0].T
    both_down = both_shares(w_down[0])
    other_gate = swapped(gate, "expert", 1)

    rows_b = crossed(packed_b)
    swap_b = partners(rows_b[:1])
    packed_g = local_call(
        pack_grad_body,
        packed,
        in_specs=[scalar] + [whole] * 2,
        out_specs=[whole] * experts,
        name="pack_grad",
    )(own, r_bwd, after(upstream, packed_b[0]))
    rows_g = crossed(packed_g)
    packed_f = local_call(
        pack_act_body,
        packed,
        in_specs=[scalar] + [whole] * 3,
        out_specs=[whole] * experts,
        name="pack_act",
    )(own, r_fwd, norm_gain, after(incoming, packed_g[0], rows_b[-1]))
    rows_f = crossed(packed_f)
    swap_g = partners(rows_g[:1], rows_b[-1])
    swap_f = partners(rows_f[:1], rows_g[-1])
    other_up = swapped(up, "expert", 1)
    side = (lax.axis_index("expert") % 2).astype(jnp.int32).reshape(1)
    shares = (side, gate, other_gate, up, other_up, both_down)
    rows_b = rows_b + swap_b + partners(rows_b[1:], swap_b[0])
    rows_g = rows_g + swap_g + partners(rows_g[1:], swap_g[0])
    rows_f = rows_f + swap_f + partners(rows_f[1:], swap_f[0], rows_b[-1])

    count = 2 * experts
    weight_specs = [scalar] + [whole] * 5
    partial_b = local_call(
        functools.partial(backward_body, count, rows), partial, scratch=[wide, wide], vmem_mib=32, in_specs=[whole] * 2 * count + weight_specs, name="experts_bwd"
    )(*rows_b, *rows_g, *shares)
    partial_f = local_call(
        functools.partial(forward_body, count, rows), partial, scratch=[wide], vmem_mib=24, in_specs=[whole] * count + weight_specs, name="experts_fwd"
    )(after(rows_f[0], partial_b[0]), *rows_f[1:], *shares)
    totals_b, home_b = crossing_home(partial_b)
    totals_f, home_f = crossing_home(partial_f)
    back_b = [partial_b[0]] + partners(partial_b[experts:experts + 1], *totals_b) + home_b
    back_f = [partial_f[0]] + partners(partial_f[experts:experts + 1], *totals_f, back_b[1]) + home_f

    grad_out = local_call(
        functools.partial(backward_home_body, experts, rows),
        tokens,
        in_specs=[scalar] + [whole] * (6 + experts),
        out_specs=whole,
        name="home_bwd",
    )(own, r_bwd, g_bwd, norm_gain, saved_in[0], upstream, *back_b)
    act_out = local_call(
        functools.partial(forward_home_body, experts, rows),
        tokens,
        in_specs=[scalar] + [whole] * (4 + experts),
        out_specs=whole,
        name="home_fwd",
    )(own, r_fwd, g_fwd, incoming, *back_f)
    return (act_out[None], grad_out[None])


def solution(mesh):
    tokens = P("section", "expert", None)
    in_specs = (
        tokens,
        tokens,
        tokens,
        P("section", None),
        P("section", None, "expert"),
        P("section", None, "expert"),
        tokens,
        tokens,
        tokens,
        tokens,
        tokens,
    )
    return jax.shard_map(
        per_device, mesh=mesh, in_specs=in_specs, out_specs=(tokens, tokens), check_vma=False
    )
```

```python
import functools
import math

import jax
import jax.numpy as jnp
from jax import lax
from jax.experimental import pallas as pl
from jax.experimental.pallas import tpu as pltpu
from jax.sharding import PartitionSpec as P

SPLIT = 4
EPS = 1e-06
CONTRACT = (((1,), (1,)), ((), ()))
OVER_ROWS = (((0,), (0,)), ((), ()))
F32 = jnp.float32
BF16 = jnp.bfloat16


def shifted(value, axis, steps):
    count = lax.axis_size(axis)
    return lax.ppermute(value, axis, [(i, (i + steps) % count) for i in range(count)])


def swapped(value, axis, bit):
    count = lax.axis_size(axis)
    return lax.ppermute(value, axis, [(i, i ^ bit) for i in range(count)])


def after(value, *others):
    return lax.optimization_barrier((value, *others))[0] if others else value


def local_call(body, out_shape, scratch=(), vmem_mib=16, **names):
    return pl.pallas_call(
        body,
        out_shape=out_shape,
        scratch_shapes=scratch,
        compiler_params=pltpu.CompilerParams(vmem_limit_bytes=vmem_mib << 20),
        cost_estimate=pl.CostEstimate(flops=1000, bytes_accessed=1000, transcendentals=0),
        **names,
    )


def silu_parts(values):
    sigma = jax.nn.sigmoid(values)
    return (values * sigma, sigma * (1.0 + values * (1.0 - sigma)))


def inverse_rms(values):
    return lax.rsqrt(jnp.mean(values * values, axis=-1, keepdims=True) + EPS)


def slots_of(routes, own, experts):
    count = routes.shape[1]
    height = -(-experts // 8) * 8
    ids = lax.broadcasted_iota(jnp.int32, (height, count), 0)
    onehot = (ids == routes).astype(F32)
    earlier = (
        lax.broadcasted_iota(jnp.int32, (count, count), 0) < lax.broadcasted_iota(jnp.int32, (count, count), 1)
    ).astype(F32)
    before = jnp.dot(onehot.astype(BF16), earlier.astype(BF16), preferred_element_type=F32)
    slot = jnp.sum(before * onehot, axis=0, keepdims=True).astype(jnp.int32)
    block = routes - own
    return (jnp.where(block < 0, block + experts, block), slot)


def chooser_of(block, slot, j, piece, rows, height):
    place = lax.broadcasted_iota(jnp.int32, (height, block.shape[1]), 0)
    return jnp.where((place == slot + piece * rows) & (block == j), 1.0, 0.0).astype(BF16)


def pack(values, own_ref, routes_ref, outs):
    experts = len(outs)
    height, cols = outs[0].shape
    pieces = values.shape[1] // cols
    rows = height // pieces
    block, slot = slots_of(routes_ref[...], own_ref[0], experts)
    for j, out in enumerate(outs):
        total = None
        for p in range(pieces):
            chooser = chooser_of(block, slot, j, p, rows, height)
            part = jnp.dot(chooser, values[:, p * cols:(p + 1) * cols], preferred_element_type=F32)
            total = part if total is None else total + part
        out[...] = total.astype(BF16)


def normed(x_ref, gain_ref):
    values = x_ref[...].astype(F32)
    return (values * inverse_rms(values) * gain_ref[...]).astype(BF16)


def pack_grad_body(own_ref, routes_ref, x_ref, *outs):
    pack(x_ref[...], own_ref, routes_ref, outs)


def pack_act_body(own_ref, routes_ref, gain_ref, x_ref, *outs):
    pack(normed(x_ref, gain_ref), own_ref, routes_ref, outs)


def first_body(own_ref, *refs):
    args, parts, joined = refs[:3], refs[3:6], refs[6]
    outs, held, stage, sems = refs[7:-5], refs[-5:-2], refs[-2], refs[-1]
    units = parts[0].shape[0]
    rows = [pl.ds(i * units, units) for i in range(3)]
    fetch = [pltpu.make_async_copy(arg, to, sems.at[i]) for i, (arg, to) in enumerate(zip(args, held))]
    load = [pltpu.make_async_copy(part, stage.at[rows[i], :], sems.at[3 + i]) for i, part in enumerate(parts)]
    store = [pltpu.make_async_copy(stage.at[rows[i], :], joined.at[rows[i], :], sems.at[6 + i]) for i in range(3)]
    for copy in fetch + load:
        copy.start()
    for copy in fetch:
        copy.wait()
    routes_ref, gain_ref, x_ref = held
    pack(normed(x_ref, gain_ref), own_ref, routes_ref, outs)
    for i in range(3):
        load[i].wait()
        store[i].start()
    for copy in store:
        copy.wait()


def unpack(refs, wide_ref, rows):
    pitch = wide_ref.shape[0] // len(refs)
    pieces = refs[0].shape[0] // rows
    for i, ref in enumerate(refs):
        value = ref[...].astype(F32)
        whole = jnp.concatenate([value[p * rows:(p + 1) * rows] for p in range(pieces)], axis=1)
        wide_ref[pl.ds(i * pitch, rows), :] = whole.astype(BF16)
    return wide_ref[...]


def spread_out(total, refs, pitch, rows):
    for i, ref in enumerate(refs):
        cols = ref.shape[1]
        whole = total[i * pitch:i * pitch + rows]
        pieces = [whole[:, p * cols:(p + 1) * cols] for p in range(ref.shape[0] // rows)]
        ref[...] = jnp.concatenate(pieces, axis=0).astype(ref.dtype)


def joined(shares, i):
    units = shares[i].shape[0]
    return jnp.concatenate([shares[i][...], shares[3][pl.ds(i * units, units), :]], axis=0)


def forward_body(count, rows, *refs):
    row_refs, shares, outs, wide_ref = refs[:count], refs[count:count + 4], refs[count + 4:-1], refs[-1]
    x = unpack(row_refs, wide_ref, rows)
    gate_pre = lax.dot_general(x, joined(shares, 0), CONTRACT, preferred_element_type=F32)
    up_pre = lax.dot_general(x, joined(shares, 1), CONTRACT, preferred_element_type=F32)
    hidden = (silu_parts(gate_pre)[0] * up_pre).astype(BF16)
    total = jnp.dot(hidden, joined(shares, 2), preferred_element_type=F32)
    spread_out(total, outs, x.shape[0] // count, rows)


def backward_body(count, rows, *refs):
    row_refs, grad_refs, shares = refs[:count], refs[count:2 * count], refs[2 * count:2 * count + 4]
    outs, wide_ref, grad_wide_ref = refs[2 * count + 4:-2], refs[-2], refs[-1]
    x = unpack(row_refs, wide_ref, rows)
    gate, up = joined(shares, 0), joined(shares, 1)
    gate_pre = lax.dot_general(x, gate, CONTRACT, preferred_element_type=F32)
    up_pre = lax.dot_general(x, up, CONTRACT, preferred_element_type=F32)
    activation, derivative = silu_parts(gate_pre)
    grads = unpack(grad_refs, grad_wide_ref, rows)
    d_hidden = lax.dot_general(grads, joined(shares, 2), CONTRACT, preferred_element_type=F32)
    d_gate = (d_hidden * up_pre * derivative).astype(BF16)
    d_up = (d_hidden * activation).astype(BF16)
    total = jnp.dot(d_gate, gate, preferred_element_type=F32) + jnp.dot(d_up, up, preferred_element_type=F32)
    spread_out(total, outs, x.shape[0] // count, rows)


def routed_sum(experts, rows, own_ref, routes_ref, gates_ref, home_refs):
    block, slot = slots_of(routes_ref[...], own_ref[0], experts)
    mine, theirs, *crossed_refs = home_refs
    blocks = [(mine[...] + theirs[...].astype(F32)).astype(BF16)] + [ref[...] for ref in crossed_refs]
    height = blocks[0].shape[0]
    columns = []
    for p in range(height // rows):
        total = None
        for j in range(experts):
            chooser = chooser_of(block, slot, j, p, rows, height)
            part = lax.dot_general(chooser, blocks[j], OVER_ROWS, preferred_element_type=F32)
            total = part if total is None else total + part
        columns.append(total)
    count = block.shape[1]
    diagonal = lax.broadcasted_iota(jnp.int32, (count, count), 0) == lax.broadcasted_iota(
        jnp.int32, (count, count), 1
    )
    gates = jnp.sum(jnp.where(diagonal, gates_ref[...], 0.0), axis=1, keepdims=True)
    return jnp.concatenate(columns, axis=1) * gates


def forward_home_body(experts, rows, own_ref, routes_ref, gates_ref, x_ref, *refs):
    mixed = routed_sum(experts, rows, own_ref, routes_ref, gates_ref, refs[:-1])
    refs[-1][...] = (x_ref[...].astype(F32) + mixed).astype(BF16)


def backward_home_body(experts, rows, own_ref, routes_ref, gates_ref, gain_ref, saved_ref, up_ref, *refs):
    d_norm = routed_sum(experts, rows, own_ref, routes_ref, gates_ref, refs[:-1])
    base = saved_ref[...].astype(F32)
    inv_scale = inverse_rms(base)
    scaled = d_norm * gain_ref[...]
    d_input = inv_scale * (
        scaled - base * inv_scale * inv_scale * jnp.mean(scaled * base, axis=-1, keepdims=True)
    )
    refs[-1][...] = (up_ref[...].astype(F32) + d_input).astype(BF16)


def crossed(blocks):
    return [blocks[0]] + [shifted(blocks[j], "expert", SPLIT * j) for j in range(1, len(blocks))]


def partners(blocks, *others):
    return [swapped(after(block, *others), "expert", 2) for block in blocks]


def crossing_home(partial):
    experts = len(partial) // 2
    mine, theirs = partial[:experts], partial[experts:]
    totals = [
        (mine[j] + swapped(theirs[j], "expert", 2).astype(F32)).astype(BF16) for j in range(1, experts)
    ]
    return totals, [shifted(totals[j - 1], "expert", -SPLIT * j) for j in range(1, experts)]


def per_device(act_in, saved_in, grad_in, norm_gain, w_gate, w_up, w_down, routes_fwd, gates_fwd, routes_bwd, gates_bwd):
    experts = lax.axis_size("expert") // SPLIT
    own = (lax.axis_index("expert") // SPLIT).astype(jnp.int32).reshape(1)
    tok_count, top_count = routes_fwd.shape[1:]
    assert top_count == 1
    width = act_in.shape[2]
    rows = min(tok_count, tok_count // experts + 2)
    pieces = 8 // math.gcd(rows, 8)
    pitch = -(-rows // 16) * 16
    scalar = pl.BlockSpec(memory_space=pltpu.SMEM)
    whole = pl.BlockSpec(memory_space=pltpu.VMEM)
    anywhere = pl.BlockSpec(memory_space=pl.ANY)

    shape = (pieces * rows, width // pieces)
    packed = [jax.ShapeDtypeStruct(shape, BF16)] * experts
    partial = [jax.ShapeDtypeStruct(shape, F32)] * experts + packed
    tokens = jax.ShapeDtypeStruct((tok_count, width), BF16)
    wide = pltpu.VMEM((2 * experts * pitch, width), BF16)

    incoming = shifted(act_in[0], "section", 1)
    upstream = shifted(grad_in[0], "section", -1)
    r_fwd = routes_fwd.reshape(1, tok_count)
    r_bwd = routes_bwd.reshape(1, tok_count)
    g_fwd = gates_fwd.reshape(1, tok_count)
    g_bwd = gates_bwd.reshape(1, tok_count)

    own_share, *packed_b = local_call(
        first_body,
        [jax.ShapeDtypeStruct((3 * w_down.shape[1], width), BF16)] + packed,
        in_specs=[scalar] + [anywhere] * 6,
        out_specs=[anywhere] + [whole] * experts,
        scratch=[
            pltpu.VMEM((1, tok_count), jnp.int32),
            pltpu.VMEM((1, width), F32),
            pltpu.VMEM((tok_count, width), BF16),
            pltpu.VMEM((3 * w_down.shape[1], width), BF16),
            pltpu.SemaphoreType.DMA((9,)),
        ],
        vmem_mib=56,
        name="join_weights_pack_saved",
    )(own, r_bwd, norm_gain, saved_in[0], w_gate[0].T, w_up[0].T, w_down[0])
    shares = (w_gate[0].T, w_up[0].T, w_down[0], swapped(own_share, "expert", 1))

    rows_b = crossed(packed_b)
    swap_b = partners(rows_b[:1])
    packed_g = local_call(
        pack_grad_body,
        packed,
        in_specs=[scalar] + [whole] * 2,
        out_specs=[whole] * experts,
        name="pack_grad",
    )(own, r_bwd, after(upstream, packed_b[0]))
    rows_g = crossed(packed_g)
    packed_f = local_call(
        pack_act_body,
        packed,
        in_specs=[scalar] + [whole] * 3,
        out_specs=[whole] * experts,
        name="pack_act",
    )(own, r_fwd, norm_gain, after(incoming, packed_g[0], rows_b[-1]))
    rows_f = crossed(packed_f)
    swap_g = partners(rows_g[:1], rows_b[-1])
    swap_f = partners(rows_f[:1], rows_g[-1])
    rows_b = rows_b + swap_b + partners(rows_b[1:], swap_b[0])
    rows_g = rows_g + swap_g + partners(rows_g[1:], swap_g[0])
    rows_f = rows_f + swap_f + partners(rows_f[1:], swap_f[0], rows_b[-1])

    count = 2 * experts
    partial_b = local_call(
        functools.partial(backward_body, count, rows), partial, scratch=[wide, wide], vmem_mib=40, name="experts_bwd"
    )(*rows_b, *rows_g, *shares)
    partial_f = local_call(
        functools.partial(forward_body, count, rows), partial, scratch=[wide], vmem_mib=32, name="experts_fwd"
    )(after(rows_f[0], partial_b[0]), *rows_f[1:], *shares)
    totals_b, home_b = crossing_home(partial_b)
    totals_f, home_f = crossing_home(partial_f)
    back_b = [partial_b[0]] + partners(partial_b[experts:experts + 1], *totals_b) + home_b
    back_f = [partial_f[0]] + partners(partial_f[experts:experts + 1], *totals_f, back_b[1]) + home_f

    grad_out = local_call(
        functools.partial(backward_home_body, experts, rows),
        tokens,
        in_specs=[scalar] + [whole] * (6 + experts),
        out_specs=whole,
        name="home_bwd",
    )(own, r_bwd, g_bwd, norm_gain, saved_in[0], upstream, *back_b)
    act_out = local_call(
        functools.partial(forward_home_body, experts, rows),
        tokens,
        in_specs=[scalar] + [whole] * (4 + experts),
        out_specs=whole,
        name="home_fwd",
    )(own, r_fwd, g_fwd, incoming, *back_f)
    return (act_out[None], grad_out[None])


def solution(mesh):
    tokens = P("section", "expert", None)
    in_specs = (
        tokens,
        tokens,
        tokens,
        P("section", None),
        P("section", None, "expert"),
        P("section", None, "expert"),
        tokens,
        tokens,
        tokens,
        tokens,
        tokens,
    )
    return jax.shard_map(
        per_device, mesh=mesh, in_specs=in_specs, out_specs=(tokens, tokens), check_vma=False
    )
```

```python
import functools
import math

import jax
import jax.numpy as jnp
from jax import lax
from jax.experimental import pallas as pl
from jax.experimental.pallas import tpu as pltpu
from jax.sharding import PartitionSpec as P

SPLIT = 4
EPS = 1e-06
CONTRACT = (((1,), (1,)), ((), ()))
OVER_ROWS = (((0,), (0,)), ((), ()))
F32 = jnp.float32
BF16 = jnp.bfloat16


def shifted(value, axis, steps):
    count = lax.axis_size(axis)
    return lax.ppermute(value, axis, [(i, (i + steps) % count) for i in range(count)])


def swapped(value, axis, bit):
    count = lax.axis_size(axis)
    return lax.ppermute(value, axis, [(i, i ^ bit) for i in range(count)])


def after(value, *others):
    return lax.optimization_barrier((value, *others))[0] if others else value


def local_call(body, out_shape, scratch=(), vmem_mib=16, **names):
    return pl.pallas_call(
        body,
        out_shape=out_shape,
        scratch_shapes=scratch,
        compiler_params=pltpu.CompilerParams(vmem_limit_bytes=vmem_mib << 20),
        cost_estimate=pl.CostEstimate(flops=1000, bytes_accessed=1000, transcendentals=0),
        **names,
    )


def silu_parts(values):
    sigma = jax.nn.sigmoid(values)
    return (values * sigma, sigma * (1.0 + values * (1.0 - sigma)))


def inverse_rms(values):
    return lax.rsqrt(jnp.mean(values * values, axis=-1, keepdims=True) + EPS)


def slots_of(routes, own, experts):
    count = routes.shape[1]
    height = -(-experts // 8) * 8
    ids = lax.broadcasted_iota(jnp.int32, (height, count), 0)
    onehot = (ids == routes).astype(F32)
    earlier = (
        lax.broadcasted_iota(jnp.int32, (count, count), 0) < lax.broadcasted_iota(jnp.int32, (count, count), 1)
    ).astype(F32)
    before = jnp.dot(onehot.astype(BF16), earlier.astype(BF16), preferred_element_type=F32)
    slot = jnp.sum(before * onehot, axis=0, keepdims=True).astype(jnp.int32)
    block = routes - own
    return (jnp.where(block < 0, block + experts, block), slot)


def chooser_of(block, slot, j, piece, rows, height):
    place = lax.broadcasted_iota(jnp.int32, (height, block.shape[1]), 0)
    return jnp.where((place == slot + piece * rows) & (block == j), 1.0, 0.0).astype(BF16)


def pack(values, own_ref, routes_ref, outs):
    experts = len(outs)
    height, cols = outs[0].shape
    pieces = values.shape[1] // cols
    rows = height // pieces
    block, slot = slots_of(routes_ref[...], own_ref[0], experts)
    for j, out in enumerate(outs):
        total = None
        for p in range(pieces):
            chooser = chooser_of(block, slot, j, p, rows, height)
            part = jnp.dot(chooser, values[:, p * cols:(p + 1) * cols], preferred_element_type=F32)
            total = part if total is None else total + part
        out[...] = total.astype(BF16)


def normed(x_ref, gain_ref):
    values = x_ref[...].astype(F32)
    return (values * inverse_rms(values) * gain_ref[...]).astype(BF16)


def pack_grad_body(own_ref, routes_ref, x_ref, *outs):
    pack(x_ref[...], own_ref, routes_ref, outs)


def pack_act_body(own_ref, routes_ref, gain_ref, x_ref, *outs):
    pack(normed(x_ref, gain_ref), own_ref, routes_ref, outs)


def first_body(own_ref, *refs):
    args, parts, joined = refs[:3], refs[3:6], refs[6]
    outs, held, stage, sems = refs[7:-5], refs[-5:-2], refs[-2], refs[-1]
    units = parts[0].shape[0]
    rows = [pl.ds(i * units, units) for i in range(3)]
    fetch = [pltpu.make_async_copy(arg, to, sems.at[i]) for i, (arg, to) in enumerate(zip(args, held))]
    load = [pltpu.make_async_copy(part, stage.at[rows[i], :], sems.at[3 + i]) for i, part in enumerate(parts)]
    store = [pltpu.make_async_copy(stage.at[rows[i], :], joined.at[rows[i], :], sems.at[6 + i]) for i in range(3)]
    for copy in fetch + load:
        copy.start()
    for copy in fetch:
        copy.wait()
    routes_ref, gain_ref, x_ref = held
    for i in range(3):
        load[i].wait()
        store[i].start()
    pack(normed(x_ref, gain_ref), own_ref, routes_ref, outs)
    for copy in store:
        copy.wait()


def unpack(refs, wide_ref, rows):
    pitch = wide_ref.shape[0] // len(refs)
    pieces = refs[0].shape[0] // rows
    for i, ref in enumerate(refs):
        value = ref[...].astype(F32)
        whole = jnp.concatenate([value[p * rows:(p + 1) * rows] for p in range(pieces)], axis=1)
        wide_ref[pl.ds(i * pitch, rows), :] = whole.astype(BF16)
    return wide_ref[...]


def spread_out(total, refs, pitch, rows):
    for i, ref in enumerate(refs):
        cols = ref.shape[1]
        whole = total[i * pitch:i * pitch + rows]
        pieces = [whole[:, p * cols:(p + 1) * cols] for p in range(ref.shape[0] // rows)]
        ref[...] = jnp.concatenate(pieces, axis=0).astype(ref.dtype)


def joined(shares, i):
    units = shares[i].shape[0]
    return jnp.concatenate([shares[i][...], shares[3][pl.ds(i * units, units), :]], axis=0)


def forward_body(count, rows, *refs):
    row_refs, shares, outs, wide_ref = refs[:count], refs[count:count + 4], refs[count + 4:-1], refs[-1]
    x = unpack(row_refs, wide_ref, rows)
    gate_pre = lax.dot_general(x, joined(shares, 0), CONTRACT, preferred_element_type=F32)
    up_pre = lax.dot_general(x, joined(shares, 1), CONTRACT, preferred_element_type=F32)
    hidden = (silu_parts(gate_pre)[0] * up_pre).astype(BF16)
    total = jnp.dot(hidden, joined(shares, 2), preferred_element_type=F32)
    spread_out(total, outs, x.shape[0] // count, rows)


def backward_body(count, rows, *refs):
    row_refs, grad_refs, shares = refs[:count], refs[count:2 * count], refs[2 * count:2 * count + 4]
    outs, wide_ref, grad_wide_ref = refs[2 * count + 4:-2], refs[-2], refs[-1]
    x = unpack(row_refs, wide_ref, rows)
    gate, up = joined(shares, 0), joined(shares, 1)
    gate_pre = lax.dot_general(x, gate, CONTRACT, preferred_element_type=F32)
    up_pre = lax.dot_general(x, up, CONTRACT, preferred_element_type=F32)
    activation, derivative = silu_parts(gate_pre)
    grads = unpack(grad_refs, grad_wide_ref, rows)
    d_hidden = lax.dot_general(grads, joined(shares, 2), CONTRACT, preferred_element_type=F32)
    d_gate = (d_hidden * up_pre * derivative).astype(BF16)
    d_up = (d_hidden * activation).astype(BF16)
    total = jnp.dot(d_gate, gate, preferred_element_type=F32) + jnp.dot(d_up, up, preferred_element_type=F32)
    spread_out(total, outs, x.shape[0] // count, rows)


def routed_sum(experts, rows, own_ref, routes_ref, gates_ref, home_refs):
    block, slot = slots_of(routes_ref[...], own_ref[0], experts)
    mine, theirs, *crossed_refs = home_refs
    blocks = [(mine[...] + theirs[...].astype(F32)).astype(BF16)] + [ref[...] for ref in crossed_refs]
    height = blocks[0].shape[0]
    columns = []
    for p in range(height // rows):
        total = None
        for j in range(experts):
            chooser = chooser_of(block, slot, j, p, rows, height)
            part = lax.dot_general(chooser, blocks[j], OVER_ROWS, preferred_element_type=F32)
            total = part if total is None else total + part
        columns.append(total)
    count = block.shape[1]
    diagonal = lax.broadcasted_iota(jnp.int32, (count, count), 0) == lax.broadcasted_iota(
        jnp.int32, (count, count), 1
    )
    gates = jnp.sum(jnp.where(diagonal, gates_ref[...], 0.0), axis=1, keepdims=True)
    return jnp.concatenate(columns, axis=1) * gates


def forward_home_body(experts, rows, own_ref, routes_ref, gates_ref, x_ref, *refs):
    mixed = routed_sum(experts, rows, own_ref, routes_ref, gates_ref, refs[:-1])
    refs[-1][...] = (x_ref[...].astype(F32) + mixed).astype(BF16)


def backward_home_body(experts, rows, own_ref, routes_ref, gates_ref, gain_ref, saved_ref, up_ref, *refs):
    d_norm = routed_sum(experts, rows, own_ref, routes_ref, gates_ref, refs[:-1])
    base = saved_ref[...].astype(F32)
    inv_scale = inverse_rms(base)
    scaled = d_norm * gain_ref[...]
    d_input = inv_scale * (
        scaled - base * inv_scale * inv_scale * jnp.mean(scaled * base, axis=-1, keepdims=True)
    )
    refs[-1][...] = (up_ref[...].astype(F32) + d_input).astype(BF16)


def crossed(blocks):
    return [blocks[0]] + [shifted(blocks[j], "expert", SPLIT * j) for j in range(1, len(blocks))]


def partners(blocks, *others):
    return [swapped(after(block, *others), "expert", 2) for block in blocks]


def totals_to_cross(partial, *others):
    experts = len(partial) // 2
    mine, theirs = partial[:experts], partial[experts:]
    swaps = partners(theirs[1:], *others)
    return [(mine[j] + swaps[j - 1].astype(F32)).astype(BF16) for j in range(1, experts)]


def crossed_home(totals, *others):
    return [shifted(after(total, *others), "expert", -SPLIT * (j + 1)) for j, total in enumerate(totals)]


def per_device(act_in, saved_in, grad_in, norm_gain, w_gate, w_up, w_down, routes_fwd, gates_fwd, routes_bwd, gates_bwd):
    experts = lax.axis_size("expert") // SPLIT
    own = (lax.axis_index("expert") // SPLIT).astype(jnp.int32).reshape(1)
    tok_count, top_count = routes_fwd.shape[1:]
    assert top_count == 1
    width = act_in.shape[2]
    rows = min(tok_count, tok_count // experts + 2)
    pieces = 8 // math.gcd(rows, 8)
    pitch = -(-rows // 16) * 16
    scalar = pl.BlockSpec(memory_space=pltpu.SMEM)
    whole = pl.BlockSpec(memory_space=pltpu.VMEM)
    anywhere = pl.BlockSpec(memory_space=pl.ANY)

    shape = (pieces * rows, width // pieces)
    packed = [jax.ShapeDtypeStruct(shape, BF16)] * experts
    partial = [jax.ShapeDtypeStruct(shape, F32)] * experts + packed
    tokens = jax.ShapeDtypeStruct((tok_count, width), BF16)
    wide = pltpu.VMEM((2 * experts * pitch, width), BF16)

    incoming = shifted(act_in[0], "section", 1)
    upstream = shifted(grad_in[0], "section", -1)
    r_fwd = routes_fwd.reshape(1, tok_count)
    r_bwd = routes_bwd.reshape(1, tok_count)
    g_fwd = gates_fwd.reshape(1, tok_count)
    g_bwd = gates_bwd.reshape(1, tok_count)

    own_share, *packed_b = local_call(
        first_body,
        [jax.ShapeDtypeStruct((3 * w_down.shape[1], width), BF16)] + packed,
        in_specs=[scalar] + [anywhere] * 6,
        out_specs=[anywhere] + [whole] * experts,
        scratch=[
            pltpu.VMEM((1, tok_count), jnp.int32),
            pltpu.VMEM((1, width), F32),
            pltpu.VMEM((tok_count, width), BF16),
            pltpu.VMEM((3 * w_down.shape[1], width), BF16),
            pltpu.SemaphoreType.DMA((9,)),
        ],
        vmem_mib=56,
        name="join_weights_pack_saved",
    )(own, r_bwd, norm_gain, saved_in[0], w_gate[0].T, w_up[0].T, w_down[0])
    shares = (w_gate[0].T, w_up[0].T, w_down[0], swapped(own_share, "expert", 1))

    rows_b = crossed(packed_b)
    swap_b = partners(rows_b[:1])
    packed_g = local_call(
        pack_grad_body,
        packed,
        in_specs=[scalar] + [whole] * 2,
        out_specs=[whole] * experts,
        name="pack_grad",
    )(own, r_bwd, after(upstream, packed_b[0]))
    rows_g = crossed(packed_g)
    packed_f = local_call(
        pack_act_body,
        packed,
        in_specs=[scalar] + [whole] * 3,
        out_specs=[whole] * experts,
        name="pack_act",
    )(own, r_fwd, norm_gain, after(incoming, packed_g[0], rows_b[-1]))
    rows_f = crossed(packed_f)
    swap_g = partners(rows_g[:1], rows_b[-1])
    swap_f = partners(rows_f[:1], rows_g[-1])
    rows_b = rows_b + swap_b + partners(rows_b[1:], swap_b[0])
    rows_g = rows_g + swap_g + partners(rows_g[1:], swap_g[0])
    rows_f = rows_f + swap_f + partners(rows_f[1:], swap_f[0], rows_b[-1])

    count = 2 * experts
    partial_b = local_call(
        functools.partial(backward_body, count, rows), partial, scratch=[wide, wide], vmem_mib=40, name="experts_bwd"
    )(*rows_b, *rows_g, *shares)
    partial_f = local_call(
        functools.partial(forward_body, count, rows), partial, scratch=[wide], vmem_mib=32, name="experts_fwd"
    )(after(rows_f[0], partial_b[0]), *rows_f[1:], *shares)
    totals_b = totals_to_cross(partial_b)
    home_b = crossed_home(totals_b)
    totals_f = totals_to_cross(partial_f, *totals_b)
    home_f = crossed_home(totals_f, *home_b)
    back_b = [partial_b[0]] + partners(partial_b[experts:experts + 1], *totals_f) + home_b
    back_f = [partial_f[0]] + partners(partial_f[experts:experts + 1], *totals_f, back_b[1]) + home_f

    grad_out = local_call(
        functools.partial(backward_home_body, experts, rows),
        tokens,
        in_specs=[scalar] + [whole] * (6 + experts),
        out_specs=whole,
        name="home_bwd",
    )(own, r_bwd, g_bwd, norm_gain, saved_in[0], upstream, *back_b)
    act_out = local_call(
        functools.partial(forward_home_body, experts, rows),
        tokens,
        in_specs=[scalar] + [whole] * (4 + experts),
        out_specs=whole,
        name="home_fwd",
    )(own, r_fwd, g_fwd, incoming, *back_f)
    return (act_out[None], grad_out[None])


def solution(mesh):
    tokens = P("section", "expert", None)
    in_specs = (
        tokens,
        tokens,
        tokens,
        P("section", None),
        P("section", None, "expert"),
        P("section", None, "expert"),
        tokens,
        tokens,
        tokens,
        tokens,
        tokens,
    )
    return jax.shard_map(
        per_device, mesh=mesh, in_specs=in_specs, out_specs=(tokens, tokens), check_vma=False
    )
```

```python
import functools
import math

import jax
import jax.numpy as jnp
from jax import lax
from jax.experimental import pallas as pl
from jax.experimental.pallas import tpu as pltpu
from jax.sharding import PartitionSpec as P

SPLIT = 4
EPS = 1e-06
CONTRACT = (((1,), (1,)), ((), ()))
OVER_ROWS = (((0,), (0,)), ((), ()))
F32 = jnp.float32
BF16 = jnp.bfloat16


def shifted(value, axis, steps):
    count = lax.axis_size(axis)
    return lax.ppermute(value, axis, [(i, (i + steps) % count) for i in range(count)])


def swapped(value, axis, bit):
    count = lax.axis_size(axis)
    return lax.ppermute(value, axis, [(i, i ^ bit) for i in range(count)])


def after(value, *others):
    return lax.optimization_barrier((value, *others))[0] if others else value


def local_call(body, out_shape, scratch=(), vmem_mib=16, **names):
    return pl.pallas_call(
        body,
        out_shape=out_shape,
        scratch_shapes=scratch,
        compiler_params=pltpu.CompilerParams(vmem_limit_bytes=vmem_mib << 20),
        cost_estimate=pl.CostEstimate(flops=1000, bytes_accessed=1000, transcendentals=0),
        **names,
    )


def silu_parts(values):
    sigma = jax.nn.sigmoid(values)
    return (values * sigma, sigma * (1.0 + values * (1.0 - sigma)))


def inverse_rms(values):
    return lax.rsqrt(jnp.mean(values * values, axis=-1, keepdims=True) + EPS)


def slots_of(routes, own, experts):
    count = routes.shape[1]
    height = -(-experts // 8) * 8
    ids = lax.broadcasted_iota(jnp.int32, (height, count), 0)
    onehot = (ids == routes).astype(F32)
    earlier = (
        lax.broadcasted_iota(jnp.int32, (count, count), 0) < lax.broadcasted_iota(jnp.int32, (count, count), 1)
    ).astype(F32)
    before = jnp.dot(onehot.astype(BF16), earlier.astype(BF16), preferred_element_type=F32)
    slot = jnp.sum(before * onehot, axis=0, keepdims=True).astype(jnp.int32)
    block = routes - own
    return (jnp.where(block < 0, block + experts, block), slot)


def chooser_of(block, slot, j, piece, rows, height):
    place = lax.broadcasted_iota(jnp.int32, (height, block.shape[1]), 0)
    return jnp.where((place == slot + piece * rows) & (block == j), 1.0, 0.0).astype(BF16)


def pack(values, own_ref, routes_ref, outs):
    experts = len(outs)
    height, cols = outs[0].shape
    pieces = values.shape[1] // cols
    rows = height // pieces
    block, slot = slots_of(routes_ref[...], own_ref[0], experts)
    for j, out in enumerate(outs):
        total = None
        for p in range(pieces):
            chooser = chooser_of(block, slot, j, p, rows, height)
            part = jnp.dot(chooser, values[:, p * cols:(p + 1) * cols], preferred_element_type=F32)
            total = part if total is None else total + part
        out[...] = total.astype(BF16)


def normed(x_ref, gain_ref):
    values = x_ref[...].astype(F32)
    return (values * inverse_rms(values) * gain_ref[...]).astype(BF16)


def pack_two_body(own_ref, routes_b_ref, routes_f_ref, gain_ref, grad_ref, x_ref, *outs):
    half = outs[0].shape[0] // 2
    pack(grad_ref[...], own_ref, routes_b_ref, [out.at[pl.ds(0, half), :] for out in outs])
    pack(normed(x_ref, gain_ref), own_ref, routes_f_ref, [out.at[pl.ds(half, half), :] for out in outs])


def first_body(own_ref, *refs):
    args, parts, joined = refs[:3], refs[3:6], refs[6]
    outs, held, stage, sems = refs[7:-5], refs[-5:-2], refs[-2], refs[-1]
    units = parts[0].shape[0]
    rows = [pl.ds(i * units, units) for i in range(3)]
    fetch = [pltpu.make_async_copy(arg, to, sems.at[i]) for i, (arg, to) in enumerate(zip(args, held))]
    load = [pltpu.make_async_copy(part, stage.at[rows[i], :], sems.at[3 + i]) for i, part in enumerate(parts)]
    store = [pltpu.make_async_copy(stage.at[rows[i], :], joined.at[rows[i], :], sems.at[6 + i]) for i in range(3)]
    for copy in fetch + load:
        copy.start()
    for copy in fetch:
        copy.wait()
    routes_ref, gain_ref, x_ref = held
    for i in range(3):
        load[i].wait()
        store[i].start()
    pack(normed(x_ref, gain_ref), own_ref, routes_ref, outs)
    for copy in store:
        copy.wait()


def unpack(blocks, wide_ref, first, pitch, rows):
    for i, block in enumerate(blocks):
        value = block.astype(F32)
        whole = jnp.concatenate([value[p * rows:(p + 1) * rows] for p in range(value.shape[0] // rows)], axis=1)
        wide_ref[pl.ds(first + i * pitch, rows), :] = whole.astype(BF16)


def pieces_of(total, i, pitch, rows, cols):
    whole = total[i * pitch:i * pitch + rows]
    return [whole[:, p:p + cols] for p in range(0, whole.shape[1], cols)]


def joined(shares, i):
    units = shares[i].shape[0]
    return jnp.concatenate([shares[i][...], shares[3][pl.ds(i * units, units), :]], axis=0)


def experts_body(count, rows, *refs):
    saved_refs, two_refs, shares = refs[:count], refs[count:2 * count], refs[2 * count:2 * count + 4]
    outs, x_ref, grads_ref = refs[2 * count + 4:-2], refs[-2], refs[-1]
    pitch = grads_ref.shape[0] // count
    half = two_refs[0].shape[0] // 2
    cols = two_refs[0].shape[1]
    split = count * pitch
    two = [ref[...] for ref in two_refs]
    unpack([ref[...] for ref in saved_refs], x_ref, 0, pitch, rows)
    unpack([value[half:] for value in two], x_ref, split, pitch, rows)
    unpack([value[:half] for value in two], grads_ref, 0, pitch, rows)
    gate, up, down = joined(shares, 0), joined(shares, 1), joined(shares, 2)
    x = x_ref[...]
    gate_pre = lax.dot_general(x, gate, CONTRACT, preferred_element_type=F32)
    up_pre = lax.dot_general(x, up, CONTRACT, preferred_element_type=F32)
    d_hidden = lax.dot_general(grads_ref[...], down, CONTRACT, preferred_element_type=F32)
    activation, derivative = silu_parts(gate_pre)
    d_gate = (d_hidden * up_pre[:split] * derivative[:split]).astype(BF16)
    d_up = (d_hidden * activation[:split]).astype(BF16)
    hidden = (activation[split:] * up_pre[split:]).astype(BF16)
    total_b = jnp.dot(d_gate, gate, preferred_element_type=F32) + jnp.dot(d_up, up, preferred_element_type=F32)
    total_f = jnp.dot(hidden, down, preferred_element_type=F32)
    for i, out in enumerate(outs):
        parts = pieces_of(total_b, i, pitch, rows, cols) + pieces_of(total_f, i, pitch, rows, cols)
        out[...] = jnp.concatenate(parts, axis=0).astype(out.dtype)


def routed_sum(experts, rows, own_ref, routes_ref, gates_ref, blocks):
    block, slot = slots_of(routes_ref[...], own_ref[0], experts)
    height = blocks[0].shape[0]
    columns = []
    for p in range(height // rows):
        total = None
        for j in range(experts):
            chooser = chooser_of(block, slot, j, p, rows, height)
            part = lax.dot_general(chooser, blocks[j], OVER_ROWS, preferred_element_type=F32)
            total = part if total is None else total + part
        columns.append(total)
    count = block.shape[1]
    diagonal = lax.broadcasted_iota(jnp.int32, (count, count), 0) == lax.broadcasted_iota(
        jnp.int32, (count, count), 1
    )
    gates = jnp.sum(jnp.where(diagonal, gates_ref[...], 0.0), axis=1, keepdims=True)
    return jnp.concatenate(columns, axis=1) * gates


def home_body(experts, rows, own_ref, routes_b, gates_b, routes_f, gates_f, gain_ref, saved_ref, up_ref, x_ref, *refs):
    mine, theirs, *crossed_refs = refs[:-2]
    act_out, grad_out = refs[-2:]
    half = mine.shape[0] // 2
    blocks = [(mine[...] + theirs[...].astype(F32)).astype(BF16)] + [ref[...] for ref in crossed_refs]
    mixed = routed_sum(experts, rows, own_ref, routes_f, gates_f, [value[half:] for value in blocks])
    act_out[...] = (x_ref[...].astype(F32) + mixed).astype(BF16)
    d_norm = routed_sum(experts, rows, own_ref, routes_b, gates_b, [value[:half] for value in blocks])
    base = saved_ref[...].astype(F32)
    inv_scale = inverse_rms(base)
    scaled = d_norm * gain_ref[...]
    d_input = inv_scale * (
        scaled - base * inv_scale * inv_scale * jnp.mean(scaled * base, axis=-1, keepdims=True)
    )
    grad_out[...] = (up_ref[...].astype(F32) + d_input).astype(BF16)


def crossed(blocks):
    return [blocks[0]] + [shifted(blocks[j], "expert", SPLIT * j) for j in range(1, len(blocks))]


def partners(blocks, *others):
    return [swapped(after(block, *others), "expert", 2) for block in blocks]


def per_device(act_in, saved_in, grad_in, norm_gain, w_gate, w_up, w_down, routes_fwd, gates_fwd, routes_bwd, gates_bwd):
    experts = lax.axis_size("expert") // SPLIT
    own = (lax.axis_index("expert") // SPLIT).astype(jnp.int32).reshape(1)
    tok_count, top_count = routes_fwd.shape[1:]
    assert top_count == 1
    width = act_in.shape[2]
    rows = min(tok_count, tok_count // experts + 2)
    pieces = 8 // math.gcd(rows, 8)
    pitch = -(-rows // 16) * 16
    scalar = pl.BlockSpec(memory_space=pltpu.SMEM)
    whole = pl.BlockSpec(memory_space=pltpu.VMEM)
    anywhere = pl.BlockSpec(memory_space=pl.ANY)

    shape = (pieces * rows, width // pieces)
    packed = [jax.ShapeDtypeStruct(shape, BF16)] * experts
    double = (2 * shape[0], shape[1])
    tokens = jax.ShapeDtypeStruct((tok_count, width), BF16)

    incoming = shifted(act_in[0], "section", 1)
    upstream = shifted(grad_in[0], "section", -1)
    r_fwd = routes_fwd.reshape(1, tok_count)
    r_bwd = routes_bwd.reshape(1, tok_count)
    g_fwd = gates_fwd.reshape(1, tok_count)
    g_bwd = gates_bwd.reshape(1, tok_count)

    own_share, *packed_b = local_call(
        first_body,
        [jax.ShapeDtypeStruct((3 * w_down.shape[1], width), BF16)] + packed,
        in_specs=[scalar] + [anywhere] * 6,
        out_specs=[anywhere] + [whole] * experts,
        scratch=[
            pltpu.VMEM((1, tok_count), jnp.int32),
            pltpu.VMEM((1, width), F32),
            pltpu.VMEM((tok_count, width), BF16),
            pltpu.VMEM((3 * w_down.shape[1], width), BF16),
            pltpu.SemaphoreType.DMA((9,)),
        ],
        vmem_mib=56,
        name="join_weights_pack_saved",
    )(own, r_bwd, norm_gain, saved_in[0], w_gate[0].T, w_up[0].T, w_down[0])
    shares = (w_gate[0].T, w_up[0].T, w_down[0], swapped(own_share, "expert", 1))

    rows_b = crossed(packed_b)
    swap_b = partners(rows_b[:1])
    packed_two = local_call(
        pack_two_body,
        [jax.ShapeDtypeStruct(double, BF16)] * experts,
        in_specs=[scalar] + [whole] * 5,
        out_specs=[whole] * experts,
        name="pack_grad_and_act",
    )(own, r_bwd, r_fwd, norm_gain, after(upstream, packed_b[0]), incoming)
    rows_two = crossed(packed_two)
    swap_two = partners(rows_two[:1], rows_b[-1])
    far_b = partners(rows_b[1:], swap_b[0], packed_two[0])
    far_two = partners(rows_two[1:], *far_b)

    def run_experts(name, rows_saved, rows_double, kinds):
        count = len(rows_saved)
        return local_call(
            functools.partial(experts_body, count, rows),
            [jax.ShapeDtypeStruct(double, kind) for kind in kinds],
            in_specs=[whole] * (2 * count + 4),
            out_specs=[whole] * count,
            scratch=[pltpu.VMEM((2 * count * pitch, width), BF16), pltpu.VMEM((count * pitch, width), BF16)],
            vmem_mib=32,
            name=name,
        )(*rows_saved, *rows_double, *shares)

    near = run_experts("experts_near", rows_b + swap_b, rows_two + swap_two, [F32] * experts + [BF16])
    far = run_experts("experts_far", far_b, [after(far_two[0], near[0])] + far_two[1:], [BF16] * (experts - 1))
    totals = [(near[j] + part.astype(F32)).astype(BF16) for j, part in enumerate(partners(far), 1)]
    home = [shifted(total, "expert", -SPLIT * j) for j, total in enumerate(totals, 1)]
    theirs = partners(near[experts:], *totals)

    act_out, grad_out = local_call(
        functools.partial(home_body, experts, rows),
        [tokens, tokens],
        in_specs=[scalar] + [whole] * (9 + experts),
        out_specs=[whole] * 2,
        name="home",
    )(own, r_bwd, g_bwd, r_fwd, g_fwd, norm_gain, saved_in[0], upstream, incoming, near[0], theirs[0], *home)
    return (act_out[None], grad_out[None])


def solution(mesh):
    tokens = P("section", "expert", None)
    in_specs = (
        tokens,
        tokens,
        tokens,
        P("section", None),
        P("section", None, "expert"),
        P("section", None, "expert"),
        tokens,
        tokens,
        tokens,
        tokens,
        tokens,
    )
    return jax.shard_map(
        per_device, mesh=mesh, in_specs=in_specs, out_specs=(tokens, tokens), check_vma=False
    )
```

```python
import functools
import math

import jax
import jax.numpy as jnp
from jax import lax
from jax.experimental import pallas as pl
from jax.experimental.pallas import tpu as pltpu
from jax.sharding import PartitionSpec as P

SPLIT = 4
EPS = 1e-06
CONTRACT = (((1,), (1,)), ((), ()))
OVER_ROWS = (((0,), (0,)), ((), ()))
F32 = jnp.float32
BF16 = jnp.bfloat16


def shifted(value, axis, steps):
    count = lax.axis_size(axis)
    return lax.ppermute(value, axis, [(i, (i + steps) % count) for i in range(count)])


def swapped(value, axis, bit):
    count = lax.axis_size(axis)
    return lax.ppermute(value, axis, [(i, i ^ bit) for i in range(count)])


def after(value, *others):
    return lax.optimization_barrier((value, *others))[0] if others else value


def local_call(body, out_shape, scratch=(), vmem_mib=16, **names):
    return pl.pallas_call(
        body,
        out_shape=out_shape,
        scratch_shapes=scratch,
        compiler_params=pltpu.CompilerParams(vmem_limit_bytes=vmem_mib << 20),
        cost_estimate=pl.CostEstimate(flops=1000, bytes_accessed=1000, transcendentals=0),
        **names,
    )


def silu_parts(values):
    sigma = jax.nn.sigmoid(values)
    return (values * sigma, sigma * (1.0 + values * (1.0 - sigma)))


def inverse_rms(values):
    return lax.rsqrt(jnp.mean(values * values, axis=-1, keepdims=True) + EPS)


def slots_of(routes, own, experts):
    count = routes.shape[1]
    height = -(-experts // 8) * 8
    ids = lax.broadcasted_iota(jnp.int32, (height, count), 0)
    onehot = (ids == routes).astype(F32)
    earlier = (
        lax.broadcasted_iota(jnp.int32, (count, count), 0) < lax.broadcasted_iota(jnp.int32, (count, count), 1)
    ).astype(F32)
    before = jnp.dot(onehot.astype(BF16), earlier.astype(BF16), preferred_element_type=F32)
    slot = jnp.sum(before * onehot, axis=0, keepdims=True).astype(jnp.int32)
    block = routes - own
    return (jnp.where(block < 0, block + experts, block), slot)


def chooser_of(block, slot, j, piece, rows, height):
    place = lax.broadcasted_iota(jnp.int32, (height, block.shape[1]), 0)
    return jnp.where((place == slot + piece * rows) & (block == j), 1.0, 0.0).astype(BF16)


def pack(values, own_ref, routes_ref, outs):
    experts = len(outs)
    height, cols = outs[0].shape
    pieces = values.shape[1] // cols
    rows = height // pieces
    block, slot = slots_of(routes_ref[...], own_ref[0], experts)
    for j, out in enumerate(outs):
        total = None
        for p in range(pieces):
            chooser = chooser_of(block, slot, j, p, rows, height)
            part = jnp.dot(chooser, values[:, p * cols:(p + 1) * cols], preferred_element_type=F32)
            total = part if total is None else total + part
        out[...] = total.astype(BF16)


def normed(x_ref, gain_ref):
    values = x_ref[...].astype(F32)
    return (values * inverse_rms(values) * gain_ref[...]).astype(BF16)


def pack_grad_body(own_ref, routes_ref, x_ref, *outs):
    pack(x_ref[...], own_ref, routes_ref, outs)


def pack_act_body(own_ref, routes_ref, gain_ref, x_ref, kept_ref, *outs):
    pack(normed(x_ref, gain_ref), own_ref, routes_ref, outs[:-1])
    outs[-1][...] = kept_ref[...]


def first_body(own_ref, *refs):
    args, parts, joined = refs[:3], refs[3:6], refs[6]
    outs, held, stage, sems = refs[7:-5], refs[-5:-2], refs[-2], refs[-1]
    units = parts[0].shape[0]
    rows = [pl.ds(i * units, units) for i in range(3)]
    fetch = [pltpu.make_async_copy(arg, to, sems.at[i]) for i, (arg, to) in enumerate(zip(args, held))]
    load = [pltpu.make_async_copy(part, stage.at[rows[i], :], sems.at[3 + i]) for i, part in enumerate(parts)]
    store = [pltpu.make_async_copy(stage.at[rows[i], :], joined.at[rows[i], :], sems.at[6 + i]) for i in range(3)]
    for copy in fetch + load:
        copy.start()
    for copy in fetch:
        copy.wait()
    routes_ref, gain_ref, x_ref = held
    for i in range(3):
        load[i].wait()
        store[i].start()
    pack(normed(x_ref, gain_ref), own_ref, routes_ref, outs)
    for copy in store:
        copy.wait()


def unpack(refs, wide_ref, rows):
    pitch = wide_ref.shape[0] // len(refs)
    pieces = refs[0].shape[0] // rows
    for i, ref in enumerate(refs):
        value = ref[...].astype(F32)
        whole = jnp.concatenate([value[p * rows:(p + 1) * rows] for p in range(pieces)], axis=1)
        wide_ref[pl.ds(i * pitch, rows), :] = whole.astype(BF16)
    return wide_ref[...]


def spread_out(total, refs, pitch, rows):
    for i, ref in enumerate(refs):
        cols = ref.shape[1]
        whole = total[i * pitch:i * pitch + rows]
        pieces = [whole[:, p * cols:(p + 1) * cols] for p in range(ref.shape[0] // rows)]
        ref[...] = jnp.concatenate(pieces, axis=0).astype(ref.dtype)


def joined(shares, i):
    units = shares[i].shape[0]
    return jnp.concatenate([shares[i][...], shares[3][pl.ds(i * units, units), :]], axis=0)


def forward_body(count, rows, *refs):
    row_refs, shares, outs, wide_ref = refs[:count], refs[count:count + 4], refs[count + 4:-1], refs[-1]
    x = unpack(row_refs, wide_ref, rows)
    gate_pre = lax.dot_general(x, joined(shares, 0), CONTRACT, preferred_element_type=F32)
    up_pre = lax.dot_general(x, joined(shares, 1), CONTRACT, preferred_element_type=F32)
    hidden = (silu_parts(gate_pre)[0] * up_pre).astype(BF16)
    total = jnp.dot(hidden, joined(shares, 2), preferred_element_type=F32)
    spread_out(total, outs, x.shape[0] // count, rows)


def backward_body(count, rows, *refs):
    row_refs, grad_refs, shares = refs[:count], refs[count:2 * count], refs[2 * count:2 * count + 4]
    outs, wide_ref, grad_wide_ref = refs[2 * count + 4:-2], refs[-2], refs[-1]
    x = unpack(row_refs, wide_ref, rows)
    gate, up = joined(shares, 0), joined(shares, 1)
    gate_pre = lax.dot_general(x, gate, CONTRACT, preferred_element_type=F32)
    up_pre = lax.dot_general(x, up, CONTRACT, preferred_element_type=F32)
    activation, derivative = silu_parts(gate_pre)
    grads = unpack(grad_refs, grad_wide_ref, rows)
    d_hidden = lax.dot_general(grads, joined(shares, 2), CONTRACT, preferred_element_type=F32)
    d_gate = (d_hidden * up_pre * derivative).astype(BF16)
    d_up = (d_hidden * activation).astype(BF16)
    total = jnp.dot(d_gate, gate, preferred_element_type=F32) + jnp.dot(d_up, up, preferred_element_type=F32)
    spread_out(total, outs, x.shape[0] // count, rows)


def routed_sum(experts, rows, own_ref, routes_ref, gates_ref, home_refs):
    block, slot = slots_of(routes_ref[...], own_ref[0], experts)
    mine, theirs, *crossed_refs = home_refs
    blocks = [(mine[...] + theirs[...].astype(F32)).astype(BF16)] + [ref[...] for ref in crossed_refs]
    height = blocks[0].shape[0]
    columns = []
    for p in range(height // rows):
        total = None
        for j in range(experts):
            chooser = chooser_of(block, slot, j, p, rows, height)
            part = lax.dot_general(chooser, blocks[j], OVER_ROWS, preferred_element_type=F32)
            total = part if total is None else total + part
        columns.append(total)
    count = block.shape[1]
    diagonal = lax.broadcasted_iota(jnp.int32, (count, count), 0) == lax.broadcasted_iota(
        jnp.int32, (count, count), 1
    )
    gates = jnp.sum(jnp.where(diagonal, gates_ref[...], 0.0), axis=1, keepdims=True)
    return jnp.concatenate(columns, axis=1) * gates


def forward_home_body(experts, rows, own_ref, routes_ref, gates_ref, x_ref, *refs):
    mixed = routed_sum(experts, rows, own_ref, routes_ref, gates_ref, refs[:-1])
    refs[-1][...] = (x_ref[...].astype(F32) + mixed).astype(BF16)


def backward_home_body(experts, rows, own_ref, routes_ref, gates_ref, gain_ref, saved_ref, up_ref, *refs):
    d_norm = routed_sum(experts, rows, own_ref, routes_ref, gates_ref, refs[:-1])
    base = saved_ref[...].astype(F32)
    inv_scale = inverse_rms(base)
    scaled = d_norm * gain_ref[...]
    d_input = inv_scale * (
        scaled - base * inv_scale * inv_scale * jnp.mean(scaled * base, axis=-1, keepdims=True)
    )
    refs[-1][...] = (up_ref[...].astype(F32) + d_input).astype(BF16)


def crossed(blocks):
    return [blocks[0]] + [shifted(blocks[j], "expert", SPLIT * j) for j in range(1, len(blocks))]


def partners(blocks, *others):
    return [swapped(after(block, *others), "expert", 2) for block in blocks]


def crossing_home(partial):
    experts = len(partial) // 2
    mine, theirs = partial[:experts], partial[experts:]
    totals = [
        (mine[j] + swapped(theirs[j], "expert", 2).astype(F32)).astype(BF16) for j in range(1, experts)
    ]
    return totals, [shifted(totals[j - 1], "expert", -SPLIT * j) for j in range(1, experts)]


def per_device(act_in, saved_in, grad_in, norm_gain, w_gate, w_up, w_down, routes_fwd, gates_fwd, routes_bwd, gates_bwd):
    experts = lax.axis_size("expert") // SPLIT
    own = (lax.axis_index("expert") // SPLIT).astype(jnp.int32).reshape(1)
    tok_count, top_count = routes_fwd.shape[1:]
    assert top_count == 1
    width = act_in.shape[2]
    rows = min(tok_count, tok_count // experts + 2)
    pieces = 8 // math.gcd(rows, 8)
    pitch = -(-rows // 16) * 16
    scalar = pl.BlockSpec(memory_space=pltpu.SMEM)
    whole = pl.BlockSpec(memory_space=pltpu.VMEM)
    anywhere = pl.BlockSpec(memory_space=pl.ANY)

    shape = (pieces * rows, width // pieces)
    packed = [jax.ShapeDtypeStruct(shape, BF16)] * experts
    partial = [jax.ShapeDtypeStruct(shape, F32)] * experts + packed
    tokens = jax.ShapeDtypeStruct((tok_count, width), BF16)
    wide = pltpu.VMEM((2 * experts * pitch, width), BF16)

    incoming = shifted(act_in[0], "section", 1)
    upstream = shifted(grad_in[0], "section", -1)
    r_fwd = routes_fwd.reshape(1, tok_count)
    r_bwd = routes_bwd.reshape(1, tok_count)
    g_fwd = gates_fwd.reshape(1, tok_count)
    g_bwd = gates_bwd.reshape(1, tok_count)

    own_share, *packed_b = local_call(
        first_body,
        [jax.ShapeDtypeStruct((3 * w_down.shape[1], width), BF16)] + packed,
        in_specs=[scalar] + [anywhere] * 6,
        out_specs=[anywhere] + [whole] * experts,
        scratch=[
            pltpu.VMEM((1, tok_count), jnp.int32),
            pltpu.VMEM((1, width), F32),
            pltpu.VMEM((tok_count, width), BF16),
            pltpu.VMEM((3 * w_down.shape[1], width), BF16),
            pltpu.SemaphoreType.DMA((9,)),
        ],
        vmem_mib=56,
        name="join_weights_pack_saved",
    )(own, r_bwd, norm_gain, saved_in[0], w_gate[0].T, w_up[0].T, w_down[0])
    shares = (w_gate[0].T, w_up[0].T, w_down[0], swapped(own_share, "expert", 1))

    rows_b = crossed(packed_b)
    swap_b = partners(rows_b[:1])
    packed_g = local_call(
        pack_grad_body,
        packed,
        in_specs=[scalar] + [whole] * 2,
        out_specs=[whole] * experts,
        name="pack_grad",
    )(own, r_bwd, after(upstream, packed_b[0]))
    rows_g = crossed(packed_g)
    *packed_f, kept_b = local_call(
        pack_act_body,
        packed + packed[:1],
        in_specs=[scalar] + [whole] * 4,
        out_specs=[whole] * (experts + 1),
        name="pack_act",
    )(own, r_fwd, norm_gain, after(incoming, packed_g[0], rows_b[-1]), packed_b[0])
    rows_f = crossed(packed_f)
    swap_g = partners(rows_g[:1], rows_b[-1])
    rows_b = [kept_b] + rows_b[1:] + swap_b + partners(rows_b[1:], swap_b[0])
    rows_g = rows_g + swap_g + partners(rows_g[1:])
    rows_f = rows_f + partners(rows_f, rows_g[-1], rows_b[-1])

    count = 2 * experts
    partial_b = local_call(
        functools.partial(backward_body, count, rows), partial, scratch=[wide, wide], vmem_mib=40, name="experts_bwd"
    )(*rows_b, *rows_g, *shares)
    partial_f = local_call(
        functools.partial(forward_body, count, rows), partial, scratch=[wide], vmem_mib=32, name="experts_fwd"
    )(after(rows_f[0], partial_b[0]), *rows_f[1:], *shares)
    totals_b, home_b = crossing_home(partial_b)
    totals_f, home_f = crossing_home(partial_f)
    back_b = [partial_b[0]] + partners(partial_b[experts:experts + 1], *totals_b) + home_b
    back_f = [partial_f[0]] + partners(partial_f[experts:experts + 1], *totals_f, back_b[1]) + home_f

    grad_out = local_call(
        functools.partial(backward_home_body, experts, rows),
        tokens,
        in_specs=[scalar] + [whole] * (6 + experts),
        out_specs=whole,
        name="home_bwd",
    )(own, r_bwd, g_bwd, norm_gain, saved_in[0], upstream, *back_b)
    act_out = local_call(
        functools.partial(forward_home_body, experts, rows),
        tokens,
        in_specs=[scalar] + [whole] * (4 + experts),
        out_specs=whole,
        name="home_fwd",
    )(own, r_fwd, g_fwd, incoming, *back_f)
    return (act_out[None], grad_out[None])


def solution(mesh):
    tokens = P("section", "expert", None)
    in_specs = (
        tokens,
        tokens,
        tokens,
        P("section", None),
        P("section", None, "expert"),
        P("section", None, "expert"),
        tokens,
        tokens,
        tokens,
        tokens,
        tokens,
    )
    return jax.shard_map(
        per_device, mesh=mesh, in_specs=in_specs, out_specs=(tokens, tokens), check_vma=False
    )
```

```python
import functools
import math

import jax
import jax.numpy as jnp
from jax import lax
from jax.experimental import pallas as pl
from jax.experimental.pallas import tpu as pltpu
from jax.sharding import PartitionSpec as P

SPLIT = 4
EPS = 1e-06
CONTRACT = (((1,), (1,)), ((), ()))
OVER_ROWS = (((0,), (0,)), ((), ()))
F32 = jnp.float32
BF16 = jnp.bfloat16


def shifted(value, axis, steps):
    count = lax.axis_size(axis)
    return lax.ppermute(value, axis, [(i, (i + steps) % count) for i in range(count)])


def swapped(value, axis, bit):
    count = lax.axis_size(axis)
    return lax.ppermute(value, axis, [(i, i ^ bit) for i in range(count)])


def after(value, *others):
    return lax.optimization_barrier((value, *others))[0] if others else value


def local_call(body, out_shape, scratch=(), vmem_mib=16, **names):
    return pl.pallas_call(
        body,
        out_shape=out_shape,
        scratch_shapes=scratch,
        compiler_params=pltpu.CompilerParams(vmem_limit_bytes=vmem_mib << 20),
        cost_estimate=pl.CostEstimate(flops=1000, bytes_accessed=1000, transcendentals=0),
        **names,
    )


def silu_parts(values):
    sigma = jax.nn.sigmoid(values)
    return (values * sigma, sigma * (1.0 + values * (1.0 - sigma)))


def inverse_rms(values):
    return lax.rsqrt(jnp.mean(values * values, axis=-1, keepdims=True) + EPS)


def slots_of(routes, own, experts):
    count = routes.shape[1]
    height = -(-experts // 8) * 8
    ids = lax.broadcasted_iota(jnp.int32, (height, count), 0)
    onehot = (ids == routes).astype(F32)
    earlier = (
        lax.broadcasted_iota(jnp.int32, (count, count), 0) < lax.broadcasted_iota(jnp.int32, (count, count), 1)
    ).astype(F32)
    before = jnp.dot(onehot.astype(BF16), earlier.astype(BF16), preferred_element_type=F32)
    slot = jnp.sum(before * onehot, axis=0, keepdims=True).astype(jnp.int32)
    block = routes - own
    return (jnp.where(block < 0, block + experts, block), slot)


def chooser_of(block, slot, j, piece, rows, height):
    place = lax.broadcasted_iota(jnp.int32, (height, block.shape[1]), 0)
    return jnp.where((place == slot + piece * rows) & (block == j), 1.0, 0.0).astype(BF16)


def pack(values, own_ref, routes_ref, outs):
    experts = len(outs)
    height, cols = outs[0].shape
    pieces = values.shape[1] // cols
    rows = height // pieces
    block, slot = slots_of(routes_ref[...], own_ref[0], experts)
    for j, out in enumerate(outs):
        total = None
        for p in range(pieces):
            chooser = chooser_of(block, slot, j, p, rows, height)
            part = jnp.dot(chooser, values[:, p * cols:(p + 1) * cols], preferred_element_type=F32)
            total = part if total is None else total + part
        out[...] = total.astype(BF16)


def normed(x_ref, gain_ref):
    values = x_ref[...].astype(F32)
    return (values * inverse_rms(values) * gain_ref[...]).astype(BF16)


def pack_grad_body(own_ref, routes_ref, x_ref, *outs):
    pack(x_ref[...], own_ref, routes_ref, outs)


def pack_act_body(own_ref, routes_ref, gain_ref, x_ref, kept_ref, *outs):
    pack(normed(x_ref, gain_ref), own_ref, routes_ref, outs[:-1])
    outs[-1][...] = kept_ref[...]


def first_body(own_ref, *refs):
    args, parts, joined = refs[:3], refs[3:6], refs[6]
    outs, held, stage, sems = refs[7:-5], refs[-5:-2], refs[-2], refs[-1]
    units = parts[0].shape[0]
    rows = [pl.ds(i * units, units) for i in range(3)]
    fetch = [pltpu.make_async_copy(arg, to, sems.at[i]) for i, (arg, to) in enumerate(zip(args, held))]
    load = [pltpu.make_async_copy(part, stage.at[rows[i], :], sems.at[3 + i]) for i, part in enumerate(parts)]
    store = [pltpu.make_async_copy(stage.at[rows[i], :], joined.at[rows[i], :], sems.at[6 + i]) for i in range(3)]
    for copy in fetch + load:
        copy.start()
    for copy in fetch:
        copy.wait()
    routes_ref, gain_ref, x_ref = held
    for i in range(3):
        load[i].wait()
        store[i].start()
    pack(normed(x_ref, gain_ref), own_ref, routes_ref, outs)
    for copy in store:
        copy.wait()


def unpack(refs, wide_ref, rows):
    pitch = wide_ref.shape[0] // len(refs)
    pieces = refs[0].shape[0] // rows
    for i, ref in enumerate(refs):
        value = ref[...].astype(F32)
        whole = jnp.concatenate([value[p * rows:(p + 1) * rows] for p in range(pieces)], axis=1)
        wide_ref[pl.ds(i * pitch, rows), :] = whole.astype(BF16)
    return wide_ref[...]


def spread_out(total, refs, pitch, rows):
    for i, ref in enumerate(refs):
        cols = ref.shape[1]
        whole = total[i * pitch:i * pitch + rows]
        pieces = [whole[:, p * cols:(p + 1) * cols] for p in range(ref.shape[0] // rows)]
        ref[...] = jnp.concatenate(pieces, axis=0).astype(ref.dtype)


def joined(shares, i):
    units = shares[i].shape[0]
    return jnp.concatenate([shares[i][...], shares[3][pl.ds(i * units, units), :]], axis=0)


def forward_body(count, rows, *refs):
    row_refs, shares, outs, wide_ref = refs[:count], refs[count:count + 4], refs[count + 4:-1], refs[-1]
    x = unpack(row_refs, wide_ref, rows)
    gate_pre = lax.dot_general(x, joined(shares, 0), CONTRACT, preferred_element_type=F32)
    up_pre = lax.dot_general(x, joined(shares, 1), CONTRACT, preferred_element_type=F32)
    hidden = (silu_parts(gate_pre)[0] * up_pre).astype(BF16)
    total = jnp.dot(hidden, joined(shares, 2), preferred_element_type=F32)
    spread_out(total, outs, x.shape[0] // count, rows)


def backward_body(count, rows, *refs):
    row_refs, grad_refs, shares = refs[:count], refs[count:2 * count], refs[2 * count:2 * count + 4]
    outs, wide_ref, grad_wide_ref = refs[2 * count + 4:-2], refs[-2], refs[-1]
    x = unpack(row_refs, wide_ref, rows)
    gate, up = joined(shares, 0), joined(shares, 1)
    gate_pre = lax.dot_general(x, gate, CONTRACT, preferred_element_type=F32)
    up_pre = lax.dot_general(x, up, CONTRACT, preferred_element_type=F32)
    activation, derivative = silu_parts(gate_pre)
    grads = unpack(grad_refs, grad_wide_ref, rows)
    d_hidden = lax.dot_general(grads, joined(shares, 2), CONTRACT, preferred_element_type=F32)
    d_gate = (d_hidden * up_pre * derivative).astype(BF16)
    d_up = (d_hidden * activation).astype(BF16)
    total = jnp.dot(d_gate, gate, preferred_element_type=F32) + jnp.dot(d_up, up, preferred_element_type=F32)
    spread_out(total, outs, x.shape[0] // count, rows)


def routed_sum(experts, rows, own_ref, routes_ref, gates_ref, home_refs):
    block, slot = slots_of(routes_ref[...], own_ref[0], experts)
    mine, theirs, *crossed_refs = home_refs
    blocks = [(mine[...] + theirs[...].astype(F32)).astype(BF16)] + [ref[...] for ref in crossed_refs]
    height = blocks[0].shape[0]
    columns = []
    for p in range(height // rows):
        total = None
        for j in range(experts):
            chooser = chooser_of(block, slot, j, p, rows, height)
            part = lax.dot_general(chooser, blocks[j], OVER_ROWS, preferred_element_type=F32)
            total = part if total is None else total + part
        columns.append(total)
    count = block.shape[1]
    diagonal = lax.broadcasted_iota(jnp.int32, (count, count), 0) == lax.broadcasted_iota(
        jnp.int32, (count, count), 1
    )
    gates = jnp.sum(jnp.where(diagonal, gates_ref[...], 0.0), axis=1, keepdims=True)
    return jnp.concatenate(columns, axis=1) * gates


def forward_home_body(experts, rows, own_ref, routes_ref, gates_ref, x_ref, *refs):
    mixed = routed_sum(experts, rows, own_ref, routes_ref, gates_ref, refs[:-1])
    refs[-1][...] = (x_ref[...].astype(F32) + mixed).astype(BF16)


def backward_home_body(experts, rows, own_ref, routes_ref, gates_ref, gain_ref, saved_ref, up_ref, *refs):
    d_norm = routed_sum(experts, rows, own_ref, routes_ref, gates_ref, refs[:-1])
    base = saved_ref[...].astype(F32)
    inv_scale = inverse_rms(base)
    scaled = d_norm * gain_ref[...]
    d_input = inv_scale * (
        scaled - base * inv_scale * inv_scale * jnp.mean(scaled * base, axis=-1, keepdims=True)
    )
    refs[-1][...] = (up_ref[...].astype(F32) + d_input).astype(BF16)


def crossed(blocks):
    return [blocks[0]] + [shifted(blocks[j], "expert", SPLIT * j) for j in range(1, len(blocks))]


def partners(blocks, *others):
    return [swapped(after(block, *others), "expert", 2) for block in blocks]


def crossing_home(partial):
    experts = len(partial) // 2
    mine, theirs = partial[:experts], partial[experts:]
    totals = [
        (mine[j] + swapped(theirs[j], "expert", 2).astype(F32)).astype(BF16) for j in range(1, experts)
    ]
    return totals, [shifted(totals[j - 1], "expert", -SPLIT * j) for j in range(1, experts)]


def per_device(act_in, saved_in, grad_in, norm_gain, w_gate, w_up, w_down, routes_fwd, gates_fwd, routes_bwd, gates_bwd):
    experts = lax.axis_size("expert") // SPLIT
    own = (lax.axis_index("expert") // SPLIT).astype(jnp.int32).reshape(1)
    tok_count, top_count = routes_fwd.shape[1:]
    assert top_count == 1
    width = act_in.shape[2]
    rows = min(tok_count, tok_count // experts + 2)
    pieces = 8 // math.gcd(rows, 8)
    pitch = -(-rows // 16) * 16
    scalar = pl.BlockSpec(memory_space=pltpu.SMEM)
    whole = pl.BlockSpec(memory_space=pltpu.VMEM)
    anywhere = pl.BlockSpec(memory_space=pl.ANY)

    shape = (pieces * rows, width // pieces)
    packed = [jax.ShapeDtypeStruct(shape, BF16)] * experts
    partial = [jax.ShapeDtypeStruct(shape, F32)] * experts + packed
    tokens = jax.ShapeDtypeStruct((tok_count, width), BF16)
    wide = pltpu.VMEM((2 * experts * pitch, width), BF16)

    incoming = shifted(act_in[0], "section", 1)
    upstream = shifted(grad_in[0], "section", -1)
    r_fwd = routes_fwd.reshape(1, tok_count)
    r_bwd = routes_bwd.reshape(1, tok_count)
    g_fwd = gates_fwd.reshape(1, tok_count)
    g_bwd = gates_bwd.reshape(1, tok_count)

    own_share, *packed_b = local_call(
        first_body,
        [jax.ShapeDtypeStruct((3 * w_down.shape[1], width), BF16)] + packed,
        in_specs=[scalar] + [anywhere] * 6,
        out_specs=[anywhere] + [whole] * experts,
        scratch=[
            pltpu.VMEM((1, tok_count), jnp.int32),
            pltpu.VMEM((1, width), F32),
            pltpu.VMEM((tok_count, width), BF16),
            pltpu.VMEM((3 * w_down.shape[1], width), BF16),
            pltpu.SemaphoreType.DMA((9,)),
        ],
        vmem_mib=56,
        name="join_weights_pack_saved",
    )(own, r_bwd, norm_gain, saved_in[0], w_gate[0].T, w_up[0].T, w_down[0])
    shares = (w_gate[0].T, w_up[0].T, w_down[0], swapped(own_share, "expert", 1))

    rows_b = crossed(packed_b)
    swap_b = partners(rows_b[:1])
    packed_g = local_call(
        pack_grad_body,
        packed,
        in_specs=[scalar] + [whole] * 2,
        out_specs=[whole] * experts,
        name="pack_grad",
    )(own, r_bwd, after(upstream, packed_b[0]))
    rows_g = crossed(packed_g)
    *packed_f, kept_b = local_call(
        pack_act_body,
        packed + packed[:1],
        in_specs=[scalar] + [whole] * 4,
        out_specs=[whole] * (experts + 1),
        name="pack_act",
    )(own, r_fwd, norm_gain, after(incoming, packed_g[0], rows_b[-1]), packed_b[0])
    rows_f = crossed(packed_f)
    swap_g = partners(rows_g[:1], rows_b[-1])
    swap_f = partners(rows_f[:1], rows_g[-1])
    rows_b = [kept_b] + rows_b[1:] + swap_b + partners(rows_b[1:], swap_b[0])
    rows_g = rows_g + swap_g + partners(rows_g[1:], swap_g[0])
    rows_f = rows_f + swap_f + partners(rows_f[1:], swap_f[0], rows_b[-1])

    count = 2 * experts
    partial_b = local_call(
        functools.partial(backward_body, count, rows), partial, scratch=[wide, wide], vmem_mib=40, name="experts_bwd"
    )(*rows_b, *rows_g, *shares)
    partial_f = local_call(
        functools.partial(forward_body, count, rows), partial, scratch=[wide], vmem_mib=32, name="experts_fwd"
    )(after(rows_f[0], partial_b[0]), *rows_f[1:], *shares)
    totals_b, home_b = crossing_home(partial_b)
    totals_f, home_f = crossing_home(partial_f)
    back_b = [partial_b[0]] + partners(partial_b[experts:experts + 1], *totals_b) + home_b
    back_f = [partial_f[0]] + partners(partial_f[experts:experts + 1], *totals_f, back_b[1]) + home_f

    grad_out = local_call(
        functools.partial(backward_home_body, experts, rows),
        tokens,
        in_specs=[scalar] + [whole] * (6 + experts),
        out_specs=whole,
        name="home_bwd",
    )(own, r_bwd, g_bwd, norm_gain, saved_in[0], upstream, *back_b)
    act_out = local_call(
        functools.partial(forward_home_body, experts, rows),
        tokens,
        in_specs=[scalar] + [whole] * (4 + experts),
        out_specs=whole,
        name="home_fwd",
    )(own, r_fwd, g_fwd, incoming, *back_f)
    return (act_out[None], grad_out[None])


def solution(mesh):
    tokens = P("section", "expert", None)
    in_specs = (
        tokens,
        tokens,
        tokens,
        P("section", None),
        P("section", None, "expert"),
        P("section", None, "expert"),
        tokens,
        tokens,
        tokens,
        tokens,
        tokens,
    )
    return jax.shard_map(
        per_device, mesh=mesh, in_specs=in_specs, out_specs=(tokens, tokens), check_vma=False
    )
```

```python
import functools
import math

import jax
import jax.numpy as jnp
from jax import lax
from jax.experimental import pallas as pl
from jax.experimental.pallas import tpu as pltpu
from jax.sharding import PartitionSpec as P

SPLIT = 4
EPS = 1e-06
CONTRACT = (((1,), (1,)), ((), ()))
OVER_ROWS = (((0,), (0,)), ((), ()))
F32 = jnp.float32
BF16 = jnp.bfloat16


def shifted(value, axis, steps):
    count = lax.axis_size(axis)
    return lax.ppermute(value, axis, [(i, (i + steps) % count) for i in range(count)])


def swapped(value, axis, bit):
    count = lax.axis_size(axis)
    return lax.ppermute(value, axis, [(i, i ^ bit) for i in range(count)])


def after(value, *others):
    return lax.optimization_barrier((value, *others))[0] if others else value


def local_call(body, out_shape, scratch=(), vmem_mib=16, **names):
    return pl.pallas_call(
        body,
        out_shape=out_shape,
        scratch_shapes=scratch,
        compiler_params=pltpu.CompilerParams(vmem_limit_bytes=vmem_mib << 20),
        cost_estimate=pl.CostEstimate(flops=1000, bytes_accessed=1000, transcendentals=0),
        **names,
    )


def silu_parts(values):
    sigma = jax.nn.sigmoid(values)
    return (values * sigma, sigma * (1.0 + values * (1.0 - sigma)))


def inverse_rms(values):
    return lax.rsqrt(jnp.mean(values * values, axis=-1, keepdims=True) + EPS)


def slots_of(routes, own, experts):
    count = routes.shape[1]
    height = -(-experts // 8) * 8
    ids = lax.broadcasted_iota(jnp.int32, (height, count), 0)
    onehot = (ids == routes).astype(F32)
    earlier = (
        lax.broadcasted_iota(jnp.int32, (count, count), 0) < lax.broadcasted_iota(jnp.int32, (count, count), 1)
    ).astype(F32)
    before = jnp.dot(onehot.astype(BF16), earlier.astype(BF16), preferred_element_type=F32)
    slot = jnp.sum(before * onehot, axis=0, keepdims=True).astype(jnp.int32)
    block = routes - own
    return (jnp.where(block < 0, block + experts, block), slot)


def chooser_of(block, slot, j, piece, rows, height):
    place = lax.broadcasted_iota(jnp.int32, (height, block.shape[1]), 0)
    return jnp.where((place == slot + piece * rows) & (block == j), 1.0, 0.0).astype(BF16)


def pack(values, own_ref, routes_ref, outs):
    experts = len(outs)
    height, cols = outs[0].shape
    pieces = values.shape[1] // cols
    rows = height // pieces
    block, slot = slots_of(routes_ref[...], own_ref[0], experts)
    for j, out in enumerate(outs):
        total = None
        for p in range(pieces):
            chooser = chooser_of(block, slot, j, p, rows, height)
            part = jnp.dot(chooser, values[:, p * cols:(p + 1) * cols], preferred_element_type=F32)
            total = part if total is None else total + part
        out[...] = total.astype(BF16)


def normed(x_ref, gain_ref):
    values = x_ref[...].astype(F32)
    return (values * inverse_rms(values) * gain_ref[...]).astype(BF16)


def pack_grad_body(own_ref, routes_ref, x_ref, *outs):
    pack(x_ref[...], own_ref, routes_ref, outs)


def pack_act_body(own_ref, routes_ref, gain_ref, x_ref, kept_ref, *outs):
    pack(normed(x_ref, gain_ref), own_ref, routes_ref, outs[:-1])
    outs[-1][...] = kept_ref[...]


def first_body(own_ref, *refs):
    args, parts, joined = refs[:3], refs[3:6], refs[6]
    outs, held, stage, sems = refs[7:-5], refs[-5:-2], refs[-2], refs[-1]
    units = parts[0].shape[0]
    rows = [pl.ds(i * units, units) for i in range(3)]
    fetch = [pltpu.make_async_copy(arg, to, sems.at[i]) for i, (arg, to) in enumerate(zip(args, held))]
    load = [pltpu.make_async_copy(part, stage.at[rows[i], :], sems.at[3 + i]) for i, part in enumerate(parts)]
    store = [pltpu.make_async_copy(stage.at[rows[i], :], joined.at[rows[i], :], sems.at[6 + i]) for i in range(3)]
    for copy in fetch + load:
        copy.start()
    for copy in fetch:
        copy.wait()
    routes_ref, gain_ref, x_ref = held
    for i in range(3):
        load[i].wait()
        store[i].start()
    pack(normed(x_ref, gain_ref), own_ref, routes_ref, outs)
    for copy in store:
        copy.wait()


def unpack(refs, wide_ref, rows):
    pitch = wide_ref.shape[0] // len(refs)
    pieces = refs[0].shape[0] // rows
    for i, ref in enumerate(refs):
        value = ref[...].astype(F32)
        whole = jnp.concatenate([value[p * rows:(p + 1) * rows] for p in range(pieces)], axis=1)
        wide_ref[pl.ds(i * pitch, rows), :] = whole.astype(BF16)
    return wide_ref[...]


def spread_out(total, refs, pitch, rows):
    for i, ref in enumerate(refs):
        cols = ref.shape[1]
        whole = total[i * pitch:i * pitch + rows]
        pieces = [whole[:, p * cols:(p + 1) * cols] for p in range(ref.shape[0] // rows)]
        ref[...] = jnp.concatenate(pieces, axis=0).astype(ref.dtype)


def joined(shares, i):
    units = shares[i].shape[0]
    return jnp.concatenate([shares[i][...], shares[3][pl.ds(i * units, units), :]], axis=0)


def forward_body(count, rows, *refs):
    row_refs, shares, outs, wide_ref = refs[:count], refs[count:count + 4], refs[count + 4:-1], refs[-1]
    x = unpack(row_refs, wide_ref, rows)
    gate_pre = lax.dot_general(x, joined(shares, 0), CONTRACT, preferred_element_type=F32)
    up_pre = lax.dot_general(x, joined(shares, 1), CONTRACT, preferred_element_type=F32)
    hidden = (silu_parts(gate_pre)[0] * up_pre).astype(BF16)
    total = jnp.dot(hidden, joined(shares, 2), preferred_element_type=F32)
    spread_out(total, outs, x.shape[0] // count, rows)


def backward_body(count, rows, *refs):
    row_refs, grad_refs, shares = refs[:count], refs[count:2 * count], refs[2 * count:2 * count + 4]
    outs, wide_ref, grad_wide_ref = refs[2 * count + 4:-2], refs[-2], refs[-1]
    x = unpack(row_refs, wide_ref, rows)
    gate, up = joined(shares, 0), joined(shares, 1)
    gate_pre = lax.dot_general(x, gate, CONTRACT, preferred_element_type=F32)
    up_pre = lax.dot_general(x, up, CONTRACT, preferred_element_type=F32)
    activation, derivative = silu_parts(gate_pre)
    grads = unpack(grad_refs, grad_wide_ref, rows)
    d_hidden = lax.dot_general(grads, joined(shares, 2), CONTRACT, preferred_element_type=F32)
    d_gate = (d_hidden * up_pre * derivative).astype(BF16)
    d_up = (d_hidden * activation).astype(BF16)
    total = jnp.dot(d_gate, gate, preferred_element_type=F32) + jnp.dot(d_up, up, preferred_element_type=F32)
    spread_out(total, outs, x.shape[0] // count, rows)


def routed_sum(experts, rows, own_ref, routes_ref, gates_ref, home_refs):
    block, slot = slots_of(routes_ref[...], own_ref[0], experts)
    mine, theirs, *crossed_refs = home_refs
    blocks = [(mine[...] + theirs[...].astype(F32)).astype(BF16)] + [ref[...] for ref in crossed_refs]
    height = blocks[0].shape[0]
    columns = []
    for p in range(height // rows):
        total = None
        for j in range(experts):
            chooser = chooser_of(block, slot, j, p, rows, height)
            part = lax.dot_general(chooser, blocks[j], OVER_ROWS, preferred_element_type=F32)
            total = part if total is None else total + part
        columns.append(total)
    count = block.shape[1]
    diagonal = lax.broadcasted_iota(jnp.int32, (count, count), 0) == lax.broadcasted_iota(
        jnp.int32, (count, count), 1
    )
    gates = jnp.sum(jnp.where(diagonal, gates_ref[...], 0.0), axis=1, keepdims=True)
    return jnp.concatenate(columns, axis=1) * gates


def forward_home_body(experts, rows, own_ref, routes_ref, gates_ref, x_ref, *refs):
    mixed = routed_sum(experts, rows, own_ref, routes_ref, gates_ref, refs[:-1])
    refs[-1][...] = (x_ref[...].astype(F32) + mixed).astype(BF16)


def backward_home_body(experts, rows, own_ref, routes_ref, gates_ref, gain_ref, saved_ref, up_ref, *refs):
    d_norm = routed_sum(experts, rows, own_ref, routes_ref, gates_ref, refs[:-1])
    base = saved_ref[...].astype(F32)
    inv_scale = inverse_rms(base)
    scaled = d_norm * gain_ref[...]
    d_input = inv_scale * (
        scaled - base * inv_scale * inv_scale * jnp.mean(scaled * base, axis=-1, keepdims=True)
    )
    refs[-1][...] = (up_ref[...].astype(F32) + d_input).astype(BF16)


def crossed(blocks):
    return [blocks[0]] + [shifted(blocks[j], "expert", SPLIT * j) for j in range(1, len(blocks))]


def partners(blocks, *others):
    return [swapped(after(block, *others), "expert", 2) for block in blocks]


def crossing_home(partial):
    experts = len(partial) // 2
    mine, theirs = partial[:experts], partial[experts:]
    totals = [
        (mine[j] + swapped(theirs[j], "expert", 2).astype(F32)).astype(BF16) for j in range(1, experts)
    ]
    return totals, [shifted(totals[j - 1], "expert", -SPLIT * j) for j in range(1, experts)]


def per_device(act_in, saved_in, grad_in, norm_gain, w_gate, w_up, w_down, routes_fwd, gates_fwd, routes_bwd, gates_bwd):
    experts = lax.axis_size("expert") // SPLIT
    own = (lax.axis_index("expert") // SPLIT).astype(jnp.int32).reshape(1)
    tok_count, top_count = routes_fwd.shape[1:]
    assert top_count == 1
    width = act_in.shape[2]
    rows = min(tok_count, tok_count // experts + 2)
    pieces = 8 // math.gcd(rows, 8)
    pitch = -(-rows // 16) * 16
    scalar = pl.BlockSpec(memory_space=pltpu.SMEM)
    whole = pl.BlockSpec(memory_space=pltpu.VMEM)
    anywhere = pl.BlockSpec(memory_space=pl.ANY)

    shape = (pieces * rows, width // pieces)
    packed = [jax.ShapeDtypeStruct(shape, BF16)] * experts
    partial = [jax.ShapeDtypeStruct(shape, F32)] * experts + packed
    tokens = jax.ShapeDtypeStruct((tok_count, width), BF16)
    wide = pltpu.VMEM((2 * experts * pitch, width), BF16)

    incoming = shifted(act_in[0], "section", 1)
    upstream = shifted(grad_in[0], "section", -1)
    r_fwd = routes_fwd.reshape(1, tok_count)
    r_bwd = routes_bwd.reshape(1, tok_count)
    g_fwd = gates_fwd.reshape(1, tok_count)
    g_bwd = gates_bwd.reshape(1, tok_count)

    own_share, *packed_b = local_call(
        first_body,
        [jax.ShapeDtypeStruct((3 * w_down.shape[1], width), BF16)] + packed,
        in_specs=[scalar] + [anywhere] * 6,
        out_specs=[anywhere] + [whole] * experts,
        scratch=[
            pltpu.VMEM((1, tok_count), jnp.int32),
            pltpu.VMEM((1, width), F32),
            pltpu.VMEM((tok_count, width), BF16),
            pltpu.VMEM((3 * w_down.shape[1], width), BF16),
            pltpu.SemaphoreType.DMA((9,)),
        ],
        vmem_mib=56,
        name="join_weights_pack_saved",
    )(own, r_bwd, norm_gain, saved_in[0], w_gate[0].T, w_up[0].T, w_down[0])
    shares = (w_gate[0].T, w_up[0].T, w_down[0], swapped(own_share, "expert", 1))

    rows_b = crossed(packed_b)
    swap_b = partners(rows_b[:1])
    packed_g = local_call(
        pack_grad_body,
        packed,
        in_specs=[scalar] + [whole] * 2,
        out_specs=[whole] * experts,
        name="pack_grad",
    )(own, r_bwd, after(upstream, packed_b[0]))
    rows_g = crossed(packed_g)
    *packed_f, kept_b = local_call(
        pack_act_body,
        packed + packed[:1],
        in_specs=[scalar] + [whole] * 4,
        out_specs=[whole] * (experts + 1),
        name="pack_act",
    )(own, r_fwd, norm_gain, after(incoming, packed_g[0], rows_b[-1]), packed_b[0])
    rows_f = crossed(packed_f)
    swap_g = partners(rows_g[:1], rows_b[-1])
    swap_f = partners(rows_f[:1], rows_g[-1])
    rows_b = [kept_b] + rows_b[1:] + swap_b + partners(rows_b[1:], swap_b[0])
    rows_g = rows_g + swap_g + partners(rows_g[1:], swap_g[0])
    rows_f = rows_f + swap_f + partners(rows_f[1:], swap_f[0], rows_b[-1])

    count = 2 * experts
    partial_b = local_call(
        functools.partial(backward_body, count, rows), partial, scratch=[wide, wide], vmem_mib=40, name="experts_bwd"
    )(*rows_b, *rows_g, *shares)
    partial_f = local_call(
        functools.partial(forward_body, count, rows), partial, scratch=[wide], vmem_mib=32, name="experts_fwd"
    )(after(rows_f[0], partial_b[0]), *rows_f[1:], *shares)
    totals_b, home_b = crossing_home(partial_b)
    totals_f, home_f = crossing_home(partial_f)
    back_b = [partial_b[0]] + partners(partial_b[experts:experts + 1], *totals_b) + home_b
    back_f = [partial_f[0]] + partners(partial_f[experts:experts + 1], *totals_f, *home_b) + home_f

    grad_out = local_call(
        functools.partial(backward_home_body, experts, rows),
        tokens,
        in_specs=[scalar] + [whole] * (6 + experts),
        out_specs=whole,
        name="home_bwd",
    )(own, r_bwd, g_bwd, norm_gain, saved_in[0], upstream, *back_b)
    act_out = local_call(
        functools.partial(forward_home_body, experts, rows),
        tokens,
        in_specs=[scalar] + [whole] * (4 + experts),
        out_specs=whole,
        name="home_fwd",
    )(own, r_fwd, g_fwd, incoming, *back_f)
    return (act_out[None], grad_out[None])


def solution(mesh):
    tokens = P("section", "expert", None)
    in_specs = (
        tokens,
        tokens,
        tokens,
        P("section", None),
        P("section", None, "expert"),
        P("section", None, "expert"),
        tokens,
        tokens,
        tokens,
        tokens,
        tokens,
    )
    return jax.shard_map(
        per_device, mesh=mesh, in_specs=in_specs, out_specs=(tokens, tokens), check_vma=False
    )
```

```python
import functools
import math

import jax
import jax.numpy as jnp
from jax import lax
from jax.experimental import pallas as pl
from jax.experimental.pallas import tpu as pltpu
from jax.sharding import PartitionSpec as P

SPLIT = 4
EPS = 1e-06
CONTRACT = (((1,), (1,)), ((), ()))
OVER_ROWS = (((0,), (0,)), ((), ()))
F32 = jnp.float32
BF16 = jnp.bfloat16


def shifted(value, axis, steps):
    count = lax.axis_size(axis)
    return lax.ppermute(value, axis, [(i, (i + steps) % count) for i in range(count)])


def swapped(value, axis, bit):
    count = lax.axis_size(axis)
    return lax.ppermute(value, axis, [(i, i ^ bit) for i in range(count)])


def after(value, *others):
    return lax.optimization_barrier((value, *others))[0] if others else value


def local_call(body, out_shape, scratch=(), vmem_mib=16, **names):
    return pl.pallas_call(
        body,
        out_shape=out_shape,
        scratch_shapes=scratch,
        compiler_params=pltpu.CompilerParams(vmem_limit_bytes=vmem_mib << 20),
        cost_estimate=pl.CostEstimate(flops=1000, bytes_accessed=1000, transcendentals=0),
        **names,
    )


def silu_parts(values):
    sigma = jax.nn.sigmoid(values)
    return (values * sigma, sigma * (1.0 + values * (1.0 - sigma)))


def inverse_rms(values):
    return lax.rsqrt(jnp.mean(values * values, axis=-1, keepdims=True) + EPS)


def slots_of(routes, own, experts):
    count = routes.shape[1]
    height = -(-experts // 8) * 8
    ids = lax.broadcasted_iota(jnp.int32, (height, count), 0)
    onehot = (ids == routes).astype(F32)
    earlier = (
        lax.broadcasted_iota(jnp.int32, (count, count), 0) < lax.broadcasted_iota(jnp.int32, (count, count), 1)
    ).astype(F32)
    before = jnp.dot(onehot.astype(BF16), earlier.astype(BF16), preferred_element_type=F32)
    slot = jnp.sum(before * onehot, axis=0, keepdims=True).astype(jnp.int32)
    block = routes - own
    return (jnp.where(block < 0, block + experts, block), slot)


def chooser_of(block, slot, j, piece, rows, height):
    place = lax.broadcasted_iota(jnp.int32, (height, block.shape[1]), 0)
    return jnp.where((place == slot + piece * rows) & (block == j), 1.0, 0.0).astype(BF16)


def pack(values, own_ref, routes_ref, outs):
    experts = len(outs)
    height, cols = outs[0].shape
    pieces = values.shape[1] // cols
    rows = height // pieces
    block, slot = slots_of(routes_ref[...], own_ref[0], experts)
    for j, out in enumerate(outs):
        total = None
        for p in range(pieces):
            chooser = chooser_of(block, slot, j, p, rows, height)
            part = jnp.dot(chooser, values[:, p * cols:(p + 1) * cols], preferred_element_type=F32)
            total = part if total is None else total + part
        out[...] = total.astype(BF16)


def normed(x_ref, gain_ref):
    values = x_ref[...].astype(F32)
    return (values * inverse_rms(values) * gain_ref[...]).astype(BF16)


def pack_grad_body(own_ref, routes_ref, x_ref, *outs):
    pack(x_ref[...], own_ref, routes_ref, outs)


def pack_act_body(own_ref, routes_ref, gain_ref, x_ref, kept_ref, *outs):
    pack(normed(x_ref, gain_ref), own_ref, routes_ref, outs[:-1])
    outs[-1][...] = kept_ref[...]


def first_body(own_ref, *refs):
    args, parts, joined = refs[:3], refs[3:6], refs[6]
    outs, held, stage, sems = refs[7:-5], refs[-5:-2], refs[-2], refs[-1]
    units = parts[0].shape[0]
    rows = [pl.ds(i * units, units) for i in range(3)]
    fetch = [pltpu.make_async_copy(arg, to, sems.at[i]) for i, (arg, to) in enumerate(zip(args, held))]
    load = [pltpu.make_async_copy(part, stage.at[rows[i], :], sems.at[3 + i]) for i, part in enumerate(parts)]
    store = [pltpu.make_async_copy(stage.at[rows[i], :], joined.at[rows[i], :], sems.at[6 + i]) for i in range(3)]
    for copy in fetch + load:
        copy.start()
    for copy in fetch:
        copy.wait()
    routes_ref, gain_ref, x_ref = held
    for i in range(3):
        load[i].wait()
        store[i].start()
    pack(normed(x_ref, gain_ref), own_ref, routes_ref, outs)
    for copy in store:
        copy.wait()


def unpack(refs, wide_ref, rows):
    pitch = wide_ref.shape[0] // len(refs)
    pieces = refs[0].shape[0] // rows
    for i, ref in enumerate(refs):
        value = ref[...].astype(F32)
        whole = jnp.concatenate([value[p * rows:(p + 1) * rows] for p in range(pieces)], axis=1)
        wide_ref[pl.ds(i * pitch, rows), :] = whole.astype(BF16)
    return wide_ref[...]


def spread_out(total, refs, pitch, rows):
    for i, ref in enumerate(refs):
        cols = ref.shape[1]
        whole = total[i * pitch:i * pitch + rows]
        pieces = [whole[:, p * cols:(p + 1) * cols] for p in range(ref.shape[0] // rows)]
        ref[...] = jnp.concatenate(pieces, axis=0).astype(ref.dtype)


def joined(shares, i):
    units = shares[i].shape[0]
    return jnp.concatenate([shares[i][...], shares[3][pl.ds(i * units, units), :]], axis=0)


def forward_body(count, rows, *refs):
    row_refs, shares, outs, wide_ref = refs[:count], refs[count:count + 4], refs[count + 4:-1], refs[-1]
    x = unpack(row_refs, wide_ref, rows)
    gate_pre = lax.dot_general(x, joined(shares, 0), CONTRACT, preferred_element_type=F32)
    up_pre = lax.dot_general(x, joined(shares, 1), CONTRACT, preferred_element_type=F32)
    hidden = (silu_parts(gate_pre)[0] * up_pre).astype(BF16)
    total = jnp.dot(hidden, joined(shares, 2), preferred_element_type=F32)
    spread_out(total, outs, x.shape[0] // count, rows)


def backward_body(count, rows, *refs):
    row_refs, grad_refs, shares = refs[:count], refs[count:2 * count], refs[2 * count:2 * count + 4]
    outs, wide_ref, grad_wide_ref = refs[2 * count + 4:-2], refs[-2], refs[-1]
    x = unpack(row_refs, wide_ref, rows)
    gate, up = joined(shares, 0), joined(shares, 1)
    gate_pre = lax.dot_general(x, gate, CONTRACT, preferred_element_type=F32)
    up_pre = lax.dot_general(x, up, CONTRACT, preferred_element_type=F32)
    activation, derivative = silu_parts(gate_pre)
    grads = unpack(grad_refs, grad_wide_ref, rows)
    d_hidden = lax.dot_general(grads, joined(shares, 2), CONTRACT, preferred_element_type=F32)
    d_gate = (d_hidden * up_pre * derivative).astype(BF16)
    d_up = (d_hidden * activation).astype(BF16)
    total = jnp.dot(d_gate, gate, preferred_element_type=F32) + jnp.dot(d_up, up, preferred_element_type=F32)
    spread_out(total, outs, x.shape[0] // count, rows)


def routed_sum(experts, rows, own_ref, routes_ref, gates_ref, home_refs):
    block, slot = slots_of(routes_ref[...], own_ref[0], experts)
    mine, theirs, *crossed_refs = home_refs
    blocks = [(mine[...] + theirs[...].astype(F32)).astype(BF16)] + [ref[...] for ref in crossed_refs]
    height = blocks[0].shape[0]
    columns = []
    for p in range(height // rows):
        total = None
        for j in range(experts):
            chooser = chooser_of(block, slot, j, p, rows, height)
            part = lax.dot_general(chooser, blocks[j], OVER_ROWS, preferred_element_type=F32)
            total = part if total is None else total + part
        columns.append(total)
    count = block.shape[1]
    diagonal = lax.broadcasted_iota(jnp.int32, (count, count), 0) == lax.broadcasted_iota(
        jnp.int32, (count, count), 1
    )
    gates = jnp.sum(jnp.where(diagonal, gates_ref[...], 0.0), axis=1, keepdims=True)
    return jnp.concatenate(columns, axis=1) * gates


def forward_home_body(experts, rows, own_ref, routes_ref, gates_ref, x_ref, *refs):
    mixed = routed_sum(experts, rows, own_ref, routes_ref, gates_ref, refs[:-1])
    refs[-1][...] = (x_ref[...].astype(F32) + mixed).astype(BF16)


def backward_home_body(experts, rows, own_ref, routes_ref, gates_ref, gain_ref, saved_ref, up_ref, *refs):
    d_norm = routed_sum(experts, rows, own_ref, routes_ref, gates_ref, refs[:-1])
    base = saved_ref[...].astype(F32)
    inv_scale = inverse_rms(base)
    scaled = d_norm * gain_ref[...]
    d_input = inv_scale * (
        scaled - base * inv_scale * inv_scale * jnp.mean(scaled * base, axis=-1, keepdims=True)
    )
    refs[-1][...] = (up_ref[...].astype(F32) + d_input).astype(BF16)


def crossed(blocks):
    return [blocks[0]] + [shifted(blocks[j], "expert", SPLIT * j) for j in range(1, len(blocks))]


def partners(blocks, *others):
    return [swapped(after(block, *others), "expert", 2) for block in blocks]


def crossing_home(partial):
    experts = len(partial) // 2
    mine, theirs = partial[:experts], partial[experts:]
    totals = [
        (mine[j] + swapped(theirs[j], "expert", 2).astype(F32)).astype(BF16) for j in range(1, experts)
    ]
    return totals, [shifted(totals[j - 1], "expert", -SPLIT * j) for j in range(1, experts)]


def per_device(act_in, saved_in, grad_in, norm_gain, w_gate, w_up, w_down, routes_fwd, gates_fwd, routes_bwd, gates_bwd):
    experts = lax.axis_size("expert") // SPLIT
    own = (lax.axis_index("expert") // SPLIT).astype(jnp.int32).reshape(1)
    tok_count, top_count = routes_fwd.shape[1:]
    assert top_count == 1
    width = act_in.shape[2]
    rows = min(tok_count, tok_count // experts + 2)
    pieces = 8 // math.gcd(rows, 8)
    pitch = -(-rows // 16) * 16
    scalar = pl.BlockSpec(memory_space=pltpu.SMEM)
    whole = pl.BlockSpec(memory_space=pltpu.VMEM)
    anywhere = pl.BlockSpec(memory_space=pl.ANY)

    shape = (pieces * rows, width // pieces)
    packed = [jax.ShapeDtypeStruct(shape, BF16)] * experts
    partial = [jax.ShapeDtypeStruct(shape, F32)] * experts + packed
    tokens = jax.ShapeDtypeStruct((tok_count, width), BF16)

    incoming = shifted(act_in[0], "section", 1)
    upstream = shifted(grad_in[0], "section", -1)
    r_fwd = routes_fwd.reshape(1, tok_count)
    r_bwd = routes_bwd.reshape(1, tok_count)
    g_fwd = gates_fwd.reshape(1, tok_count)
    g_bwd = gates_bwd.reshape(1, tok_count)

    own_share, *packed_b = local_call(
        first_body,
        [jax.ShapeDtypeStruct((3 * w_down.shape[1], width), BF16)] + packed,
        in_specs=[scalar] + [anywhere] * 6,
        out_specs=[anywhere] + [whole] * experts,
        scratch=[
            pltpu.VMEM((1, tok_count), jnp.int32),
            pltpu.VMEM((1, width), F32),
            pltpu.VMEM((tok_count, width), BF16),
            pltpu.VMEM((3 * w_down.shape[1], width), BF16),
            pltpu.SemaphoreType.DMA((9,)),
        ],
        vmem_mib=56,
        name="join_weights_pack_saved",
    )(own, r_bwd, norm_gain, saved_in[0], w_gate[0].T, w_up[0].T, w_down[0])
    shares = (w_gate[0].T, w_up[0].T, w_down[0], swapped(own_share, "expert", 1))

    rows_b = crossed(packed_b)
    swap_b = partners(rows_b[:1])
    packed_g = local_call(
        pack_grad_body,
        packed,
        in_specs=[scalar] + [whole] * 2,
        out_specs=[whole] * experts,
        name="pack_grad",
    )(own, r_bwd, after(upstream, packed_b[0]))
    rows_g = crossed(packed_g)
    *packed_f, kept_b = local_call(
        pack_act_body,
        packed + packed[:1],
        in_specs=[scalar] + [whole] * 4,
        out_specs=[whole] * (experts + 1),
        name="pack_act",
    )(own, r_fwd, norm_gain, after(incoming, packed_g[0], rows_b[-1]), packed_b[0])
    rows_f = crossed(packed_f)
    swap_g = partners(rows_g[:1], rows_b[-1])
    swap_f = partners(rows_f[:1], rows_g[-1])
    rows_b = [kept_b] + rows_b[1:] + swap_b + partners(rows_b[1:], swap_b[0])
    rows_g = rows_g + swap_g + partners(rows_g[1:], swap_g[0])
    rows_f = rows_f + swap_f + partners(rows_f[1:], swap_f[0], rows_b[-1])

    def run_experts(body, name, inputs, count, out_shape):
        wides = [pltpu.VMEM((count * pitch, width), BF16)] * (len(inputs) // count)
        return local_call(
            functools.partial(body, count, rows), out_shape, scratch=wides, vmem_mib=40, name=name
        )(*inputs, *shares)

    near = experts + 1
    partial_b = run_experts(backward_body, "experts_bwd_near", rows_b[:near] + rows_g[:near], near, partial[:near])
    far_g = [after(rows_g[near], partial_b[0])] + rows_g[near + 1:]
    partial_b = partial_b + run_experts(
        backward_body, "experts_bwd_far", rows_b[near:] + far_g, experts - 1, partial[near:]
    )
    rows_f = [after(rows_f[0], partial_b[-1])] + rows_f[1:]
    partial_f = run_experts(forward_body, "experts_fwd", rows_f, 2 * experts, partial)
    totals_b, home_b = crossing_home(partial_b)
    totals_f, home_f = crossing_home(partial_f)
    back_b = [partial_b[0]] + partners(partial_b[experts:experts + 1], *totals_b) + home_b
    back_f = [partial_f[0]] + partners(partial_f[experts:experts + 1], *totals_f, *home_b) + home_f

    grad_out = local_call(
        functools.partial(backward_home_body, experts, rows),
        tokens,
        in_specs=[scalar] + [whole] * (6 + experts),
        out_specs=whole,
        name="home_bwd",
    )(own, r_bwd, g_bwd, norm_gain, saved_in[0], upstream, *back_b)
    act_out = local_call(
        functools.partial(forward_home_body, experts, rows),
        tokens,
        in_specs=[scalar] + [whole] * (4 + experts),
        out_specs=whole,
        name="home_fwd",
    )(own, r_fwd, g_fwd, incoming, *back_f)
    return (act_out[None], grad_out[None])


def solution(mesh):
    tokens = P("section", "expert", None)
    in_specs = (
        tokens,
        tokens,
        tokens,
        P("section", None),
        P("section", None, "expert"),
        P("section", None, "expert"),
        tokens,
        tokens,
        tokens,
        tokens,
        tokens,
    )
    return jax.shard_map(
        per_device, mesh=mesh, in_specs=in_specs, out_specs=(tokens, tokens), check_vma=False
    )
```

```python
import functools
import math

import jax
import jax.numpy as jnp
from jax import lax
from jax.experimental import pallas as pl
from jax.experimental.pallas import tpu as pltpu
from jax.sharding import PartitionSpec as P

SPLIT = 4
EPS = 1e-06
CONTRACT = (((1,), (1,)), ((), ()))
OVER_ROWS = (((0,), (0,)), ((), ()))
F32 = jnp.float32
BF16 = jnp.bfloat16


def shifted(value, axis, steps):
    count = lax.axis_size(axis)
    return lax.ppermute(value, axis, [(i, (i + steps) % count) for i in range(count)])


def swapped(value, axis, bit):
    count = lax.axis_size(axis)
    return lax.ppermute(value, axis, [(i, i ^ bit) for i in range(count)])


def after(value, *others):
    return lax.optimization_barrier((value, *others))[0] if others else value


def local_call(body, out_shape, scratch=(), vmem_mib=16, **names):
    return pl.pallas_call(
        body,
        out_shape=out_shape,
        scratch_shapes=scratch,
        compiler_params=pltpu.CompilerParams(vmem_limit_bytes=vmem_mib << 20),
        cost_estimate=pl.CostEstimate(flops=1000, bytes_accessed=1000, transcendentals=0),
        **names,
    )


def silu_parts(values):
    sigma = jax.nn.sigmoid(values)
    return (values * sigma, sigma * (1.0 + values * (1.0 - sigma)))


def inverse_rms(values):
    return lax.rsqrt(jnp.mean(values * values, axis=-1, keepdims=True) + EPS)


def slots_of(routes, own, experts):
    count = routes.shape[1]
    height = -(-experts // 8) * 8
    ids = lax.broadcasted_iota(jnp.int32, (height, count), 0)
    onehot = (ids == routes).astype(F32)
    earlier = (
        lax.broadcasted_iota(jnp.int32, (count, count), 0) < lax.broadcasted_iota(jnp.int32, (count, count), 1)
    ).astype(F32)
    before = jnp.dot(onehot.astype(BF16), earlier.astype(BF16), preferred_element_type=F32)
    slot = jnp.sum(before * onehot, axis=0, keepdims=True).astype(jnp.int32)
    block = routes - own
    return (jnp.where(block < 0, block + experts, block), slot)


def chooser_of(block, slot, j, piece, rows, height):
    place = lax.broadcasted_iota(jnp.int32, (height, block.shape[1]), 0)
    return jnp.where((place == slot + piece * rows) & (block == j), 1.0, 0.0).astype(BF16)


def pack(values, own_ref, routes_ref, outs):
    experts = len(outs)
    height, cols = outs[0].shape
    pieces = values.shape[1] // cols
    rows = height // pieces
    block, slot = slots_of(routes_ref[...], own_ref[0], experts)
    for j, out in enumerate(outs):
        total = None
        for p in range(pieces):
            chooser = chooser_of(block, slot, j, p, rows, height)
            part = jnp.dot(chooser, values[:, p * cols:(p + 1) * cols], preferred_element_type=F32)
            total = part if total is None else total + part
        out[...] = total.astype(BF16)


def normed(x_ref, gain_ref):
    values = x_ref[...].astype(F32)
    return (values * inverse_rms(values) * gain_ref[...]).astype(BF16)


def pack_grad_body(own_ref, routes_ref, x_ref, *outs):
    pack(x_ref[...], own_ref, routes_ref, outs)


def pack_act_body(own_ref, routes_ref, gain_ref, x_ref, kept_ref, *outs):
    pack(normed(x_ref, gain_ref), own_ref, routes_ref, outs[:-1])
    outs[-1][...] = kept_ref[...]


def first_body(own_ref, *refs):
    args, parts, joined = refs[:3], refs[3:6], refs[6]
    outs, held, stage, sems = refs[7:-5], refs[-5:-2], refs[-2], refs[-1]
    units = parts[0].shape[0]
    piece = units // 2
    fetch = [pltpu.make_async_copy(arg, to, sems.at[i]) for i, (arg, to) in enumerate(zip(args, held))]
    load, store = [], []
    for i in range(6):
        rows = pl.ds(i * piece, piece)
        source = parts[i // 2].at[pl.ds(i % 2 * piece, piece), :]
        load.append(pltpu.make_async_copy(source, stage.at[rows, :], sems.at[3 + i]))
        store.append(pltpu.make_async_copy(stage.at[rows, :], joined.at[rows, :], sems.at[9 + i]))
    for copy in fetch + load:
        copy.start()
    for copy in fetch:
        copy.wait()
    routes_ref, gain_ref, x_ref = held
    for i in range(6):
        load[i].wait()
        store[i].start()
    pack(normed(x_ref, gain_ref), own_ref, routes_ref, outs)
    for copy in store:
        copy.wait()


def unpack(refs, wide_ref, rows):
    pitch = wide_ref.shape[0] // len(refs)
    pieces = refs[0].shape[0] // rows
    for i, ref in enumerate(refs):
        value = ref[...].astype(F32)
        whole = jnp.concatenate([value[p * rows:(p + 1) * rows] for p in range(pieces)], axis=1)
        wide_ref[pl.ds(i * pitch, rows), :] = whole.astype(BF16)
    return wide_ref[...]


def spread_out(total, refs, pitch, rows):
    for i, ref in enumerate(refs):
        cols = ref.shape[1]
        whole = total[i * pitch:i * pitch + rows]
        pieces = [whole[:, p * cols:(p + 1) * cols] for p in range(ref.shape[0] // rows)]
        ref[...] = jnp.concatenate(pieces, axis=0).astype(ref.dtype)


def joined(shares, i):
    units = shares[i].shape[0]
    return jnp.concatenate([shares[i][...], shares[3][pl.ds(i * units, units), :]], axis=0)


def forward_body(count, rows, *refs):
    row_refs, shares, outs, wide_ref = refs[:count], refs[count:count + 4], refs[count + 4:-1], refs[-1]
    x = unpack(row_refs, wide_ref, rows)
    gate_pre = lax.dot_general(x, joined(shares, 0), CONTRACT, preferred_element_type=F32)
    up_pre = lax.dot_general(x, joined(shares, 1), CONTRACT, preferred_element_type=F32)
    hidden = (silu_parts(gate_pre)[0] * up_pre).astype(BF16)
    total = jnp.dot(hidden, joined(shares, 2), preferred_element_type=F32)
    spread_out(total, outs, x.shape[0] // count, rows)


def backward_body(count, rows, *refs):
    row_refs, grad_refs, shares = refs[:count], refs[count:2 * count], refs[2 * count:2 * count + 4]
    outs, wide_ref, grad_wide_ref = refs[2 * count + 4:-2], refs[-2], refs[-1]
    x = unpack(row_refs, wide_ref, rows)
    gate, up = joined(shares, 0), joined(shares, 1)
    gate_pre = lax.dot_general(x, gate, CONTRACT, preferred_element_type=F32)
    up_pre = lax.dot_general(x, up, CONTRACT, preferred_element_type=F32)
    activation, derivative = silu_parts(gate_pre)
    grads = unpack(grad_refs, grad_wide_ref, rows)
    d_hidden = lax.dot_general(grads, joined(shares, 2), CONTRACT, preferred_element_type=F32)
    d_gate = (d_hidden * up_pre * derivative).astype(BF16)
    d_up = (d_hidden * activation).astype(BF16)
    total = jnp.dot(d_gate, gate, preferred_element_type=F32) + jnp.dot(d_up, up, preferred_element_type=F32)
    spread_out(total, outs, x.shape[0] // count, rows)


def routed_sum(experts, rows, own_ref, routes_ref, gates_ref, home_refs):
    block, slot = slots_of(routes_ref[...], own_ref[0], experts)
    mine, theirs, *crossed_refs = home_refs
    blocks = [(mine[...] + theirs[...].astype(F32)).astype(BF16)] + [ref[...] for ref in crossed_refs]
    height = blocks[0].shape[0]
    columns = []
    for p in range(height // rows):
        total = None
        for j in range(experts):
            chooser = chooser_of(block, slot, j, p, rows, height)
            part = lax.dot_general(chooser, blocks[j], OVER_ROWS, preferred_element_type=F32)
            total = part if total is None else total + part
        columns.append(total)
    count = block.shape[1]
    diagonal = lax.broadcasted_iota(jnp.int32, (count, count), 0) == lax.broadcasted_iota(
        jnp.int32, (count, count), 1
    )
    gates = jnp.sum(jnp.where(diagonal, gates_ref[...], 0.0), axis=1, keepdims=True)
    return jnp.concatenate(columns, axis=1) * gates


def forward_home_body(experts, rows, own_ref, routes_ref, gates_ref, x_ref, *refs):
    mixed = routed_sum(experts, rows, own_ref, routes_ref, gates_ref, refs[:-1])
    refs[-1][...] = (x_ref[...].astype(F32) + mixed).astype(BF16)


def backward_home_body(experts, rows, own_ref, routes_ref, gates_ref, gain_ref, saved_ref, up_ref, *refs):
    d_norm = routed_sum(experts, rows, own_ref, routes_ref, gates_ref, refs[:-1])
    base = saved_ref[...].astype(F32)
    inv_scale = inverse_rms(base)
    scaled = d_norm * gain_ref[...]
    d_input = inv_scale * (
        scaled - base * inv_scale * inv_scale * jnp.mean(scaled * base, axis=-1, keepdims=True)
    )
    refs[-1][...] = (up_ref[...].astype(F32) + d_input).astype(BF16)


def crossed(blocks):
    return [blocks[0]] + [shifted(blocks[j], "expert", SPLIT * j) for j in range(1, len(blocks))]


def partners(blocks, *others):
    return [swapped(after(block, *others), "expert", 2) for block in blocks]


def crossing_home(partial):
    experts = len(partial) // 2
    mine, theirs = partial[:experts], partial[experts:]
    totals = [
        (mine[j] + swapped(theirs[j], "expert", 2).astype(F32)).astype(BF16) for j in range(1, experts)
    ]
    return totals, [shifted(totals[j - 1], "expert", -SPLIT * j) for j in range(1, experts)]


def per_device(act_in, saved_in, grad_in, norm_gain, w_gate, w_up, w_down, routes_fwd, gates_fwd, routes_bwd, gates_bwd):
    experts = lax.axis_size("expert") // SPLIT
    own = (lax.axis_index("expert") // SPLIT).astype(jnp.int32).reshape(1)
    tok_count, top_count = routes_fwd.shape[1:]
    assert top_count == 1
    width = act_in.shape[2]
    rows = min(tok_count, tok_count // experts + 2)
    pieces = 8 // math.gcd(rows, 8)
    pitch = -(-rows // 16) * 16
    scalar = pl.BlockSpec(memory_space=pltpu.SMEM)
    whole = pl.BlockSpec(memory_space=pltpu.VMEM)
    anywhere = pl.BlockSpec(memory_space=pl.ANY)

    shape = (pieces * rows, width // pieces)
    packed = [jax.ShapeDtypeStruct(shape, BF16)] * experts
    partial = [jax.ShapeDtypeStruct(shape, F32)] * experts + packed
    tokens = jax.ShapeDtypeStruct((tok_count, width), BF16)

    incoming = shifted(act_in[0], "section", 1)
    upstream = shifted(grad_in[0], "section", -1)
    r_fwd = routes_fwd.reshape(1, tok_count)
    r_bwd = routes_bwd.reshape(1, tok_count)
    g_fwd = gates_fwd.reshape(1, tok_count)
    g_bwd = gates_bwd.reshape(1, tok_count)

    own_share, *packed_b = local_call(
        first_body,
        [jax.ShapeDtypeStruct((3 * w_down.shape[1], width), BF16)] + packed,
        in_specs=[scalar] + [anywhere] * 6,
        out_specs=[anywhere] + [whole] * experts,
        scratch=[
            pltpu.VMEM((1, tok_count), jnp.int32),
            pltpu.VMEM((1, width), F32),
            pltpu.VMEM((tok_count, width), BF16),
            pltpu.VMEM((3 * w_down.shape[1], width), BF16),
            pltpu.SemaphoreType.DMA((15,)),
        ],
        vmem_mib=56,
        name="join_weights_pack_saved",
    )(own, r_bwd, norm_gain, saved_in[0], w_gate[0].T, w_up[0].T, w_down[0])
    shares = (w_gate[0].T, w_up[0].T, w_down[0], swapped(own_share, "expert", 1))

    rows_b = crossed(packed_b)
    swap_b = partners(rows_b[:1])
    packed_g = local_call(
        pack_grad_body,
        packed,
        in_specs=[scalar] + [whole] * 2,
        out_specs=[whole] * experts,
        name="pack_grad",
    )(own, r_bwd, after(upstream, packed_b[0]))
    rows_g = crossed(packed_g)
    *packed_f, kept_b = local_call(
        pack_act_body,
        packed + packed[:1],
        in_specs=[scalar] + [whole] * 4,
        out_specs=[whole] * (experts + 1),
        name="pack_act",
    )(own, r_fwd, norm_gain, after(incoming, packed_g[0], rows_b[-1]), packed_b[0])
    rows_f = crossed(packed_f)
    swap_g = partners(rows_g[:1], rows_b[-1])
    swap_f = partners(rows_f[:1], rows_g[-1])
    rows_b = [kept_b] + rows_b[1:] + swap_b + partners(rows_b[1:], swap_b[0])
    rows_g = rows_g + swap_g + partners(rows_g[1:], swap_g[0])
    rows_f = rows_f + swap_f + partners(rows_f[1:], swap_f[0], rows_b[-1])

    def run_experts(body, name, inputs, count, out_shape):
        wides = [pltpu.VMEM((count * pitch, width), BF16)] * (len(inputs) // count)
        return local_call(
            functools.partial(body, count, rows), out_shape, scratch=wides, vmem_mib=40, name=name
        )(*inputs, *shares)

    near = experts + 1
    partial_b = run_experts(backward_body, "experts_bwd_near", rows_b[:near] + rows_g[:near], near, partial[:near])
    far_g = [after(rows_g[near], partial_b[0])] + rows_g[near + 1:]
    partial_b = partial_b + run_experts(
        backward_body, "experts_bwd_far", rows_b[near:] + far_g, experts - 1, partial[near:]
    )
    rows_f = [after(rows_f[0], partial_b[-1])] + rows_f[1:]
    partial_f = run_experts(forward_body, "experts_fwd", rows_f, 2 * experts, partial)
    totals_b, home_b = crossing_home(partial_b)
    totals_f, home_f = crossing_home(partial_f)
    back_b = [partial_b[0]] + partners(partial_b[experts:experts + 1], *totals_b) + home_b
    back_f = [partial_f[0]] + partners(partial_f[experts:experts + 1], *totals_f, *home_b) + home_f

    grad_out = local_call(
        functools.partial(backward_home_body, experts, rows),
        tokens,
        in_specs=[scalar] + [whole] * (6 + experts),
        out_specs=whole,
        name="home_bwd",
    )(own, r_bwd, g_bwd, norm_gain, saved_in[0], upstream, *back_b)
    act_out = local_call(
        functools.partial(forward_home_body, experts, rows),
        tokens,
        in_specs=[scalar] + [whole] * (4 + experts),
        out_specs=whole,
        name="home_fwd",
    )(own, r_fwd, g_fwd, incoming, *back_f)
    return (act_out[None], grad_out[None])


def solution(mesh):
    tokens = P("section", "expert", None)
    in_specs = (
        tokens,
        tokens,
        tokens,
        P("section", None),
        P("section", None, "expert"),
        P("section", None, "expert"),
        tokens,
        tokens,
        tokens,
        tokens,
        tokens,
    )
    return jax.shard_map(
        per_device, mesh=mesh, in_specs=in_specs, out_specs=(tokens, tokens), check_vma=False
    )
```

```python
import functools
import math

import jax
import jax.numpy as jnp
from jax import lax
from jax.experimental import pallas as pl
from jax.experimental.pallas import tpu as pltpu
from jax.sharding import PartitionSpec as P

SPLIT = 4
EPS = 1e-06
CONTRACT = (((1,), (1,)), ((), ()))
OVER_ROWS = (((0,), (0,)), ((), ()))
F32 = jnp.float32
BF16 = jnp.bfloat16


def shifted(value, axis, steps):
    count = lax.axis_size(axis)
    return lax.ppermute(value, axis, [(i, (i + steps) % count) for i in range(count)])


def swapped(value, axis, bit):
    count = lax.axis_size(axis)
    return lax.ppermute(value, axis, [(i, i ^ bit) for i in range(count)])


def after(value, *others):
    return lax.optimization_barrier((value, *others))[0] if others else value


def local_call(body, out_shape, scratch=(), vmem_mib=16, **names):
    return pl.pallas_call(
        body,
        out_shape=out_shape,
        scratch_shapes=scratch,
        compiler_params=pltpu.CompilerParams(vmem_limit_bytes=vmem_mib << 20),
        cost_estimate=pl.CostEstimate(flops=1000, bytes_accessed=1000, transcendentals=0),
        **names,
    )


def silu_parts(values):
    sigma = jax.nn.sigmoid(values)
    return (values * sigma, sigma * (1.0 + values * (1.0 - sigma)))


def inverse_rms(values):
    return lax.rsqrt(jnp.mean(values * values, axis=-1, keepdims=True) + EPS)


def slots_of(routes, own, experts):
    count = routes.shape[1]
    height = -(-experts // 8) * 8
    ids = lax.broadcasted_iota(jnp.int32, (height, count), 0)
    onehot = (ids == routes).astype(F32)
    earlier = (
        lax.broadcasted_iota(jnp.int32, (count, count), 0) < lax.broadcasted_iota(jnp.int32, (count, count), 1)
    ).astype(F32)
    before = jnp.dot(onehot.astype(BF16), earlier.astype(BF16), preferred_element_type=F32)
    slot = jnp.sum(before * onehot, axis=0, keepdims=True).astype(jnp.int32)
    block = routes - own
    return (jnp.where(block < 0, block + experts, block), slot)


def chooser_of(block, slot, j, piece, rows, height):
    place = lax.broadcasted_iota(jnp.int32, (height, block.shape[1]), 0)
    return jnp.where((place == slot + piece * rows) & (block == j), 1.0, 0.0).astype(BF16)


def pack(values, own_ref, routes_ref, outs):
    experts = len(outs)
    height, cols = outs[0].shape
    pieces = values.shape[1] // cols
    rows = height // pieces
    block, slot = slots_of(routes_ref[...], own_ref[0], experts)
    for j, out in enumerate(outs):
        total = None
        for p in range(pieces):
            chooser = chooser_of(block, slot, j, p, rows, height)
            part = jnp.dot(chooser, values[:, p * cols:(p + 1) * cols], preferred_element_type=F32)
            total = part if total is None else total + part
        out[...] = total.astype(BF16)


def normed(x_ref, gain_ref):
    values = x_ref[...].astype(F32)
    return (values * inverse_rms(values) * gain_ref[...]).astype(BF16)


def pack_grad_body(own_ref, routes_ref, x_ref, *outs):
    pack(x_ref[...], own_ref, routes_ref, outs)


def pack_act_body(own_ref, routes_ref, gain_ref, x_ref, kept_ref, *outs):
    pack(normed(x_ref, gain_ref), own_ref, routes_ref, outs[:-1])
    outs[-1][...] = kept_ref[...]


def first_body(own_ref, *refs):
    args, parts, joined = refs[:3], refs[3:6], refs[6]
    outs, held, stage, sems = refs[7:-5], refs[-5:-2], refs[-2], refs[-1]
    units = parts[0].shape[0]
    rows = [pl.ds(i * units, units) for i in range(3)]
    fetch = [pltpu.make_async_copy(arg, to, sems.at[i]) for i, (arg, to) in enumerate(zip(args, held))]
    load = [pltpu.make_async_copy(part, stage.at[rows[i], :], sems.at[3 + i]) for i, part in enumerate(parts)]
    store = [pltpu.make_async_copy(stage.at[rows[i], :], joined.at[rows[i], :], sems.at[6 + i]) for i in range(3)]
    for copy in fetch + load:
        copy.start()
    for copy in fetch:
        copy.wait()
    routes_ref, gain_ref, x_ref = held
    for i in range(3):
        load[i].wait()
        store[i].start()
    pack(normed(x_ref, gain_ref), own_ref, routes_ref, outs)
    for copy in store:
        copy.wait()


def unpack(refs, wide_ref, rows):
    pitch = wide_ref.shape[0] // len(refs)
    pieces = refs[0].shape[0] // rows
    for i, ref in enumerate(refs):
        value = ref[...].astype(F32)
        whole = jnp.concatenate([value[p * rows:(p + 1) * rows] for p in range(pieces)], axis=1)
        wide_ref[pl.ds(i * pitch, rows), :] = whole.astype(BF16)
    return wide_ref[...]


def spread_out(total, refs, pitch, rows):
    for i, ref in enumerate(refs):
        cols = ref.shape[1]
        whole = total[i * pitch:i * pitch + rows]
        pieces = [whole[:, p * cols:(p + 1) * cols] for p in range(ref.shape[0] // rows)]
        ref[...] = jnp.concatenate(pieces, axis=0).astype(ref.dtype)


def joined(shares, i):
    units = shares[i].shape[0]
    return jnp.concatenate([shares[i][...], shares[3][pl.ds(i * units, units), :]], axis=0)


def forward_body(count, rows, *refs):
    row_refs, shares, outs, wide_ref = refs[:count], refs[count:count + 4], refs[count + 4:-1], refs[-1]
    x = unpack(row_refs, wide_ref, rows)
    gate_pre = lax.dot_general(x, joined(shares, 0), CONTRACT, preferred_element_type=F32)
    up_pre = lax.dot_general(x, joined(shares, 1), CONTRACT, preferred_element_type=F32)
    hidden = (silu_parts(gate_pre)[0] * up_pre).astype(BF16)
    total = jnp.dot(hidden, joined(shares, 2), preferred_element_type=F32)
    spread_out(total, outs, x.shape[0] // count, rows)


def backward_body(count, rows, *refs):
    row_refs, grad_refs, shares = refs[:count], refs[count:2 * count], refs[2 * count:2 * count + 4]
    outs, wide_ref, grad_wide_ref = refs[2 * count + 4:-2], refs[-2], refs[-1]
    x = unpack(row_refs, wide_ref, rows)
    gate, up = joined(shares, 0), joined(shares, 1)
    gate_pre = lax.dot_general(x, gate, CONTRACT, preferred_element_type=F32)
    up_pre = lax.dot_general(x, up, CONTRACT, preferred_element_type=F32)
    activation, derivative = silu_parts(gate_pre)
    grads = unpack(grad_refs, grad_wide_ref, rows)
    d_hidden = lax.dot_general(grads, joined(shares, 2), CONTRACT, preferred_element_type=F32)
    d_gate = (d_hidden * up_pre * derivative).astype(BF16)
    d_up = (d_hidden * activation).astype(BF16)
    total = jnp.dot(d_gate, gate, preferred_element_type=F32) + jnp.dot(d_up, up, preferred_element_type=F32)
    spread_out(total, outs, x.shape[0] // count, rows)


def routed_sum(experts, rows, own_ref, routes_ref, gates_ref, home_refs):
    block, slot = slots_of(routes_ref[...], own_ref[0], experts)
    mine, theirs, *crossed_refs = home_refs
    blocks = [(mine[...] + theirs[...].astype(F32)).astype(BF16)] + [ref[...] for ref in crossed_refs]
    height = blocks[0].shape[0]
    columns = []
    for p in range(height // rows):
        total = None
        for j in range(experts):
            chooser = chooser_of(block, slot, j, p, rows, height)
            part = lax.dot_general(chooser, blocks[j], OVER_ROWS, preferred_element_type=F32)
            total = part if total is None else total + part
        columns.append(total)
    count = block.shape[1]
    diagonal = lax.broadcasted_iota(jnp.int32, (count, count), 0) == lax.broadcasted_iota(
        jnp.int32, (count, count), 1
    )
    gates = jnp.sum(jnp.where(diagonal, gates_ref[...], 0.0), axis=1, keepdims=True)
    return jnp.concatenate(columns, axis=1) * gates


def forward_home_body(experts, rows, own_ref, routes_ref, gates_ref, x_ref, *refs):
    mixed = routed_sum(experts, rows, own_ref, routes_ref, gates_ref, refs[:-1])
    refs[-1][...] = (x_ref[...].astype(F32) + mixed).astype(BF16)


def backward_home_body(experts, rows, own_ref, routes_ref, gates_ref, gain_ref, saved_ref, up_ref, *refs):
    d_norm = routed_sum(experts, rows, own_ref, routes_ref, gates_ref, refs[:-1])
    base = saved_ref[...].astype(F32)
    inv_scale = inverse_rms(base)
    scaled = d_norm * gain_ref[...]
    d_input = inv_scale * (
        scaled - base * inv_scale * inv_scale * jnp.mean(scaled * base, axis=-1, keepdims=True)
    )
    refs[-1][...] = (up_ref[...].astype(F32) + d_input).astype(BF16)


def crossed(blocks):
    return [blocks[0]] + [shifted(blocks[j], "expert", SPLIT * j) for j in range(1, len(blocks))]


def partners(blocks, *others):
    return [swapped(after(block, *others), "expert", 2) for block in blocks]


def crossing_home(partial):
    experts = len(partial) // 2
    mine, theirs = partial[:experts], partial[experts:]
    totals = [
        (mine[j] + swapped(theirs[j], "expert", 2).astype(F32)).astype(BF16) for j in range(1, experts)
    ]
    return totals, [shifted(totals[j - 1], "expert", -SPLIT * j) for j in range(1, experts)]


def per_device(act_in, saved_in, grad_in, norm_gain, w_gate, w_up, w_down, routes_fwd, gates_fwd, routes_bwd, gates_bwd):
    experts = lax.axis_size("expert") // SPLIT
    own = (lax.axis_index("expert") // SPLIT).astype(jnp.int32).reshape(1)
    tok_count, top_count = routes_fwd.shape[1:]
    assert top_count == 1
    width = act_in.shape[2]
    rows = min(tok_count, tok_count // experts + 2)
    pieces = 8 // math.gcd(rows, 8)
    pitch = -(-rows // 16) * 16
    scalar = pl.BlockSpec(memory_space=pltpu.SMEM)
    whole = pl.BlockSpec(memory_space=pltpu.VMEM)
    anywhere = pl.BlockSpec(memory_space=pl.ANY)

    shape = (pieces * rows, width // pieces)
    packed = [jax.ShapeDtypeStruct(shape, BF16)] * experts
    partial = [jax.ShapeDtypeStruct(shape, F32)] * experts + packed
    tokens = jax.ShapeDtypeStruct((tok_count, width), BF16)

    incoming = shifted(act_in[0], "section", 1)
    upstream = shifted(grad_in[0], "section", -1)
    r_fwd = routes_fwd.reshape(1, tok_count)
    r_bwd = routes_bwd.reshape(1, tok_count)
    g_fwd = gates_fwd.reshape(1, tok_count)
    g_bwd = gates_bwd.reshape(1, tok_count)

    own_share, *packed_b = local_call(
        first_body,
        [jax.ShapeDtypeStruct((3 * w_down.shape[1], width), BF16)] + packed,
        in_specs=[scalar] + [anywhere] * 6,
        out_specs=[anywhere] + [whole] * experts,
        scratch=[
            pltpu.VMEM((1, tok_count), jnp.int32),
            pltpu.VMEM((1, width), F32),
            pltpu.VMEM((tok_count, width), BF16),
            pltpu.VMEM((3 * w_down.shape[1], width), BF16),
            pltpu.SemaphoreType.DMA((9,)),
        ],
        vmem_mib=56,
        name="join_weights_pack_saved",
    )(own, r_bwd, norm_gain, saved_in[0], w_gate[0].T, w_up[0].T, w_down[0])
    shares = (w_gate[0].T, w_up[0].T, w_down[0], swapped(own_share, "expert", 1))

    rows_b = crossed(packed_b)
    swap_b = partners(rows_b[:1])
    packed_g = local_call(
        pack_grad_body,
        packed,
        in_specs=[scalar] + [whole] * 2,
        out_specs=[whole] * experts,
        name="pack_grad",
    )(own, r_bwd, after(upstream, packed_b[0]))
    rows_g = crossed(packed_g)
    *packed_f, kept_b = local_call(
        pack_act_body,
        packed + packed[:1],
        in_specs=[scalar] + [whole] * 4,
        out_specs=[whole] * (experts + 1),
        name="pack_act",
    )(own, r_fwd, norm_gain, after(incoming, packed_g[0], rows_b[-1]), packed_b[0])
    rows_f = crossed(packed_f)
    swap_g = partners(rows_g[:1], rows_b[-1])
    swap_f = partners(rows_f[:1], rows_g[-1])
    rows_b = [kept_b] + rows_b[1:] + swap_b + partners(rows_b[1:], swap_b[0])
    rows_g = rows_g + swap_g + partners(rows_g[1:], swap_g[0])
    rows_f = rows_f + swap_f + partners(rows_f[1:], swap_f[0], rows_b[-1])

    def run_experts(body, name, inputs, count, out_shape):
        wides = [pltpu.VMEM((count * pitch, width), BF16)] * (len(inputs) // count)
        return local_call(
            functools.partial(body, count, rows), out_shape, scratch=wides, vmem_mib=40, name=name
        )(*inputs, *shares)

    near = experts + 1
    far_b = run_experts(backward_body, "experts_bwd_far", rows_b[near:] + rows_g[near:], experts - 1, partial[near:])
    near_b = [after(rows_b[0], far_b[0])] + rows_b[1:near]
    partial_b = run_experts(backward_body, "experts_bwd_near", near_b + rows_g[:near], near, partial[:near]) + far_b
    rows_f = [after(rows_f[0], partial_b[0])] + rows_f[1:]
    partial_f = run_experts(forward_body, "experts_fwd", rows_f, 2 * experts, partial)
    totals_b, home_b = crossing_home(partial_b)
    totals_f, home_f = crossing_home(partial_f)
    back_b = [partial_b[0]] + partners(partial_b[experts:experts + 1], *totals_b) + home_b
    back_f = [partial_f[0]] + partners(partial_f[experts:experts + 1], *totals_f, *home_b) + home_f

    grad_out = local_call(
        functools.partial(backward_home_body, experts, rows),
        tokens,
        in_specs=[scalar] + [whole] * (6 + experts),
        out_specs=whole,
        name="home_bwd",
    )(own, r_bwd, g_bwd, norm_gain, saved_in[0], upstream, *back_b)
    act_out = local_call(
        functools.partial(forward_home_body, experts, rows),
        tokens,
        in_specs=[scalar] + [whole] * (4 + experts),
        out_specs=whole,
        name="home_fwd",
    )(own, r_fwd, g_fwd, incoming, *back_f)
    return (act_out[None], grad_out[None])


def solution(mesh):
    tokens = P("section", "expert", None)
    in_specs = (
        tokens,
        tokens,
        tokens,
        P("section", None),
        P("section", None, "expert"),
        P("section", None, "expert"),
        tokens,
        tokens,
        tokens,
        tokens,
        tokens,
    )
    return jax.shard_map(
        per_device, mesh=mesh, in_specs=in_specs, out_specs=(tokens, tokens), check_vma=False
    )
```

```python
import functools
import math

import jax
import jax.numpy as jnp
from jax import lax
from jax.experimental import pallas as pl
from jax.experimental.pallas import tpu as pltpu
from jax.sharding import PartitionSpec as P

SPLIT = 4
EPS = 1e-06
CONTRACT = (((1,), (1,)), ((), ()))
OVER_ROWS = (((0,), (0,)), ((), ()))
F32 = jnp.float32
BF16 = jnp.bfloat16


def shifted(value, axis, steps):
    count = lax.axis_size(axis)
    return lax.ppermute(value, axis, [(i, (i + steps) % count) for i in range(count)])


def swapped(value, axis, bit):
    count = lax.axis_size(axis)
    return lax.ppermute(value, axis, [(i, i ^ bit) for i in range(count)])


def after(value, *others):
    return lax.optimization_barrier((value, *others))[0] if others else value


def local_call(body, out_shape, scratch=(), vmem_mib=16, **names):
    return pl.pallas_call(
        body,
        out_shape=out_shape,
        scratch_shapes=scratch,
        compiler_params=pltpu.CompilerParams(vmem_limit_bytes=vmem_mib << 20),
        cost_estimate=pl.CostEstimate(flops=1000, bytes_accessed=1000, transcendentals=0),
        **names,
    )


def silu_parts(values):
    sigma = jax.nn.sigmoid(values)
    return (values * sigma, sigma * (1.0 + values * (1.0 - sigma)))


def inverse_rms(values):
    return lax.rsqrt(jnp.mean(values * values, axis=-1, keepdims=True) + EPS)


def slots_of(routes, own, experts):
    count = routes.shape[1]
    height = -(-experts // 8) * 8
    ids = lax.broadcasted_iota(jnp.int32, (height, count), 0)
    onehot = (ids == routes).astype(F32)
    earlier = (
        lax.broadcasted_iota(jnp.int32, (count, count), 0) < lax.broadcasted_iota(jnp.int32, (count, count), 1)
    ).astype(F32)
    before = jnp.dot(onehot.astype(BF16), earlier.astype(BF16), preferred_element_type=F32)
    slot = jnp.sum(before * onehot, axis=0, keepdims=True).astype(jnp.int32)
    block = routes - own
    return (jnp.where(block < 0, block + experts, block), slot)


def chooser_of(block, slot, j, piece, rows, height):
    place = lax.broadcasted_iota(jnp.int32, (height, block.shape[1]), 0)
    return jnp.where((place == slot + piece * rows) & (block == j), 1.0, 0.0).astype(BF16)


def pack(values, own_ref, routes_ref, outs):
    experts = len(outs)
    height, cols = outs[0].shape
    pieces = values.shape[1] // cols
    rows = height // pieces
    block, slot = slots_of(routes_ref[...], own_ref[0], experts)
    for j, out in enumerate(outs):
        total = None
        for p in range(pieces):
            chooser = chooser_of(block, slot, j, p, rows, height)
            part = jnp.dot(chooser, values[:, p * cols:(p + 1) * cols], preferred_element_type=F32)
            total = part if total is None else total + part
        out[...] = total.astype(BF16)


def normed(x_ref, gain_ref):
    values = x_ref[...].astype(F32)
    return (values * inverse_rms(values) * gain_ref[...]).astype(BF16)


def pack_grad_body(own_ref, routes_ref, x_ref, *outs):
    pack(x_ref[...], own_ref, routes_ref, outs)


def pack_act_body(own_ref, routes_ref, gain_ref, x_ref, kept_ref, *outs):
    pack(normed(x_ref, gain_ref), own_ref, routes_ref, outs[:-1])
    outs[-1][...] = kept_ref[...]


def first_body(own_ref, *refs):
    args, parts, joined = refs[:3], refs[3:6], refs[6]
    outs, held, stage, sems = refs[7:-5], refs[-5:-2], refs[-2], refs[-1]
    units = parts[0].shape[0]
    rows = [pl.ds(i * units, units) for i in range(3)]
    fetch = [pltpu.make_async_copy(arg, to, sems.at[i]) for i, (arg, to) in enumerate(zip(args, held))]
    load = [pltpu.make_async_copy(part, stage.at[rows[i], :], sems.at[3 + i]) for i, part in enumerate(parts)]
    store = [pltpu.make_async_copy(stage.at[rows[i], :], joined.at[rows[i], :], sems.at[6 + i]) for i in range(3)]
    for copy in fetch + load:
        copy.start()
    for copy in fetch:
        copy.wait()
    routes_ref, gain_ref, x_ref = held
    for i in range(3):
        load[i].wait()
        store[i].start()
    pack(normed(x_ref, gain_ref), own_ref, routes_ref, outs)
    for copy in store:
        copy.wait()


def unpack(refs, wide_ref, rows):
    pitch = wide_ref.shape[0] // len(refs)
    pieces = refs[0].shape[0] // rows
    for i, ref in enumerate(refs):
        value = ref[...].astype(F32)
        whole = jnp.concatenate([value[p * rows:(p + 1) * rows] for p in range(pieces)], axis=1)
        wide_ref[pl.ds(i * pitch, rows), :] = whole.astype(BF16)
    return wide_ref[...]


def spread_out(total, refs, pitch, rows):
    for i, ref in enumerate(refs):
        cols = ref.shape[1]
        whole = total[i * pitch:i * pitch + rows]
        pieces = [whole[:, p * cols:(p + 1) * cols] for p in range(ref.shape[0] // rows)]
        ref[...] = jnp.concatenate(pieces, axis=0).astype(ref.dtype)


def joined(shares, i):
    units = shares[i].shape[0]
    return jnp.concatenate([shares[i][...], shares[3][pl.ds(i * units, units), :]], axis=0)


def forward_body(count, rows, *refs):
    row_refs, shares, outs, wide_ref = refs[:count], refs[count:count + 4], refs[count + 4:-1], refs[-1]
    x = unpack(row_refs, wide_ref, rows)
    gate_pre = lax.dot_general(x, joined(shares, 0), CONTRACT, preferred_element_type=F32)
    up_pre = lax.dot_general(x, joined(shares, 1), CONTRACT, preferred_element_type=F32)
    hidden = (silu_parts(gate_pre)[0] * up_pre).astype(BF16)
    total = jnp.dot(hidden, joined(shares, 2), preferred_element_type=F32)
    spread_out(total, outs, x.shape[0] // count, rows)


def backward_body(count, rows, *refs):
    row_refs, grad_refs, shares = refs[:count], refs[count:2 * count], refs[2 * count:2 * count + 4]
    outs, wide_ref, grad_wide_ref = refs[2 * count + 4:-2], refs[-2], refs[-1]
    x = unpack(row_refs, wide_ref, rows)
    gate, up = joined(shares, 0), joined(shares, 1)
    gate_pre = lax.dot_general(x, gate, CONTRACT, preferred_element_type=F32)
    up_pre = lax.dot_general(x, up, CONTRACT, preferred_element_type=F32)
    activation, derivative = silu_parts(gate_pre)
    grads = unpack(grad_refs, grad_wide_ref, rows)
    d_hidden = lax.dot_general(grads, joined(shares, 2), CONTRACT, preferred_element_type=F32)
    d_gate = (d_hidden * up_pre * derivative).astype(BF16)
    d_up = (d_hidden * activation).astype(BF16)
    total = jnp.dot(d_gate, gate, preferred_element_type=F32) + jnp.dot(d_up, up, preferred_element_type=F32)
    spread_out(total, outs, x.shape[0] // count, rows)


def own_sum(mine, theirs):
    return (mine[...] + theirs[...].astype(F32)).astype(BF16)


def routed_sum(experts, rows, own_ref, routes_ref, gates_ref, blocks):
    block, slot = slots_of(routes_ref[...], own_ref[0], experts)
    height = blocks[0][1].shape[0]
    columns = []
    for p in range(height // rows):
        total = None
        for j, value in blocks:
            chooser = chooser_of(block, slot, j, p, rows, height)
            part = lax.dot_general(chooser, value, OVER_ROWS, preferred_element_type=F32)
            total = part if total is None else total + part
        columns.append(total)
    count = block.shape[1]
    diagonal = lax.broadcasted_iota(jnp.int32, (count, count), 0) == lax.broadcasted_iota(
        jnp.int32, (count, count), 1
    )
    gates = jnp.sum(jnp.where(diagonal, gates_ref[...], 0.0), axis=1, keepdims=True)
    return jnp.concatenate(columns, axis=1) * gates


def forward_crossed_body(experts, rows, own_ref, routes_ref, gates_ref, x_ref, *refs):
    blocks = [(j, ref[...]) for j, ref in enumerate(refs[:-1], 1)]
    refs[-1][...] = x_ref[...].astype(F32) + routed_sum(experts, rows, own_ref, routes_ref, gates_ref, blocks)


def forward_home_body(experts, rows, own_ref, routes_ref, gates_ref, sum_ref, mine, theirs, out):
    blocks = [(0, own_sum(mine, theirs))]
    out[...] = (sum_ref[...] + routed_sum(experts, rows, own_ref, routes_ref, gates_ref, blocks)).astype(BF16)


def backward_home_body(experts, rows, own_ref, routes_ref, gates_ref, gain_ref, saved_ref, up_ref, *refs):
    blocks = [(0, own_sum(*refs[:2]))] + [(j, ref[...]) for j, ref in enumerate(refs[2:-1], 1)]
    d_norm = routed_sum(experts, rows, own_ref, routes_ref, gates_ref, blocks)
    base = saved_ref[...].astype(F32)
    inv_scale = inverse_rms(base)
    scaled = d_norm * gain_ref[...]
    d_input = inv_scale * (
        scaled - base * inv_scale * inv_scale * jnp.mean(scaled * base, axis=-1, keepdims=True)
    )
    refs[-1][...] = (up_ref[...].astype(F32) + d_input).astype(BF16)


def crossed(blocks):
    return [blocks[0]] + [shifted(blocks[j], "expert", SPLIT * j) for j in range(1, len(blocks))]


def partners(blocks, *others):
    return [swapped(after(block, *others), "expert", 2) for block in blocks]


def crossing_home(partial):
    experts = len(partial) // 2
    mine, theirs = partial[:experts], partial[experts:]
    totals = [
        (mine[j] + swapped(theirs[j], "expert", 2).astype(F32)).astype(BF16) for j in range(1, experts)
    ]
    return totals, [shifted(totals[j - 1], "expert", -SPLIT * j) for j in range(1, experts)]


def per_device(act_in, saved_in, grad_in, norm_gain, w_gate, w_up, w_down, routes_fwd, gates_fwd, routes_bwd, gates_bwd):
    experts = lax.axis_size("expert") // SPLIT
    own = (lax.axis_index("expert") // SPLIT).astype(jnp.int32).reshape(1)
    tok_count, top_count = routes_fwd.shape[1:]
    assert top_count == 1
    width = act_in.shape[2]
    rows = min(tok_count, tok_count // experts + 2)
    pieces = 8 // math.gcd(rows, 8)
    pitch = -(-rows // 16) * 16
    scalar = pl.BlockSpec(memory_space=pltpu.SMEM)
    whole = pl.BlockSpec(memory_space=pltpu.VMEM)
    anywhere = pl.BlockSpec(memory_space=pl.ANY)

    shape = (pieces * rows, width // pieces)
    packed = [jax.ShapeDtypeStruct(shape, BF16)] * experts
    partial = [jax.ShapeDtypeStruct(shape, F32)] * experts + packed
    tokens = jax.ShapeDtypeStruct((tok_count, width), BF16)

    incoming = shifted(act_in[0], "section", 1)
    upstream = shifted(grad_in[0], "section", -1)
    r_fwd = routes_fwd.reshape(1, tok_count)
    r_bwd = routes_bwd.reshape(1, tok_count)
    g_fwd = gates_fwd.reshape(1, tok_count)
    g_bwd = gates_bwd.reshape(1, tok_count)

    own_share, *packed_b = local_call(
        first_body,
        [jax.ShapeDtypeStruct((3 * w_down.shape[1], width), BF16)] + packed,
        in_specs=[scalar] + [anywhere] * 6,
        out_specs=[anywhere] + [whole] * experts,
        scratch=[
            pltpu.VMEM((1, tok_count), jnp.int32),
            pltpu.VMEM((1, width), F32),
            pltpu.VMEM((tok_count, width), BF16),
            pltpu.VMEM((3 * w_down.shape[1], width), BF16),
            pltpu.SemaphoreType.DMA((9,)),
        ],
        vmem_mib=56,
        name="join_weights_pack_saved",
    )(own, r_bwd, norm_gain, saved_in[0], w_gate[0].T, w_up[0].T, w_down[0])
    shares = (w_gate[0].T, w_up[0].T, w_down[0], swapped(own_share, "expert", 1))

    rows_b = crossed(packed_b)
    swap_b = partners(rows_b[:1])
    packed_g = local_call(
        pack_grad_body,
        packed,
        in_specs=[scalar] + [whole] * 2,
        out_specs=[whole] * experts,
        name="pack_grad",
    )(own, r_bwd, after(upstream, packed_b[0]))
    rows_g = crossed(packed_g)
    *packed_f, kept_b = local_call(
        pack_act_body,
        packed + packed[:1],
        in_specs=[scalar] + [whole] * 4,
        out_specs=[whole] * (experts + 1),
        name="pack_act",
    )(own, r_fwd, norm_gain, after(incoming, packed_g[0], rows_b[-1]), packed_b[0])
    rows_f = crossed(packed_f)
    swap_g = partners(rows_g[:1], rows_b[-1])
    swap_f = partners(rows_f[:1], rows_g[-1])
    rows_b = [kept_b] + rows_b[1:] + swap_b + partners(rows_b[1:], swap_b[0])
    rows_g = rows_g + swap_g + partners(rows_g[1:], swap_g[0])
    rows_f = rows_f + swap_f + partners(rows_f[1:], swap_f[0], rows_b[-1])

    def run_experts(body, name, inputs, count, out_shape):
        wides = [pltpu.VMEM((count * pitch, width), BF16)] * (len(inputs) // count)
        return local_call(
            functools.partial(body, count, rows), out_shape, scratch=wides, vmem_mib=40, name=name
        )(*inputs, *shares)

    near = experts + 1
    far_b = run_experts(backward_body, "experts_bwd_far", rows_b[near:] + rows_g[near:], experts - 1, partial[near:])
    near_b = [after(rows_b[0], far_b[0])] + rows_b[1:near]
    partial_b = run_experts(backward_body, "experts_bwd_near", near_b + rows_g[:near], near, partial[:near]) + far_b
    rows_f = [after(rows_f[0], partial_b[0])] + rows_f[1:]
    partial_f = run_experts(forward_body, "experts_fwd", rows_f, 2 * experts, partial)
    totals_b, home_b = crossing_home(partial_b)
    totals_f, home_f = crossing_home(partial_f)
    back_b = [partial_b[0]] + partners(partial_b[experts:experts + 1], *totals_b) + home_b
    back_f = [partial_f[0]] + partners(partial_f[experts:experts + 1], *totals_f, *home_b) + home_f

    grad_out = local_call(
        functools.partial(backward_home_body, experts, rows),
        tokens,
        in_specs=[scalar] + [whole] * (6 + experts),
        out_specs=whole,
        name="home_bwd",
    )(own, r_bwd, g_bwd, norm_gain, saved_in[0], upstream, *back_b)
    crossed_sum = local_call(
        functools.partial(forward_crossed_body, experts, rows),
        jax.ShapeDtypeStruct((tok_count, width), F32),
        in_specs=[scalar] + [whole] * (2 + experts),
        out_specs=whole,
        name="home_fwd_crossed",
    )(own, r_fwd, g_fwd, incoming, *home_f)
    act_out = local_call(
        functools.partial(forward_home_body, experts, rows),
        tokens,
        in_specs=[scalar] + [whole] * 5,
        out_specs=whole,
        name="home_fwd",
    )(own, r_fwd, g_fwd, crossed_sum, *back_f[:2])
    return (act_out[None], grad_out[None])


def solution(mesh):
    tokens = P("section", "expert", None)
    in_specs = (
        tokens,
        tokens,
        tokens,
        P("section", None),
        P("section", None, "expert"),
        P("section", None, "expert"),
        tokens,
        tokens,
        tokens,
        tokens,
        tokens,
    )
    return jax.shard_map(
        per_device, mesh=mesh, in_specs=in_specs, out_specs=(tokens, tokens), check_vma=False
    )
```
